128 devices in a mesh: seq: 16 (over x, y), head: 8 (over z, core).
Axes of the slice: x: 4, y: 4, z: 4, core: 2. Of those that a mesh axis runs over, the one named last changes fastest.
Arguments:
- hidden: bfloat16 [2, 4096, 2048], P(None, 'seq', 'head'), may hold values from -6 to 6
- cotangent: float32 [2, 4096, 2048], P(None, 'seq', 'head'), may hold values from -6 to 6
- opening_flags: int32 [2, 4096], P(None, 'seq'), may hold values from 0 to 1, as said below
- vectors: bfloat16 [1, 16, 2048], P(None, 'seq', 'head'), may hold values from -9 to 2, as said below
- shift_first: bfloat16 [1, 160, 2048], P(None, 'seq', 'head'), may hold values from -0.125 to 0.125
- shift_second: bfloat16 [1, 160, 2048], P(None, 'seq', 'head'), may hold values from -1 to 1
- decay_first: bfloat16 [1, 64, 2048], P(None, 'seq', 'head'), may hold values from -0.125 to 0.125
- decay_second: bfloat16 [1, 64, 2048], P(None, 'seq', 'head'), may hold values from -0.75 to 0.75
- time_weights: bfloat16 [1, 4, 2048, 2048], P(None, None, 'seq', 'head'), may hold values from -0.125 to 0.125
- time_output: bfloat16 [1, 2048, 2048], P(None, 'head', 'seq'), may hold values from -0.125 to 0.125
- channel_key: bfloat16 [1, 2048, 7168], P(None, 'seq', 'head'), may hold values from -0.125 to 0.125
- channel_value: bfloat16 [1, 7168, 2048], P(None, 'head', 'seq'), may hold values from -0.0625 to 0.0625
- channel_recept: bfloat16 [1, 2048, 2048], P(None, 'seq', 'head'), may hold values from -0.125 to 0.125
Outputs:
- result: float32 [2, 4096, 2048], P(None, 'seq', 'head')
- hidden_grad: float32 [2, 4096, 2048], P(None, 'seq', 'head')
- vectors_grad: float32 [1, 16, 2048], P(None, 'seq', 'head')
- shift_first_grad: float32 [1, 160, 2048], P(None, 'seq', 'head')
- shift_second_grad: float32 [1, 160, 2048], P(None, 'seq', 'head')
- decay_first_grad: float32 [1, 64, 2048], P(None, 'seq', 'head')
- decay_second_grad: float32 [1, 64, 2048], P(None, 'seq', 'head')
- time_weights_grad: float32 [1, 4, 2048, 2048], P(None, None, 'seq', 'head')
- time_output_grad: float32 [1, 2048, 2048], P(None, 'head', 'seq')
- channel_key_grad: float32 [1, 2048, 7168], P(None, 'seq', 'head')
- channel_value_grad: float32 [1, 7168, 2048], P(None, 'head', 'seq')
- channel_recept_grad: float32 [1, 2048, 2048], P(None, 'seq', 'head')
The draws below stay inside these ranges and needn't reach their ends.
Inputs may be any that keep to these rules, and one draw needn't show every extreme that they name: `opening_flags`: 1 marks the first token of a sequence, where token shift and WKV state restart; position 0 of every batch row is 1; one batch row, drawn from the seed, holds a single sequence, the others up to four. `vectors`: row 8 lies in -9 to -3; rows 2 to 7, 14 and 15 in 0 to 2.
All inputs are finite; a program needn't handle non-finite values.
Results may differ from the reference program's by a relative error of at most 0.03.
Values may be sent and summed in bfloat16 or wider, within the bound.
A program may use at most 192 MiB of HBM per device.

```python
import jax
import jax.numpy as jnp
from jax import lax

D = 2048
ATTENTION_COUNT = 32
CHANNELS_PER_ATT = 64
FF = 7168
MIX_RANK = 32
DECAY_RANK = 64
LAYERS = 1
BATCH = 2
SPAN = 4096


def draw_vectors(key, part):
    key = jax.random.fold_in(key, 11)
    normal_key, uniform_key = jax.random.split(key)
    array_shape = (LAYERS, 16, D)
    normal_random_draw = jnp.clip(jax.random.normal(normal_key, array_shape, jnp.float32), -4.0, 4.0)
    flat_random_draw = jax.random.uniform(uniform_key, array_shape, jnp.float32)
    line_ordinal = lax.broadcasted_iota(jnp.int32, array_shape, 1)
    scaling_arrays = 1.0 + 0.15 * normal_random_draw
    offset_arrays = 0.3 * normal_random_draw
    fading_arrays = -9.0 + 6.0 * flat_random_draw
    extra_random_draw = 0.5 * normal_random_draw
    mixing_arrays = 2.0 * flat_random_draw
    flags_scaling = (line_ordinal == 0) | (line_ordinal == 10) | (line_ordinal == 12)
    flags_offset = (line_ordinal == 1) | (line_ordinal == 11) | (line_ordinal == 13)
    random_draws = jnp.where(flags_scaling, scaling_arrays, jnp.where(flags_offset, offset_arrays, jnp.where(line_ordinal == 8, fading_arrays, jnp.where(line_ordinal == 9, extra_random_draw, mixing_arrays))))
    return random_draws.astype(jnp.bfloat16)


def draw_opening_flags(key, part):
    key = jax.random.fold_in(key, 5)
    whole_key, place_key = jax.random.split(key)
    single_row = jax.random.randint(whole_key, (), 0, BATCH)
    places = jax.random.randint(place_key, (BATCH, 3), 1, SPAN)
    positions = lax.broadcasted_iota(jnp.int32, (BATCH, SPAN), 1)
    row_numbers = lax.broadcasted_iota(jnp.int32, (BATCH, SPAN), 0)
    hits = jnp.any(positions[:, None, :] == places[:, :, None], axis=1)
    hits = jnp.logical_and(hits, row_numbers != single_row)
    return jnp.where(positions == 0, 1, jnp.where(hits, 1, 0)).astype(jnp.int32)


def level_of(rng, shape, cuts, least, top_value):
    loudness = 1.0
    for axis_at, parts in cuts:
        steps = jax.random.uniform(jax.random.fold_in(jax.random.fold_in(rng, 6), axis_at), (parts,), jnp.float32, least / len(cuts), top_value / len(cuts))
        loudness = loudness * jnp.repeat(jnp.exp(steps), shape[axis_at] // parts).reshape((-1,) + (1,) * (len(shape) - 1 - axis_at))
    return loudness


def normal_values(own_key, extent, spread, reach, cuts=(), kind=jnp.bfloat16):
    values = spread * jax.random.normal(own_key, extent, jnp.float32)
    if cuts:
        values = values * level_of(own_key, extent, cuts, -0.22, 0.18)
    return jnp.clip(values, -reach, reach).astype(kind)


def setup_inputs(seed: int = 0) -> dict:
    seeds = jax.random.split(jax.random.key(seed), 14)
    hidden = normal_values(seeds[0], (BATCH, SPAN, D), 1.0, 6.0, ((1, 16), (2, 8)))
    cotangent = normal_values(seeds[1], (BATCH, SPAN, D), 1.0, 6.0, ((1, 16), (2, 8)), jnp.float32)
    opening_flags = draw_opening_flags(jax.random.fold_in(seeds[13], 71), 0)
    vectors = draw_vectors(jax.random.fold_in(seeds[13], 71), 0)
    shift_first = normal_values(seeds[4], (LAYERS, 5 * MIX_RANK, D), D ** -0.5, 0.125, ((1, 16), (2, 8)))
    shift_second = normal_values(seeds[5], (LAYERS, 5 * MIX_RANK, D), MIX_RANK ** -0.5, 1.0, ((1, 16), (2, 8)))
    decay_first = normal_values(seeds[6], (LAYERS, DECAY_RANK, D), D ** -0.5, 0.125, ((1, 16), (2, 8)))
    decay_second = normal_values(seeds[7], (LAYERS, DECAY_RANK, D), DECAY_RANK ** -0.5, 0.75, ((1, 16), (2, 8)))
    time_weights = normal_values(seeds[8], (LAYERS, 4, D, D), D ** -0.5, 0.125, ((2, 16), (3, 8)))
    time_output = normal_values(seeds[9], (LAYERS, D, D), D ** -0.5, 0.125, ((1, 8), (2, 16)))
    channel_key = normal_values(seeds[10], (LAYERS, D, FF), D ** -0.5, 0.125, ((1, 16), (2, 8)))
    channel_value = normal_values(seeds[11], (LAYERS, FF, D), FF ** -0.5, 0.0625, ((1, 8), (2, 16)))
    channel_recept = normal_values(seeds[12], (LAYERS, D, D), D ** -0.5, 0.125, ((1, 16), (2, 8)))
    return dict(hidden=hidden, cotangent=cotangent, opening_flags=opening_flags, vectors=vectors, shift_first=shift_first, shift_second=shift_second, decay_first=decay_first, decay_second=decay_second, time_weights=time_weights, time_output=time_output, channel_key=channel_key, channel_value=channel_value, channel_recept=channel_recept)


@jax.custom_vjp
def low(v):
    return lax.optimization_barrier(v.astype(jnp.bfloat16)).astype(jnp.float32)

@jax.custom_vjp
def low_back(v):
    return v

def low_keep(v):
    return (low(v), None)

def low_pass(kept, grad):
    return (grad,)

def back_keep(v):
    return (v, None)

def back_low(kept, grad):
    return (low(grad),)
low.defvjp(low_keep, low_pass)
low_back.defvjp(back_keep, back_low)
finest_accuracy = lax.Precision.HIGHEST
group_epsilon = 0.00064

def matmul(operand, matrix):
    return jnp.einsum('...i,ij->...j', operand, matrix, precision=finest_accuracy)

def layer_norm(payload_lines, gain_row, bias_row):
    centered = payload_lines - lax.optimization_barrier(jnp.mean(payload_lines, -1, keepdims=True))
    return centered * lax.rsqrt(lax.optimization_barrier(jnp.mean(centered * centered, -1, keepdims=True)) + 1e-05) * gain_row + bias_row

def shift_rows(payload_lines, retention_ratio):
    earlier = jnp.concatenate([jnp.zeros_like(payload_lines[:, :1]), payload_lines[:, :-1]], axis=1)
    return earlier * retention_ratio[:, :, None]

def scaled_memory_update(acceptance_lines, lookup_table, payload_lines, logarithmic_fading, extra_weight_array, retention_ratio):

    def to_blocks(array):
        return jnp.moveaxis(array.reshape(BATCH, SPAN // 16, 16, ATTENTION_COUNT, CHANNELS_PER_ATT), 1, 0)
    blocks = (to_blocks(acceptance_lines), to_blocks(lookup_table), to_blocks(payload_lines), to_blocks(logarithmic_fading), jnp.moveaxis(retention_ratio.reshape(BATCH, SPAN // 16, 16), 1, 0))
    extra_split_apart = extra_weight_array.reshape(ATTENTION_COUNT, CHANNELS_PER_ATT)

    def token_step(memory_current, token):
        symbol_acceptance, token_keys, token_values, token_decay, token_keep = token
        memory_current = memory_current * token_keep[:, None, None, None]
        dyadic_tensor = token_keys[..., :, None] * token_values[..., None, :]
        tier_result = jnp.einsum('qaz,qazh->qah', symbol_acceptance, memory_current + extra_split_apart[..., None] * dyadic_tensor, precision=finest_accuracy)
        return (jnp.exp(token_decay)[..., None] * memory_current + dyadic_tensor, tier_result)

    def block_step(memory_current, block_inputs):
        moved = tuple((jnp.moveaxis(block_piece, 1, 0) for block_piece in block_inputs))
        memory_current, outputs = lax.scan(token_step, memory_current, moved)
        return (memory_current, jnp.moveaxis(outputs, 0, 1))
    initial = jnp.zeros((BATCH, ATTENTION_COUNT, CHANNELS_PER_ATT, CHANNELS_PER_ATT), jnp.float32)
    final_state, outputs = lax.scan(jax.checkpoint(block_step), initial, blocks)
    return jnp.moveaxis(outputs, 0, 1).reshape(BATCH, SPAN, D)

def time_mix(normed, vector_rows, first, second, decay_one, decay_two, weights_in, weight_out, retention_ratio):
    differ = shift_rows(normed, retention_ratio) - normed
    mixed = low(normed + differ * vector_rows[2])
    shift_inner = low(jnp.tanh(low_back(matmul(mixed, first.T))))
    targets = []
    for target_index in range(5):
        lower_edge = target_index * MIX_RANK
        upper_edge = (target_index + 1) * MIX_RANK
        mix_term = low_back(matmul(shift_inner[..., lower_edge:upper_edge], second[lower_edge:upper_edge]))
        targets.append(low(normed + differ * (vector_rows[3 + target_index] + mix_term)))
    decay_hidden = low(jnp.tanh(low_back(matmul(targets[0], decay_one.T))))
    logarithmic_fading = -jnp.exp(vector_rows[8] + low_back(matmul(decay_hidden, decay_two)))
    lookup_table = low_back(matmul(targets[1], weights_in[0]))
    payload_lines = low_back(matmul(targets[2], weights_in[1]))
    acceptance_lines = low_back(matmul(targets[3], weights_in[2]))
    gate_pre = low_back(matmul(targets[4], weights_in[3]))
    mixed_out = scaled_memory_update(acceptance_lines, lookup_table, payload_lines, logarithmic_fading, vector_rows[9], retention_ratio)
    grouped = mixed_out.reshape(BATCH, SPAN, ATTENTION_COUNT, CHANNELS_PER_ATT)
    centered = grouped - lax.optimization_barrier(jnp.mean(grouped, -1, keepdims=True))
    normal_random_draw = centered * lax.rsqrt(lax.optimization_barrier(jnp.mean(centered * centered, -1, keepdims=True)) + group_epsilon)
    normed_out = normal_random_draw.reshape(BATCH, SPAN, D) * vector_rows[10] + vector_rows[11]
    gated = low(normed_out * jax.nn.silu(gate_pre))
    return low_back(matmul(gated, weight_out))

def channel_mix(normed, vector_rows, key_weight, value_weight, recept_weight, retention_ratio):
    differ = shift_rows(normed, retention_ratio) - normed
    pair_key = low(normed + differ * vector_rows[14])
    pair_recept = low(normed + differ * vector_rows[15])
    key_pre = low_back(matmul(pair_key, key_weight))
    squared = low(jnp.square(jax.nn.softplus(key_pre)))
    channel_out = low_back(matmul(squared, value_weight))
    recept_gate = jax.nn.sigmoid(low_back(matmul(pair_recept, recept_weight)))
    return recept_gate * channel_out

def forward(hidden, vectors, shift_first, shift_second, decay_first, decay_second, time_weights, time_output, channel_key, channel_value, channel_recept, retention_ratio):
    current = hidden
    for layer_index in range(LAYERS):
        vector_rows = vectors[layer_index]
        normed = layer_norm(current, vector_rows[0], vector_rows[1])
        current = current + time_mix(normed, vector_rows, shift_first[layer_index], shift_second[layer_index], decay_first[layer_index], decay_second[layer_index], time_weights[layer_index], time_output[layer_index], retention_ratio)
        normed_two = layer_norm(current, vector_rows[12], vector_rows[13])
        current = current + channel_mix(normed_two, vector_rows, channel_key[layer_index], channel_value[layer_index], channel_recept[layer_index], retention_ratio)
    return current

def reference(hidden, cotangent, opening_flags, vectors, shift_first, shift_second, decay_first, decay_second, time_weights, time_output, channel_key, channel_value, channel_recept):
    retention_ratio = 1.0 - opening_flags.astype(jnp.float32)
    params = tuple((array.astype(jnp.float32) for array in (hidden, vectors, shift_first, shift_second, decay_first, decay_second, time_weights, time_output, channel_key, channel_value, channel_recept)))

    def wrapped(*inputs):
        return forward(*inputs, retention_ratio)
    result, reverse_function = jax.vjp(wrapped, *params)
    grads = reverse_function(cotangent.astype(jnp.float32))
    return (result, grads[0], grads[1], grads[2], grads[3], grads[4], grads[5], grads[6], grads[7], grads[8], grads[9], grads[10])
```

```python
import functools
from types import SimpleNamespace

import jax
import jax.numpy as jnp
import numpy as np
from jax import lax
from jax.experimental import pallas as pl
from jax.experimental.pallas import tpu as pltpu
from jax.sharding import PartitionSpec as P

MESH = pl.DeviceIdType.MESH
BF = jnp.bfloat16
F32 = jnp.float32
EPS = 1e-5
GEPS = 64e-5
N = 512
TB = 256
TC = 32
W = 256
C = 64
LV = 6
D = 2048
FFL = 896
VMEM_LIMIT = 63 * 2**20
R_FIRST, R_SECOND, R_DECAY1, R_VEC, R_DECAY2 = 0, 160, 320, 384, 400


def nt(a, b):
    return lax.dot_general(a, b, (((1,), (1,)), ((), ())), preferred_element_type=F32)


def nn(a, b):
    return jnp.dot(a, b, preferred_element_type=F32)


def place():
    return lax.axis_index("seq"), lax.axis_index("head")


def sibling():
    s, h = place()
    return s, h // 2 * 2 + 1 - lax.rem(h, 2)


def chip(k, core=0):
    h = place()[1]
    c = lax.rem(h, 2)
    return lax.rem(h // 2 + k, 4) * 2 + (1 - c if core else c)


def zdev(k):
    return place()[0], chip(k)


def seq_index(first, ka, kb):
    s = place()[0]
    x, y = s // 4, lax.rem(s, 4)
    if first:
        return lax.rem(x + ka, 4) * 4 + lax.rem(y + kb, 4)
    return lax.rem(x + kb, 4) * 4 + lax.rem(y + ka, 4)


def seq_dev(first, ka, kb):
    return seq_index(first, ka, kb), place()[1]


class Copy:
    def __init__(self, net, i, make):
        self.net, self.i, self.make = net, i, make

    def desc(self):
        src, dst, dev = self.make()
        return pltpu.make_async_remote_copy(
            src_ref=src,
            dst_ref=dst,
            send_sem=self.net.ss.at[self.i],
            recv_sem=self.net.rs.at[self.i],
            device_id=dev,
            device_id_type=MESH,
        )

    def start(self):
        self.desc().start()
        self.net.out.append(self)

    def wait_recv(self):
        self.desc().wait_recv()

    def wait_send(self):
        self.desc().wait_send()


class Net:
    def __init__(self, ss, rs):
        self.ss, self.rs, self.n, self.out = ss, rs, 0, []

    def copy(self, make):
        self.n += 1
        return Copy(self, self.n - 1, make)

    def drain(self, copies=None):
        for c in list(self.out) if copies is None else copies:
            c.wait_send()
            self.out.remove(c)


def greet(peers):
    b = pltpu.get_barrier_semaphore()
    for p in peers:
        pl.semaphore_signal(b, inc=1, device_id=p, device_id_type=MESH)
    pl.semaphore_wait(b, len(peers))


def head_peers():
    s, h = place()
    return [(s, lax.rem(h + k, 8)) for k in range(1, 8)]


def seq_peers():
    s, h = place()
    return [(lax.rem(s + k, 16), h) for k in range(1, 16)]


def diagonal_peers(step):
    s, h = place()
    return [(lax.rem(s + step, 16), lax.rem(h + k, 8)) for k in range(1, 8)]


ORDER = (1, 3, 2)


def half(ref, i):
    n = ref.shape[0]
    m = n // 2 if len(ref.shape) == 3 else (n // 2 + 15) // 16 * 16
    return ref.at[m:n] if i else ref.at[0:m]


class HeadGather:
    def __init__(self, net, slot):
        self.net = net

        def own():
            return slot(place()[1])

        def at(k):
            return slot(chip(k))

        def copy(ref, dev):
            return net.copy(lambda: (ref(), ref(), dev()))

        up, down = lambda: zdev(1), lambda: zdev(3)
        self.ua = copy(lambda: half(own(), 0), up)
        self.db = copy(lambda: half(own(), 1), down)
        self.ub = copy(lambda: half(own(), 1), up)
        self.da = copy(lambda: half(own(), 0), down)
        self.mine = copy(own, sibling)
        self.fa = copy(lambda: half(at(3), 0), up)
        self.fb = copy(lambda: half(at(1), 1), down)
        self.s3 = copy(lambda: at(3), sibling)
        self.s1 = copy(lambda: at(1), sibling)
        self.sa = copy(lambda: half(at(2), 0), sibling)
        self.sb = copy(lambda: half(at(2), 1), sibling)

    def start(self):
        for c in (self.ua, self.db, self.ub, self.da, self.mine):
            c.start()

    def relay(self):
        self.ua.wait_recv()
        self.fa.start()
        self.db.wait_recv()
        self.fb.start()
        self.ub.wait_recv()
        self.s3.start()
        self.da.wait_recv()
        self.s1.start()

    def relay_far(self):
        self.fa.wait_recv()
        self.sa.start()
        self.fb.wait_recv()
        self.sb.start()

    def finish(self):
        for c in (self.mine, self.s3, self.s1, self.sa, self.sb):
            c.wait_recv()

    def drain(self):
        near = [self.ua, self.db, self.ub, self.da, self.mine]
        self.net.drain(near + [self.fa, self.fb, self.s3, self.s1, self.sa, self.sb])


class HeadScatter:
    def __init__(self, net, part, fromsib, tosend, fromz):
        self.net, self.part, self.fromsib, self.tosend, self.fromz = net, part, fromsib, tosend, fromz
        self.a = {
            k: net.copy(lambda k=k: (part.at[chip(k, 1)], fromsib.at[k], sibling()))
            for k in range(4)
        }

        def copy(i, j, k, dev):
            return net.copy(lambda: (half(tosend.at[i], k), half(fromz.at[j], k), zdev(dev)))

        self.fa, self.fb = copy(1, 2, 0, 1), copy(1, 2, 1, 3)
        self.ua, self.ub = copy(0, 0, 0, 1), copy(0, 0, 1, 1)
        self.da, self.db = copy(2, 1, 0, 3), copy(2, 1, 1, 3)
        self.all = [*self.a.values(), self.fa, self.fb, self.ua, self.ub, self.da, self.db]

    def theirs(self, k):
        return chip(k, 1)

    def ours(self, k):
        return chip(k)

    def give(self, k):
        self.a[k].start()

    def both(self, k, i):
        own = half(self.part.at[chip(k)], i)[...].astype(F32)
        return own + half(self.fromsib.at[k], i)[...].astype(F32)

    def put(self, i, k, x):
        half(self.tosend.at[i], k)[...] = x.astype(BF)

    def pass_far(self):
        self.a[2].wait_recv()
        self.put(1, 0, self.both(2, 0))
        self.fa.start()
        self.put(1, 1, self.both(2, 1))
        self.fb.start()
        self.a[1].wait_recv()
        self.put(0, 1, self.both(1, 1))
        self.ub.start()
        self.a[3].wait_recv()
        self.put(2, 0, self.both(3, 0))
        self.da.start()

    def pass_near(self):
        far = self.fromz.at[2]
        self.fa.wait_recv()
        self.put(0, 0, self.both(1, 0) + half(far, 0)[...].astype(F32))
        self.ua.start()
        self.fb.wait_recv()
        self.put(2, 1, self.both(3, 1) + half(far, 1)[...].astype(F32))
        self.db.start()

    def total(self):
        self.a[0].wait_recv()
        t = self.part[chip(0)].astype(F32) + self.fromsib[0].astype(F32)
        for c in (self.ub, self.da, self.ua, self.db):
            c.wait_recv()
        return t + self.fromz[0].astype(F32) + self.fromz[1].astype(F32)

    def drain(self):
        self.net.drain(self.all)


class SeqGather:
    def __init__(self, net, src, slot, xfirst, sem):
        self.net, self.src, self.slot, self.sem = net, src, slot, sem

        def at(k):
            return slot(seq_index(xfirst, k, 0))

        self.first = {
            k: net.copy(lambda k=k: (src, at(0), seq_dev(xfirst, k, 0))) for k in ORDER
        }
        self.own2 = [
            net.copy(lambda k=k: (src, at(0), seq_dev(xfirst, 0, k))) for k in (1, 3)
        ]
        self.second = {
            (k, j): net.copy(lambda k=k, j=j: (at(4 - k), at(4 - k), seq_dev(xfirst, 0, j)))
            for k in ORDER
            for j in (1, 3)
        }

        def came(k, j):
            return slot(seq_index(xfirst, (4 - k) % 4, j))

        self.far = {
            k: net.copy(
                lambda k=k, j=j: (came(k, 4 - j), came(k, 4 - j), seq_dev(xfirst, 0, j))
            )
            for k, j in ((0, 1), (1, 1), (3, 3), (2, 3))
        }

    def local(self):
        return pltpu.make_async_copy(self.src, self.slot(place()[0]), self.sem)

    def p0(self):
        self.local().start()
        for c in self.first.values():
            c.start()

    def p1(self):
        self.p0()
        for c in self.own2:
            c.start()

    def p2(self, own=False):
        if own:
            for c in self.own2:
                c.start()
        for k in ORDER:
            self.first[k].wait_recv()
            for j in (1, 3):
                self.second[k, j].start()

    def p3(self):
        self.own2[0].wait_recv()
        self.far[0].start()
        for k, j in ((1, 1), (3, 3), (2, 3)):
            self.second[k, j].wait_recv()
            self.far[k].start()

    def finish(self):
        self.local().wait()
        self.own2[1].wait_recv()
        for k, j in ((1, 3), (3, 1), (2, 1)):
            self.second[k, j].wait_recv()
        for c in self.far.values():
            c.wait_recv()

    def drain(self):
        self.net.drain(
            [*self.first.values(), *self.own2, *self.second.values(), *self.far.values()]
        )


class SeqScatter:
    def __init__(self, net, src, recv, acc, recv2, xfirst, own_sem=None, sems=None):
        self.net, self.src, self.recv, self.acc, self.recv2 = net, src, recv, acc, recv2
        self.xfirst, self.own_sem, self.sems = xfirst, own_sem, sems
        f = xfirst
        self.c1 = {
            k: net.copy(
                lambda k=k: (src.at[pl.ds(self.line(0, k) * 4, 4)], recv.at[k - 1], seq_dev(f, k, 0))
            )
            for k in ORDER
        }
        self.c2 = {
            k: net.copy(lambda k=k: (acc.at[self.line(1, k)], recv2.at[k - 1], seq_dev(f, 0, k)))
            for k in ORDER
        }

    def line(self, axis, k):
        s = place()[0]
        x, y = s // 4, lax.rem(s, 4)
        return lax.rem((x if (axis == 0) == self.xfirst else y) + k, 4)

    def own(self):
        return pltpu.make_async_copy(
            self.src.at[pl.ds(self.line(0, 0) * 4, 4)], self.acc, self.own_sem
        )

    def near(self):
        self.c1[1].start()
        self.c1[3].start()

    def far(self):
        self.c1[2].start()

    def p2(self, stage=None):
        for k in ORDER:
            self.c1[k].wait_recv()
        if stage is None:
            a = self.line(0, 0) * 4

            def body(j):
                t = self.src[a + j].astype(F32) + self.recv[0, j].astype(F32)
                t = t + self.recv[1, j].astype(F32) + self.recv[2, j].astype(F32)
                self.acc[j] = t.astype(BF)

            fori(4, body)
        else:
            copies = [
                pltpu.make_async_copy(self.recv.at[:, j], stage[j % 2], self.sems.at[j])
                for j in range(4)
            ]
            copies[0].start()
            self.own().wait()
            for j in range(4):
                if j < 3:
                    copies[j + 1].start()
                copies[j].wait()
                st = stage[j % 2]
                t = self.acc[j].astype(F32) + st[0].astype(F32)
                self.acc[j] = (t + st[1].astype(F32) + st[2].astype(F32)).astype(BF)
        for k in ORDER:
            self.c2[k].start()

    def finish(self, out):
        for k in ORDER:
            self.c2[k].wait_recv()
        t = self.acc[self.line(1, 0)].astype(F32) + self.recv2[0].astype(F32)
        out[...] = t + self.recv2[1].astype(F32) + self.recv2[2].astype(F32)


def fori(n, body):
    def step(i, carry):
        body(i)
        return carry

    lax.fori_loop(0, n, step, 0)


def row_stats(x3):
    m = jnp.sum(jnp.sum(x3, axis=0), axis=1, keepdims=True) / D
    d = x3 - m[None]
    v = jnp.sum(jnp.sum(d * d, axis=0), axis=1, keepdims=True) / D
    return m, lax.rsqrt(v + EPS)


def iota(shape, dim):
    return lax.broadcasted_iota(jnp.int32, shape, dim)


def shift_down(u, first, keep):
    r = pltpu.roll(u, 1, 0)
    return jnp.where(iota(u.shape, 0) == 0, first, r) * keep


def shift_up(u):
    return jnp.where(iota(u.shape, 0) == u.shape[0] - 1, 0.0, pltpu.roll(u, u.shape[0] - 1, 0))


def rows_of(b):
    return slice(b * TB, (b + 1) * TB)


def slab_of(ref, i):
    return ref[:, i].reshape(TB, W)


class Norm1:
    def __init__(self, R):
        self.R = R

    def stats(self, b):
        R = self.R

        def body(i):
            at = pl.multiple_of(i * 64, 64)
            m, r = row_stats(R.xF[b, :, pl.ds(at, 64), :].astype(F32))
            R.mean[pl.ds(b * TB + at, 64), :] = m
            R.rstd[pl.ds(b * TB + at, 64), :] = r

        fori(4, body)

    def edge_stats(self):
        m, r = row_stats(self.R.bord[...].astype(F32))
        self.R.bmean[...] = m
        self.R.brstd[...] = r

    def block(self, i, b):
        R = self.R
        v = R.smF[i, R_VEC : R_VEC + 16, :].astype(F32)
        rows = rows_of(b)
        n = (R.xF[b, i].astype(F32) - R.mean[rows, :]) * R.rstd[rows, :]
        normed = n * v[0:1] + v[1:2]
        at = slice(16 * b, 16 * b + 16)
        e = (R.bord[i, at, :].astype(F32) - R.bmean[at, :]) * R.brstd[at, :]
        first = (e * v[0:1] + v[1:2])[15:16]
        differ = shift_down(normed, first, R.keep[rows, :]) - normed
        return n, normed, differ, v


def tree(r, k, wk, keep):
    row = iota((C, W), 0)
    p = jnp.broadcast_to(keep, (C, W))
    q = jnp.ones((C, W), F32)
    t = wk
    out = []
    for level in range(LV):
        m = 1 << level
        second = (row // m) % 2 == 1
        e = jnp.where(second, p, q)
        out.append((jnp.where(second, r, k), e))
        other = jnp.where(second, pltpu.roll(t, m, 0), pltpu.roll(t, C - m, 0))
        p = jnp.where(second, p * other, p)
        q = jnp.where(second, q, q * other)
        t = t * other
    return out, p, q, t


def spread(x, hm):
    return jnp.concatenate([x] * 4, axis=0) * hm


def fold(st):
    f = st[:, 0:128] + st[:, 128:256]
    return jnp.concatenate([f[0:64] + f[64:128], f[128:192] + f[192:256]], axis=0)


def unfold(c, hmf):
    f = jnp.concatenate([c[0:64], c[0:64], c[64:128], c[64:128]], axis=0)
    return jnp.concatenate([f, f], axis=1) * hmf


def head_sum(x, hm):
    hi = x.astype(BF)
    lo = (x - hi.astype(F32)).astype(BF)
    return nn(hi, hm) + nn(lo, hm)


def constants():
    sel = np.zeros((464, 512), np.float32)
    for base, count, off in ((0, 10, 0), (160, 10, 10), (320, 4, 20), (384, 1, 28), (400, 4, 24)):
        for q in range(16):
            for i in range(count):
                sel[base + q * count + i, q * 32 + off + i] = 1
    shmask = np.zeros((8, 160), np.float32)
    for j in range(5):
        shmask[j, 32 * j : 32 * j + 32] = 1
    f = np.arange(256) // 64
    hm = (f[:, None] == f[None, :]).astype(np.float32)
    t = np.arange(64)[:, None]
    u = (np.arange(256) % 64)[None, :]
    lev, levt, sums = [], [], []
    a = np.arange(64)[:, None]
    e = np.arange(64)[None, :]
    for m in (1, 2, 4, 8, 16, 32):
        same = t // (2 * m) == u // (2 * m)
        lev.append(same & (t // m % 2 == 1) & (u // m % 2 == 0))
        levt.append(same & (t // m % 2 == 0) & (u // m % 2 == 1))
        half = a // m == e // m
        sums.append(half & np.where(a // m % 2 == 0, e < a, e > a))
    sums += [e < a, e > a]
    lev = np.stack(lev + levt).astype(np.float32)
    sums = np.concatenate(sums, axis=1).astype(np.float32)
    return (
        jnp.asarray(sel, BF),
        jnp.asarray(shmask, F32),
        jnp.asarray(hm, BF),
        jnp.asarray(lev, F32),
        jnp.asarray(sums, BF),
    )


def layer_kernel(names, *refs):
    R = SimpleNamespace(**dict(zip(names, refs)))
    s, h = place()
    prv, nxt = lax.rem(s + 15, 16), lax.rem(s + 1, 16)
    net = Net(R.ss, R.rs)
    both = (0, 1)
    z1 = jnp.zeros((1, W), F32)

    hid = [HeadGather(net, lambda i, b=b: R.xF.at[b, i]) for b in both]
    smg = HeadGather(net, lambda i: R.smF.at[i])
    midg = [HeadGather(net, lambda i, b=b: R.midF.at[b, i]) for b in both]
    gkvg = [HeadGather(net, lambda i, b=b: R.gF.at[b, i]) for b in both]
    gzg = [HeadGather(net, lambda i, b=b: R.midF.at[b, i]) for b in both]

    def scatter(b, e):
        return HeadScatter(
            net, R.part.at[b], R.fromsib.at[e, b], R.tosend.at[b], R.fromz.at[e, b]
        )

    rs1, rs2, rs3, rs4 = [[scatter(b, e) for b in both] for e in (0, 1, 0, 1)]

    def rows128(ref, q):
        return ref.at[pl.ds(pl.multiple_of(q * 128, 128), 128), :]

    def cols128(ref, q):
        return ref.at[:, pl.ds(pl.multiple_of(q * 128, 128), 128)]

    tws = [
        SeqGather(net, R.tw.at[i], lambda q, i=i: rows128(R.twV.at[i], q), i % 2 == 0, R.ls.at[i])
        for i in range(4)
    ]
    tos = SeqGather(net, R.to, lambda q: cols128(R.toV, q), True, R.ls.at[4])
    cks = SeqGather(net, R.ck, lambda q: rows128(R.ckF, q), True, R.ls.at[5])
    cvs = SeqGather(net, R.cv, lambda q: cols128(R.cvF, q), False, R.ls.at[6])
    crs = SeqGather(net, R.cr, lambda q: rows128(R.crF, q), False, R.ls.at[7])
    sca = SeqScatter(net, R.gaH, R.ra1, R.ra2, R.ra3, True, R.ls.at[8], R.ls.at[20:24])
    scb = SeqScatter(net, R.gbH, R.rb1, R.rb2, R.rb3, False, R.ls.at[9], R.ls.at[24:28])

    def seq_step(k):
        sq, hq = place()
        return lax.rem(sq + k, 16), hq

    smalls = [
        net.copy(lambda k=k: (R.small, R.sm.at[place()[0]], seq_step(k))) for k in range(1, 16)
    ]

    def beside(k, step):
        sq, hq = place()
        return lax.rem(sq + step, 16), lax.rem(hq + k, 8)

    edges = [net.copy(lambda k=k: (R.bsrc, R.bord.at[place()[1]], beside(k, 1))) for k in range(8)]
    cots = {
        (b, k): net.copy(
            lambda b=b, k=k: (
                R.cot.at[b, pl.ds(pl.multiple_of(beside(k, 0)[1] * TC, TC), TC), :],
                R.gch.at[b, place()[1]],
                beside(k, 0),
            )
        )
        for b in both
        for k in range(1, 8)
    }
    last = [net.copy(lambda k=k: (R.bsend.at[beside(k, 0)[1]], R.brecv.at[place()[1]], beside(k, 15))) for k in range(8)]
    rex = [
        net.copy(lambda k=k: (R.rsend, R.rrecv.at[place()[1]], beside(k, 0))) for k in range(1, 8)
    ]
    smo = [
        net.copy(lambda k=k: (R.psend.at[seq_step(k)[0]], R.psrecv.at[place()[0]], seq_step(k)))
        for k in range(1, 16)
    ]

    def mid_border(b, k):
        return pltpu.make_async_remote_copy(
            src_ref=R.mb.at[b],
            dst_ref=R.bmid.at[b],
            send_sem=R.bs.at[b * 8 + k],
            recv_sem=R.br.at[b],
            device_id=(nxt, k),
            device_id_type=MESH,
        )

    def grad_border(b, frm):
        return pltpu.make_async_remote_copy(
            src_ref=R.gsend.at[b],
            dst_ref=R.grecv.at[b, frm],
            send_sem=R.bs.at[16 + b],
            recv_sem=R.br.at[2 + b * 8 + frm],
            device_id=(prv, 7),
            device_id_type=MESH,
        )

    def carry_copy(e, b, dst, frm):
        return pltpu.make_async_remote_copy(
            src_ref=R.csend.at[e, b],
            dst_ref=R.crecv.at[b, frm],
            send_sem=R.cs.at[(2 * e + b) * 16 + dst],
            recv_sem=R.cr_.at[(2 * e + b) * 16 + frm],
            device_id=(dst, h),
            device_id_type=MESH,
        )

    def carry_each(e, b, act):
        def body(i, _):
            act(carry_copy(e, b, i, s))
            return 0

        lo, hi = (s + 1, 16) if e == 0 else (0, s)
        lax.fori_loop(lo, hi, body, 0)

    def carry_send(e, b, state, total):
        R.csend[e, b, 0:128, :] = fold(state).astype(BF)
        R.csend[e, b, 128:144, :] = jnp.concatenate(
            [total[:, 0:128], total[:, 128:256], jnp.zeros((14, 128), F32)], axis=0
        ).astype(BF)
        carry_each(e, b, lambda c: c.start())

    def carry_wait(e, b, hmf):
        R.carry[b] = jnp.zeros((128, 128), F32)

        def body(i, _):
            j = i if e == 0 else 15 - i
            carry_copy(e, b, 0, j).wait_recv()
            tt = R.crecv[b, j, 128:144, :].astype(F32)
            for g in range(2):
                at = slice(g * 64, g * 64 + 64)
                R.carry[b, at, :] = R.carry[b, at, :] * tt[g : g + 1] + R.crecv[b, j, at, :].astype(F32)
            return 0

        lax.fori_loop(0, s if e == 0 else 15 - s, body, 0)
        return unfold(R.carry[b], hmf)

    R.small[...] = jnp.concatenate(
        [a[...].astype(F32) for a in (R.sf, R.s2nd, R.d1st, R.d2nd, R.vectors)]
        + [jnp.zeros((3, W), F32)],
        axis=0,
    ).astype(BF)
    for b in both:
        R.bsrc[16 * b : 16 * b + 16, :] = R.x[b, TB - 16 : TB, :]
        R.xF[b, h] = R.x[b]
    greet(head_peers() + seq_peers() + diagonal_peers(1) + diagonal_peers(15))
    hid[0].start()
    for c in smalls + edges:
        c.start()
    hid[1].start()
    R.sm[s] = R.small[...]
    for c in smalls:
        c.wait_recv()
    for t in tws:
        t.p1()
    comp = nn(R.sel[...], R.sm[...].reshape(512, W)).astype(BF)
    R.smF[h] = comp[0:400]
    R.ds2[...] = comp[400:464]
    smg.start()
    for b in both:
        hid[b].relay()
    for t in tws:
        t.p2()
    tos.p1()
    for b in both:
        hid[b].relay_far()
    smg.relay()
    hid[0].finish()
    n1 = Norm1(R)
    n1.stats(0)
    smg.relay_far()
    hid[1].finish()
    n1.stats(1)
    for c in edges:
        c.wait_recv()
    n1.edge_stats()
    smg.finish()
    vl = R.smF[h, R_VEC : R_VEC + 16, :].astype(F32)
    hmb = R.hm[...]
    hmf = hmb.astype(F32)

    def time_forward(**kw):
        L = SimpleNamespace(**kw)

        def shift(b):
            rows = rows_of(b)
            L.mixacc[...] = jnp.zeros_like(L.mixacc)

            def body(i):
                n, normed, differ, v = n1.block(i, b)
                mixed = (normed + differ * v[2:3]).astype(BF)
                L.mixacc[...] += nt(mixed, R.smF[i, R_FIRST : R_FIRST + 160, :])

            fori(8, body)
            hidden = jnp.tanh(L.mixacc[...])
            R.sh[rows, :] = hidden
            for j in range(5):
                L.shm[j, rows, :] = (hidden * R.shmask[j : j + 1, :]).astype(BF)

        def targets(b):
            rows = rows_of(b)
            L.proj[:, rows, :] = jnp.zeros((4, TB, W), F32)
            L.dacc[...] = jnp.zeros_like(L.dacc)

            def body(i):
                col = pl.ds(pl.multiple_of(i * W, W), W)
                n, normed, differ, v = n1.block(i, b)
                second = R.smF[i, R_SECOND : R_SECOND + 160, :]
                for j in range(5):
                    mix = nn(L.shm[j, rows, :], second)
                    target = (normed + differ * (v[3 + j : 4 + j] + mix)).astype(BF)
                    if j == 0:
                        L.dacc[...] += nt(target, R.smF[i, R_DECAY1 : R_DECAY1 + 64, :])
                    else:
                        L.proj[j - 1, rows, :] += nn(target, R.twV[j - 1, col, :])

            fori(8, body)
            hidden = jnp.tanh(L.dacc[...])
            R.dh[rows, :] = hidden
            ld = -jnp.exp(vl[8:9] + nn(hidden.astype(BF), R.ds2[...]))
            R.logd[rows, :] = ld
            L.wdec[rows, :] = jnp.exp(ld) * R.keep[rows, :]
            R.proj[:, rows, :] = L.proj[:, rows, :].astype(BF)

        def states(b):
            L.st[b] = jnp.zeros((W, W), F32)
            R.tpre[8 + b : 9 + b, :] = jnp.ones((1, W), F32)

            def body(c):
                rows = pl.ds(pl.multiple_of(b * TB + c * C, C), C)
                i = b * 4 + c
                r, k, v = L.proj[2, rows, :], L.proj[0, rows, :], L.proj[1, rows, :]
                lv, p, q, t = tree(r, k, L.wdec[rows, :], R.keep[rows, :])
                for l, (a, e) in enumerate(lv):
                    L.xs[l, rows, :] = (a * e).astype(BF)
                R.rp[rows, :] = (r * p).astype(BF)
                L.starts[i] = L.st[b].astype(BF)
                R.tch[pl.ds(i, 1), :] = t[0:1]
                before = R.tpre[8 + b : 9 + b, :]
                R.tpre[pl.ds(i, 1), :] = before
                R.tpre[8 + b : 9 + b, :] = before * t[0:1]
                L.st[b] = L.st[b] * t[0:1] + nn(v.T.astype(BF), (k * q).astype(BF)) * hmf

            fori(4, body)
            carry_send(0, b, L.st[b], R.tpre[8 + b : 9 + b, :])

        def inner(b):
            def body(c):
                rows = pl.ds(pl.multiple_of(b * TB + c * C, C), C)
                r, k, v = L.proj[2, rows, :], L.proj[0, rows, :], L.proj[1, rows, :]
                a = jnp.zeros((C, W), F32)
                at = jnp.zeros((C, W), F32)
                for l in range(LV):
                    xl = L.xs[l, rows, :]
                    y = nt(xl, spread(xl, hmb))
                    a = a + y * R.levels[l]
                    at = at + y * R.levels[LV + l]
                R.scores[rows, :] = at.astype(BF)
                bonus = head_sum(r * vl[9:10] * k, hmb)
                L.ov[rows, :] = nn(a.astype(BF), spread(v.astype(BF), hmb)) + bonus * v

            fori(4, body)

        def outer(b):
            st = carry_wait(0, b, hmf)
            L.st[b] = st
            if b == 1:
                for g in (cks, crs):
                    g.p2(True)

            def body(c):
                i = b * 4 + c
                rows = pl.ds(pl.multiple_of(b * TB + c * C, C), C)
                start = L.starts[i].astype(F32) + L.st[b] * R.tpre[pl.ds(i, 1), :]
                R.starts[i] = fold(start).astype(BF)
                o = L.ov[rows, :] + nt(R.rp[rows, :], start.astype(BF))
                d = o - head_sum(o, hmb) / 64.0
                sc = lax.rsqrt(head_sum(d * d, hmb) / 64.0 + GEPS)
                gn = d * sc
                R.gnorm[rows, :] = gn
                R.gscale[rows, :] = sc
                g = L.proj[3, rows, :]
                R.gate[rows, :] = (
                    (gn * vl[10:11] + vl[11:12]) * (g * jax.nn.sigmoid(g))
                ).astype(BF)

            fori(4, body)

        def out(b):
            def body(i):
                y = nn(R.gate[rows_of(b), :], R.toV[:, pl.ds(pl.multiple_of(i * W, W), W)])
                R.part[b, :, i] = y.astype(BF).reshape(8, TC, W)

            fori(8, body)
            for k in (2, 1, 3, 0):
                rs1[b].give(k)

        for t in tws:
            t.p3()
        tos.p2()
        shift(0)
        shift(1)
        for t in tws:
            t.finish()
        for g in (cks, crs, cvs):
            g.p0()
        targets(0)
        states(0)
        tos.p3()
        targets(1)
        states(1)
        saved = pltpu.make_async_copy(R.twV, R.twF, R.ls.at[10])
        saved.start()
        inner(0)
        for c in cots.values():
            c.start()
        inner(1)
        outer(0)
        tos.finish()
        out(0)
        outer(1)
        rs1[0].pass_far()
        out(1)
        rs1[0].pass_near()
        rs1[1].pass_far()
        saved.wait()

    f32n = pltpu.VMEM((N, W), F32)
    pl.run_scoped(
        time_forward,
        mixacc=pltpu.VMEM((TB, 160), F32),
        shm=pltpu.VMEM((5, N, 160), BF),
        dacc=pltpu.VMEM((TB, 64), F32),
        proj=pltpu.VMEM((4, N, W), F32),
        wdec=f32n,
        xs=pltpu.VMEM((LV, N, W), BF),
        starts=pltpu.VMEM((8, W, W), BF),
        st=pltpu.VMEM((2, W, W), F32),
        ov=f32n,
    )

    def middle(b):
        m = rs1[b].total() + R.xF[b, :, pl.ds(pl.multiple_of(h * TC, TC), TC), :].astype(F32)
        R.mid[b] = m
        R.midF[b, h] = m.astype(BF)
        for i in range(8):
            R.mb[b, i : i + 1, :] = R.mid[b, i, TC - 1 : TC, :]
        midg[b].start()

        @pl.when(h == 7)
        def _():
            for k in range(8):
                mid_border(b, k).start()

    def channel(**kw):
        L = SimpleNamespace(**kw)
        loads = [
            pltpu.make_async_copy(a, c, R.ls.at[11 + i])
            for i, (a, c) in enumerate(((R.ckF, L.ck), (R.crF, L.cr), (R.cvF, L.cv)))
        ]

        def pairs(i):
            at = pl.ds(pl.multiple_of(lax.rem(i, 4) * N, N), N)
            return R.twV.at[i // 4, at, :], R.twV.at[2 + i // 4, at, :]

        def block(i, b):
            rows = rows_of(b)
            v = R.smF[i, R_VEC : R_VEC + 16, :].astype(F32)
            u = slab_of(R.midF.at[b], i).astype(F32)
            n2 = (u - L.mean[rows, :]) * L.rstd[rows, :] * v[12:13] + v[13:14]
            first = L.bstat[b, pl.ds(i, 1), :] * v[12:13] + v[13:14]
            return n2, shift_down(n2, first, R.keep[rows, :]) - n2, v

        def mixing(b):
            rows = rows_of(b)

            def stat_body(i):
                m, r = row_stats(R.midF[b, i].astype(F32))
                at = pl.ds(pl.multiple_of(b * TB + i * TC, TC), TC)
                L.mean[at, :] = m
                L.rstd[at, :] = r

            fori(8, stat_body)
            mid_border(b, 0).wait_recv()
            e = R.bmid[b]
            m = jnp.sum(jnp.sum(e, axis=0, keepdims=True), axis=1, keepdims=True) / D
            d = e - m
            v = jnp.sum(jnp.sum(d * d, axis=0, keepdims=True), axis=1, keepdims=True) / D
            L.bstat[b] = d * lax.rsqrt(v + EPS)
            if b == 0:
                for c in loads[0:2]:
                    c.wait()
            L.kp[rows, :] = jnp.zeros((TB, FFL), F32)
            L.rec[rows, :] = jnp.zeros((TB, W), F32)

            def body(i):
                at = pl.ds(pl.multiple_of(i * W, W), W)
                n2, d2, v = block(i, b)
                a = (n2 + d2 * v[14:15]).astype(BF)
                c = (n2 + d2 * v[15:16]).astype(BF)
                pk, pr = pairs(i)
                pk[rows, :] = a
                pr[rows, :] = c
                L.kp[rows, :] += nn(a, L.ck[at, :])
                L.rec[rows, :] += nn(c, L.cr[at, :])

            fori(8, body)
            g = jax.nn.sigmoid(L.rec[rows, :])
            L.rec[rows, :] = g
            R.gF[b, h] = (R.cot[b] * g).astype(BF).reshape(8, TC, W)
            gkvg[b].start()

        def hidden_units(b):
            def square(i):
                at = pl.ds(pl.multiple_of(b * TB + i * 64, 64), 64)
                u = L.kp[at, :]
                e = jnp.exp(-jnp.abs(u))
                p = jnp.maximum(u, 0.0) + jnp.log(1.0 + e)
                L.sq[at, :] = (p * p).astype(BF)
                L.kp[at, :] = 2.0 * p * jnp.where(u >= 0, 1.0, e) / (1.0 + e)

            fori(4, square)
            if b == 0:
                cvs.finish()
                loads[2].start()
                loads[2].wait()
            rs1[b].drain()

            def out(i):
                y = nn(L.sq[rows_of(b), :], L.cv[:, pl.ds(pl.multiple_of(i * W, W), W)])
                R.part[b, i] = y.astype(BF).reshape(8, TC, W)

            for k in (2, 1, 3, 0):
                out(rs2[b].theirs(k))
                rs2[b].give(k)
                out(rs2[b].ours(k))

        def key_grad(b):
            rows = rows_of(b)
            gkvg[b].finish()
            L.gs[...] = jnp.zeros_like(L.gs)

            def body(i):
                a = R.gF[b, i].reshape(TB, W)
                L.gs[...] += nt(a, L.cv[:, pl.ds(pl.multiple_of(i * W, W), W)])

            fori(8, body)
            L.gk[rows, :] = (L.gs[...] * L.kp[rows, :]).astype(BF)

        def result(b):
            rows = rows_of(b)
            co = rs2[b].total().reshape(TB, W)
            g = L.rec[rows, :]
            R.result[b] = slab_of(R.midF.at[b], h).astype(F32) + g * co
            L.gr[rows, :] = (R.cot[b] * co * g * (1.0 - g)).astype(BF)

        def back(b):
            rows = rows_of(b)
            rs2[b].drain()
            midg[b].drain()

            def body(i):
                at = pl.ds(pl.multiple_of(i * W, W), W)
                n2, d2, v = block(i, b)
                gpk = nt(L.gk[rows, :], L.ck[at, :])
                gpr = nt(L.gr[rows, :], L.cr[at, :])
                R.vg[i, 2 + 2 * b : 3 + 2 * b, :] = jnp.sum(gpk * d2, axis=0, keepdims=True)
                R.vg[i, 3 + 2 * b : 4 + 2 * b, :] = jnp.sum(gpr * d2, axis=0, keepdims=True)
                gd = gpk * v[14:15] + gpr * v[15:16]
                kg = gd * R.keep[rows, :]
                R.gsend[b, pl.ds(i, 1), :] = kg[0:1]
                y = gpk + gpr - gd + shift_up(kg)
                R.part[b, :, i] = y.astype(BF).reshape(8, TC, W)

            fori(8, body)
            for k in (2, 1, 3, 0):
                rs3[b].give(k)
            grad_border(b, h).start()

        def norm_back(b):
            u = R.mid[b]
            m, r = row_stats(u)
            n2 = (u - m[None]) * r[None]
            L.gout[...] = rs3[b].total()

            @pl.when(h == 7)
            def _():
                for i in range(8):
                    grad_border(b, i).wait_recv()
                t = jnp.sum(R.grecv[b], axis=0)
                for i in range(8):
                    L.gout[i, TC - 1 : TC, :] += t[i : i + 1]

            go = L.gout[...]
            gain = R.smF[:, R_VEC + 12 : R_VEC + 13, :].astype(F32)
            v12 = jnp.sum(go * n2, axis=1, keepdims=True)
            v13 = jnp.sum(go, axis=1, keepdims=True)
            if b == 0:
                R.vg[:, 0:1, :] = v12
                R.vg[:, 1:2, :] = v13
            else:
                R.vg[:, 0:1, :] += v12
                R.vg[:, 1:2, :] += v13
            gn = go * gain
            ma = jnp.sum(jnp.sum(gn, axis=0), axis=1, keepdims=True) / D
            mb = jnp.sum(jnp.sum(gn * n2, axis=0), axis=1, keepdims=True) / D
            R.midF[b, h] = (R.gch[b] + (gn - ma[None] - n2 * mb[None]) * r[None]).astype(BF)
            gzg[b].start()

        def staged(home, rows, xfirst, sem, make):
            def copies(i):
                got = []
                for e in range(2):
                    q = 2 * i + e
                    if not xfirst:
                        q = lax.rem(q, 4) * 4 + q // 4
                    at = lax.rem(i, 2)
                    got.append(
                        pltpu.make_async_copy(
                            L.stage.at[at, e, 0:rows], home.at[q], R.ls.at[sem + 2 * at + e]
                        )
                    )
                return got

            def body(i):
                @pl.when(i >= 2)
                def _():
                    for c in copies(i - 2):
                        c.wait()

                y = make(i)
                for e in range(2):
                    at = 0
                    for t in y:
                        L.stage[lax.rem(i, 2), e, at : at + t.shape[0], :] = t[
                            :, 128 * e : 128 * e + 128
                        ].astype(BF)
                        at += t.shape[0]
                for c in copies(i):
                    c.start()

            fori(8, body)
            for i in (6, 7):
                for c in copies(i):
                    c.wait()

        def value_weight():
            L.tr[...] = L.sq[...].T
            staged(
                R.gbH, FFL, False, 28, lambda i: [nn(L.tr[...], R.gF[:, i].reshape(N, W))]
            )

        def key_weight():
            L.tr[...] = L.gk[...].T
            L.grT[...] = L.gr[...].T

            def make(i):
                pk, pr = pairs(i)
                return [nn(L.tr[...], pk[...]), nn(L.grT[...], pr[...])]

            staged(R.gaH, FFL + W, True, 32, make)

        middle(0)
        rs1[1].pass_near()
        for g in (cks, crs):
            g.p3()
        midg[0].relay()
        midg[0].relay_far()
        middle(1)
        cvs.p2(True)
        for g in (cks, crs):
            g.finish()
        for c in loads[0:2]:
            c.start()
        for t in tws:
            t.drain()
        midg[0].finish()
        midg[1].relay()
        mixing(0)
        midg[1].relay_far()
        midg[1].finish()
        gkvg[0].relay()
        cvs.p3()
        mixing(1)
        gkvg[0].relay_far()
        hidden_units(0)
        gkvg[1].relay()
        rs2[0].pass_far()
        gkvg[1].relay_far()
        key_grad(0)
        rs2[0].pass_near()
        hidden_units(1)
        rs2[1].pass_far()
        result(0)
        back(0)
        rs2[1].pass_near()
        key_grad(1)
        rs3[0].pass_far()
        value_weight()
        result(1)
        rs3[0].pass_near()
        back(1)
        for c in cots.values():
            c.wait_recv()
        scb.near()
        scb.own().start()
        norm_back(0)
        rs3[1].pass_far()
        key_weight()
        sca.near()
        sca.own().start()
        gzg[0].relay()
        rs3[1].pass_near()
        gzg[0].relay_far()
        norm_back(1)

    for b in both:
        R.gch[b, h] = R.cot[b, pl.ds(pl.multiple_of(h * TC, TC), TC), :]
    pl.run_scoped(
        channel,
        ck=pltpu.VMEM((D, FFL), BF),
        cv=pltpu.VMEM((FFL, D), BF),
        cr=pltpu.VMEM((D, W), BF),
        mean=pltpu.VMEM((N, 1), F32),
        rstd=pltpu.VMEM((N, 1), F32),
        bstat=pltpu.VMEM((2, 8, W), F32),
        kp=pltpu.VMEM((N, FFL), F32),
        rec=f32n,
        sq=pltpu.VMEM((N, FFL), BF),
        gk=pltpu.VMEM((N, FFL), BF),
        gr=pltpu.VMEM((N, W), BF),
        gs=pltpu.VMEM((TB, FFL), F32),
        tr=pltpu.VMEM((FFL, N), BF),
        grT=pltpu.VMEM((W, N), BF),
        gout=pltpu.VMEM((8, TC, W), F32),
        stage=pltpu.VMEM((2, 2, FFL + W, 128), BF),
    )

    def time_backward(**kw):
        O = SimpleNamespace(**kw)
        sea = SeqScatter(net, O.ea, R.ea1, O.ea2, R.ea3, True)
        seb = SeqScatter(net, O.eb, R.eb1, O.eb2, R.eb3, False)
        O.shT[...] = R.sh[...].T.astype(BF)
        for b in both:
            gkvg[b].drain()

        def shm(j, rows):
            return (R.sh[rows, :] * R.shmask[j : j + 1, :]).astype(BF)

        def wkv_backward(**kw):
            L = SimpleNamespace(**kw)

            def gated(b):
                rows = rows_of(b)
                L.gated[rows, :] = jnp.zeros((TB, W), F32)

                def body(i):
                    a = slab_of(R.midF.at[b], i)
                    L.gated[rows, :] += nt(a, R.toV[:, pl.ds(pl.multiple_of(i * W, W), W)])

                fori(8, body)

                def gate_body(i, acc):
                    at = pl.ds(pl.multiple_of(b * TB + i * 64, 64), 64)
                    gd = L.gated[at, :]
                    gn = R.gnorm[at, :]
                    g = R.proj[3, at, :].astype(F32)
                    sg = jax.nn.sigmoid(g)
                    gno = gd * (g * sg)
                    dg = gd * (gn * vl[10:11] + vl[11:12]) * sg * (1.0 + g * (1.0 - sg))
                    O.gp[3, at, :] = dg.astype(BF)
                    gg = gno * vl[10:11]
                    ma = head_sum(gg, hmb) / 64.0
                    mb = head_sum(gg * gn, hmb) / 64.0
                    L.go[at, :] = R.gscale[at, :] * (gg - ma - gn * mb)
                    return (
                        acc[0] + jnp.sum(gno * gn, axis=0, keepdims=True),
                        acc[1] + jnp.sum(gno, axis=0, keepdims=True),
                    )

                return lax.fori_loop(0, 4, gate_body, (z1, z1))

            def adjoint(b):
                L.ds[b] = jnp.zeros((W, W), F32)
                L.tsuf[8 + b : 9 + b, :] = jnp.ones((1, W), F32)

                def body(e):
                    i = b * 4 + 3 - e
                    rows = pl.ds(pl.multiple_of(i * C, C), C)
                    L.dsl[i] = L.ds[b].astype(BF)
                    t = R.tch[pl.ds(i, 1), :]
                    after = L.tsuf[8 + b : 9 + b, :]
                    L.tsuf[pl.ds(i, 1), :] = after
                    L.tsuf[8 + b : 9 + b, :] = after * t
                    L.ds[b] = L.ds[b] * t + nn(L.go[rows, :].T.astype(BF), R.rp[rows, :]) * hmf

                fori(4, body)
                carry_send(1, b, L.ds[b], L.tsuf[8 + b : 9 + b, :])

            def output_weight():
                L.gatT[...] = R.gate[...].T

                def body(i):
                    a = R.midF[:, :, i].reshape(N, W)
                    put(O.eb, i, 0, nn(L.gatT[...], a).astype(BF), False)

                fori(8, body)

            def gate_weight():
                O.gpT[3] = O.gp[3].T

                def body(i):
                    y = jnp.zeros((W, W), F32)
                    for b in both:
                        rows = rows_of(b)
                        n, normed, differ, v = n1.block(i, b)
                        mix = nn(shm(4, rows), R.smF[i, R_SECOND : R_SECOND + 160, :])
                        target = (normed + differ * (v[7:8] + mix)).astype(BF)
                        y = y + nn(O.gpT[3, :, rows], target)
                    put(O.ea, i, 0, y.astype(BF), True)

                fori(8, body)

            def inner(b, gu):
                def body(c, gu):
                    rows = pl.ds(pl.multiple_of(b * TB + c * C, C), C)
                    r, k, v = [R.proj[j, rows, :].astype(F32) for j in (2, 0, 1)]
                    g, kp = L.go[rows, :], R.keep[rows, :]
                    lv, p, q, t = tree(r, k, jnp.exp(R.logd[rows, :]) * kp, kp)
                    L.pP[rows, :] = p
                    L.pQ[rows, :] = q
                    vb, gb = v.astype(BF), g.astype(BF)
                    gsp = spread(gb, hmb)
                    da = nt(gb, spread(vb, hmb))
                    dat = nt(vb, gsp)
                    row = iota((C, W), 0)
                    agr = jnp.zeros((C, W), F32)
                    agk = jnp.zeros((C, W), F32)
                    ys = []
                    for l, (a, e) in enumerate(lv):
                        x = (a * e).astype(BF)
                        d = (da * R.levels[l] + dat * R.levels[LV + l]).astype(BF)
                        gx = nn(d, spread(x, hmb))
                        second = (row // (1 << l)) % 2 == 1
                        ge = gx * e
                        agr = agr + jnp.where(second, ge, 0.0)
                        agk = agk + jnp.where(second, 0.0, ge)
                        ys.append((x.astype(F32) * gx).astype(BF))
                    L.gG[rows, :] = nn(R.sums[:, 0 : LV * C], jnp.concatenate(ys, axis=0))
                    u = vl[9:10]
                    dad = head_sum(g * v, hmb)
                    bonus = head_sum(r * u * k, hmb)
                    L.gr[rows, :] = agr + u * k * dad
                    L.gk[rows, :] = agk + u * r * dad
                    L.gv[rows, :] = nn(R.scores[rows, :], gsp) + bonus * g
                    return gu + jnp.sum(r * k * dad, axis=0, keepdims=True)

                return lax.fori_loop(0, 4, body, gu)

            def outer(b, g8):
                L.ds[b] = carry_wait(1, b, hmf)

                def body(c, g8):
                    i = b * 4 + c
                    rows = pl.ds(pl.multiple_of(i * C, C), C)
                    st = unfold(R.starts[i].astype(F32), hmf)
                    de = L.dsl[i].astype(F32) + L.ds[b] * L.tsuf[pl.ds(i, 1), :]
                    deb = de.astype(BF)
                    p, q = L.pP[rows, :], L.pQ[rows, :]
                    kq = (R.proj[0, rows, :].astype(F32) * q).astype(BF)
                    rpc = R.rp[rows, :]
                    gkq = nn(R.proj[1, rows, :], deb)
                    grp = nn(L.go[rows, :].astype(BF), st.astype(BF))
                    O.gp[1, rows, :] = (L.gv[rows, :] + nt(kq, deb)).astype(BF)
                    O.gp[0, rows, :] = (L.gk[rows, :] + gkq * q).astype(BF)
                    O.gp[2, rows, :] = (L.gr[rows, :] + grp * p).astype(BF)
                    ky = (kq.astype(F32) * gkq).astype(BF)
                    ry = (rpc.astype(F32) * grp).astype(BF)
                    cst = jnp.sum(st * de, axis=0, keepdims=True) * R.tch[pl.ds(i, 1), :]
                    gl = nn(R.sums[:, LV * C :], jnp.concatenate([ky, ry], axis=0))
                    gw = (L.gG[rows, :] + gl + cst) * R.logd[rows, :]
                    O.gw[rows, :] = gw.astype(BF)
                    return g8 + jnp.sum(gw, axis=0, keepdims=True)

                return lax.fori_loop(0, 4, body, g8)

            gzg[0].finish()
            gzg[1].relay()
            a10, a11 = gated(0)
            adjoint(0)
            gzg[1].relay_far()
            gzg[1].finish()
            b10, b11 = gated(1)
            adjoint(1)
            sca.far()
            scb.far()
            output_weight()
            seb.near()
            seb.far()
            g9 = inner(0, z1)
            gate_weight()
            sea.near()
            sea.far()
            g9 = inner(1, g9)
            scb.p2([L.stage.at[0, :, 0:FFL], L.stage.at[1, :, 0:FFL]])
            g8 = outer(0, z1)
            sca.p2([L.stage.at[0], L.stage.at[1]])
            g8 = outer(1, g8)
            R.gvec[0:1, :] = g8
            R.gvec[1:2, :] = g9
            R.gvec[2:3, :] = a10 + b10
            R.gvec[3:4, :] = a11 + b11

        reload = pltpu.make_async_copy(R.twF, R.twV, R.ls.at[10])
        reload.start()
        pl.run_scoped(
            wkv_backward,
            gated=f32n,
            go=f32n,
            gr=f32n,
            gk=f32n,
            gv=f32n,
            gG=f32n,
            pP=f32n,
            pQ=f32n,
            dsl=pltpu.VMEM((8, W, W), BF),
            ds=pltpu.VMEM((2, W, W), F32),
            tsuf=pltpu.VMEM((16, W), F32),
            gatT=pltpu.VMEM((W, N), BF),
            stage=pltpu.VMEM((2, 3, FFL + W, 128), BF),
        )

        for j in range(3):
            O.gpT[j] = O.gp[j].T
        dhv = R.dh[...]
        gdv = nt(O.gw[...], R.ds2[...]) * (1.0 - dhv * dhv)
        O.gdp[...] = gdv.astype(BF)
        O.gdpT[...] = gdv.T.astype(BF)
        O.lsm[400:464, :] = nn(dhv.T.astype(BF), O.gw[...])
        reload.wait()

        def normed_back(**kw):
            L = SimpleNamespace(**kw)
            sta = SeqScatter(net, L.ta, R.ta1, L.ta2, R.ta3, True)
            stb = SeqScatter(net, L.tb, R.tb1, L.tb2, R.tb3, False)
            sms = HeadScatter(net, L.sg, R.sgsib, L.sgsend, R.sgz)
            L.gsh[...] = jnp.zeros_like(L.gsh)
            rank = iota((160, W), 0)

            def target_body(i):
                at = pl.ds(pl.multiple_of(i * W, W), W)
                second = R.smF[i, R_SECOND : R_SECOND + 160, :]
                dfirst = R.smF[i, R_DECAY1 : R_DECAY1 + 64, :]
                ws = [jnp.zeros((W, W), F32) for _ in range(3)]
                gsec = jnp.zeros((160, W), F32)
                gd1 = jnp.zeros((64, W), F32)
                rowsum = [z1] * 5
                for b in both:
                    rows = rows_of(b)
                    n, normed, differ, v = n1.block(i, b)
                    a1 = jnp.zeros((TB, W), F32)
                    a2 = jnp.zeros((TB, W), F32)
                    for j in range(5):
                        m = v[3 + j : 4 + j] + nn(shm(j, rows), second)
                        if j < 4:
                            target = (normed + differ * m).astype(BF)
                        if j == 0:
                            gt = nn(O.gdp[rows, :], dfirst)
                            gd1 = gd1 + nn(O.gdpT[:, rows], target)
                        else:
                            gt = nt(O.gp[j - 1, rows, :], R.twV[j - 1, at, :])
                            if j < 4:
                                ws[j - 1] = ws[j - 1] + nn(O.gpT[j - 1, :, rows], target)
                        a1 = a1 + gt
                        a2 = a2 + gt * m
                        qv = gt * differ
                        rowsum[j] = rowsum[j] + jnp.sum(qv, axis=0, keepdims=True)
                        qb = qv.astype(BF)
                        gsec = gsec + jnp.where(rank // 32 == j, nn(O.shT[:, rows], qb), 0.0)
                        L.gsh[rows, :] += nt(qb, second) * R.shmask[j : j + 1, :]
                    L.s1[i, rows, :] = a1.astype(BF)
                    R.gF[b, i] = a2.astype(BF).reshape(8, TC, W)
                put(L.ta, i, 0, ws[0].astype(BF), True)
                put(L.tb, i, 0, ws[1].astype(BF), False)
                put(L.ta, i, W, ws[2][0:128].astype(BF), True)
                put(L.tb, i, W, ws[2][128:256].astype(BF), False)
                L.sg[i, R_SECOND : R_SECOND + 160, :] = gsec.astype(BF)
                L.sg[i, R_DECAY1 : R_DECAY1 + 64, :] = gd1.astype(BF)
                for j in range(5):
                    L.psm[i, 3 + j : 4 + j, :] = rowsum[j]

            fori(8, target_body)
            sea.p2()
            seb.p2()
            sta.near()
            stb.near()
            hidden = R.sh[...]
            gs2 = L.gsh[...] * (1.0 - hidden * hidden)
            L.gshp[...] = gs2.astype(BF)
            L.gshpT[...] = gs2.T.astype(BF)
            L.rsum[...] = jnp.zeros_like(L.rsum)
            lane = iota((TB, 128), 1)

            def mixed_back(b):
                rows = rows_of(b)

                def body(i):
                    first = R.smF[i, R_FIRST : R_FIRST + 160, :]
                    n, normed, differ, v = n1.block(i, b)
                    mixed = (normed + differ * v[2:3]).astype(BF)
                    gm = nn(L.gshp[rows, :], first)
                    gf = nn(L.gshpT[:, rows], mixed)
                    g2 = jnp.sum(gm * differ, axis=0, keepdims=True)
                    gd = R.gF[b, i].reshape(TB, W).astype(F32) + gm * v[2:3]
                    kg = gd * R.keep[rows, :]
                    R.bsend[i, b : b + 1, :] = kg[0:1]
                    gn = L.s1[i, rows, :].astype(F32) + gm - gd + shift_up(kg)
                    R.part[b, i] = gn.astype(BF).reshape(8, TC, W)
                    gg = gn * v[0:1]
                    ra = jnp.sum(gg, axis=1, keepdims=True)
                    rb = jnp.sum(gg * n, axis=1, keepdims=True)
                    L.rsum[rows, :] += jnp.where(lane == 0, ra, jnp.where(lane == 1, rb, 0.0))
                    if b == 0:
                        L.sg[i, R_FIRST : R_FIRST + 160, :] = gf.astype(BF)
                        L.psm[i, 2:3, :] = g2
                    else:
                        had = L.sg[i, R_FIRST : R_FIRST + 160, :].astype(F32)
                        L.sg[i, R_FIRST : R_FIRST + 160, :] = (had + gf).astype(BF)
                        vg = R.vg[i]
                        L.sg[i, R_VEC : R_VEC + 16, :] = jnp.concatenate(
                            [
                                jnp.zeros((2, W), F32),
                                L.psm[i, 2:3, :] + g2,
                                L.psm[i, 3:8, :],
                                jnp.zeros((4, W), F32),
                                vg[0:2],
                                vg[2:4] + vg[4:6],
                            ],
                            axis=0,
                        ).astype(BF)

                fori(8, body)
                for k in (2, 1, 3, 0):
                    rs4[b].give(k)

            for b in both:
                rs3[b].drain()
            R.bsend[...] = jnp.zeros_like(R.bsend)
            mixed_back(0)
            mixed_back(1)
            for c in last:
                c.start()
            sta.far()
            stb.far()
            rs4[0].pass_far()
            for k in (2, 1, 3, 0):
                sms.give(k)
            sca.finish(R.oca)
            scb.finish(R.ocb)
            rs4[0].pass_near()
            rs4[1].pass_far()
            sea.finish(R.oea)
            seb.finish(R.oeb)
            for c in last:
                c.wait_recv()
            edge = jnp.sum(R.brecv[...], axis=0)
            lane8 = iota((1, 128), 1)
            for b in both:
                at = slice(b * TB + TB - 16, b * TB + TB)
                n = (R.xF[b, h, TB - 16 : TB, :].astype(F32) - R.mean[at, :]) * R.rstd[at, :]
                e = edge[b : b + 1] * vl[0:1]
                ra = jnp.sum(e, axis=1, keepdims=True)
                rb = jnp.sum(e * n[15:16], axis=1, keepdims=True)
                end = slice(b * TB + TB - 1, b * TB + TB)
                L.rsum[end, :] += jnp.where(lane8 == 0, ra, jnp.where(lane8 == 1, rb, 0.0))
            R.rsend[...] = L.rsum[...].T[0:8]
            R.rrecv[h] = R.rsend[...]
            for c in rex:
                c.start()
            rs4[1].pass_near()
            sms.pass_far()
            sta.p2()
            stb.p2()
            for c in rex:
                c.wait_recv()
            tot = jnp.sum(R.rrecv[...], axis=0)
            L.rsum[...] = jnp.concatenate([tot, jnp.zeros((120, N), F32)], axis=0).T / D
            sms.pass_near()
            g0, g1 = z1, z1
            for b in both:
                rows = rows_of(b)
                R.mid[b] = rs4[b].total()
                R.mid[b, 7, TC - 1 : TC, :] += edge[b : b + 1]
                gl = R.mid[b].reshape(TB, W)
                n = (R.xF[b, h].astype(F32) - R.mean[rows, :]) * R.rstd[rows, :]
                g0 = g0 + jnp.sum(gl * n, axis=0, keepdims=True)
                g1 = g1 + jnp.sum(gl, axis=0, keepdims=True)
                R.hgrad[b] = slab_of(R.midF.at[b], h).astype(F32) + R.rstd[rows, :] * (
                    gl * vl[0:1] - L.rsum[rows, 0:1] - n * L.rsum[rows, 1:2]
                )
            O.lsm[0:400, :] = sms.total()
            O.lsm[R_VEC : R_VEC + 2, :] += jnp.concatenate([g0, g1], axis=0)
            O.lsm[R_VEC + 8 : R_VEC + 12, :] += R.gvec[0:4, :]
            R.psend[...] = (
                lax.dot_general(R.sel[...], O.lsm[...].astype(BF), (((0,), (0,)), ((), ())), preferred_element_type=F32).astype(BF).reshape(16, 32, W)
            )
            for c in smo:
                c.start()
            R.psrecv[s] = R.psend[s]
            for c in smo:
                c.wait_recv()
            R.osm[...] = jnp.sum(R.psrecv[...].astype(F32), axis=0)
            sta.finish(R.ota)
            stb.finish(R.otb)
            net.drain()

        RT = W + 128
        pl.run_scoped(
            normed_back,
            s1=pltpu.VMEM((8, N, W), BF),
            ta=pltpu.VMEM((16, RT, 128), BF),
            tb=pltpu.VMEM((16, RT, 128), BF),
            ta2=pltpu.VMEM((4, RT, 128), BF),
            tb2=pltpu.VMEM((4, RT, 128), BF),
            sg=pltpu.VMEM((8, 400, W), BF),
            sgsend=pltpu.VMEM((3, 400, W), BF),
            gsh=pltpu.VMEM((N, 160), F32),
            gshp=pltpu.VMEM((N, 160), BF),
            gshpT=pltpu.VMEM((160, N), BF),
            rsum=pltpu.VMEM((N, 128), F32),
            psm=pltpu.VMEM((8, 8, W), F32),
        )

    pl.run_scoped(
        time_backward,
        ea=pltpu.VMEM((16, W, 128), BF),
        eb=pltpu.VMEM((16, W, 128), BF),
        ea2=pltpu.VMEM((4, W, 128), BF),
        eb2=pltpu.VMEM((4, W, 128), BF),
        shT=pltpu.VMEM((160, N), BF),
        gp=pltpu.VMEM((4, N, W), BF),
        gpT=pltpu.VMEM((4, W, N), BF),
        gw=pltpu.VMEM((N, W), BF),
        gdp=pltpu.VMEM((N, 64), BF),
        gdpT=pltpu.VMEM((64, N), BF),
        lsm=pltpu.VMEM((464, W), F32),
    )
    for b in both:

        @pl.when(h == 7)
        def _():
            for k in range(8):
                mid_border(b, k).wait_send()

        grad_border(b, h).wait_send()
        for e in both:
            carry_each(e, b, lambda c: c.wait_send())


def put(ref, i, row, y, xfirst):
    for e in range(2):
        q = 2 * i + e
        if not xfirst:
            q = lax.rem(q, 4) * 4 + q // 4
        ref[q, row : row + y.shape[0], :] = y[:, 128 * e : 128 * e + 128]


VM = pl.BlockSpec(memory_space=pltpu.VMEM)
HB = pl.BlockSpec(memory_space=pl.ANY)
SD = jax.ShapeDtypeStruct


def run_layer(ins):
    far = ("tw", "to", "ck", "cv", "cr")
    RA, RB, RT = FFL + W, FFL, W + 128
    outs = dict(
        result=((2, TB, W), F32, VM),
        hgrad=((2, TB, W), F32, VM),
        oca=((RA, 128), F32, VM),
        ocb=((RB, 128), F32, VM),
        oea=((W, 128), F32, VM),
        oeb=((W, 128), F32, VM),
        ota=((RT, 128), F32, VM),
        otb=((RT, 128), F32, VM),
        osm=((32, W), F32, VM),
        twF=((4, D, W), BF, HB),
        ckF=((D, FFL), BF, HB),
        cvF=((FFL, D), BF, HB),
        crF=((D, W), BF, HB),
        gaH=((16, RA, 128), BF, HB),
        gbH=((16, RB, 128), BF, HB),
        ra1=((3, 4, RA, 128), BF, HB),
        rb1=((3, 4, RB, 128), BF, HB),
    )
    scr = dict(
        small=((32, W), BF),
        sm=((16, 32, W), BF),
        bsrc=((32, W), BF),
        xF=((2, 8, TB, W), BF),
        bord=((8, 32, W), BF),
        smF=((8, 400, W), BF),
        ds2=((64, W), BF),
        twV=((4, D, W), BF),
        toV=((W, D), BF),
        midF=((2, 8, 8, TC, W), BF),
        mid=((2, 8, TC, W), F32),
        mb=((2, 8, W), F32),
        bmid=((2, 8, W), F32),
        gch=((2, 8, TC, W), F32),
        gF=((2, 8, 8, TC, W), BF),
        mean=((N, 1), F32),
        rstd=((N, 1), F32),
        bmean=((32, 1), F32),
        brstd=((32, 1), F32),
        sh=((N, 160), F32),
        dh=((N, 64), F32),
        proj=((4, N, W), BF),
        logd=((N, W), F32),
        gnorm=((N, W), F32),
        gscale=((N, W), F32),
        scores=((N, W), BF),
        starts=((8, 128, 128), BF),
        rp=((N, W), BF),
        gate=((N, W), BF),
        tch=((8, W), F32),
        tpre=((16, W), F32),
        carry=((2, 128, 128), F32),
        csend=((2, 2, 144, 128), BF),
        crecv=((2, 16, 144, 128), BF),
        part=((2, 8, 8, TC, W), BF),
        tosend=((2, 3, 8, TC, W), BF),
        fromsib=((2, 2, 4, 8, TC, W), BF),
        fromz=((2, 2, 3, 8, TC, W), BF),
        gsend=((2, 8, W), F32),
        grecv=((2, 8, 8, W), F32),
        vg=((8, 8, W), F32),
        gvec=((8, W), F32),
        bsend=((8, 8, W), F32),
        brecv=((8, 8, W), F32),
        rsend=((8, N), F32),
        rrecv=((8, 8, N), F32),
        sgsib=((4, 400, W), BF),
        sgz=((3, 400, W), BF),
        psend=((16, 32, W), BF),
        psrecv=((16, 32, W), BF),
        ra2=((4, RA, 128), BF),
        ra3=((3, RA, 128), BF),
        rb2=((4, RB, 128), BF),
        rb3=((3, RB, 128), BF),
        ea1=((3, 4, W, 128), BF),
        ea3=((3, W, 128), BF),
        eb1=((3, 4, W, 128), BF),
        eb3=((3, W, 128), BF),
        ta1=((3, 4, RT, 128), BF),
        ta3=((3, RT, 128), BF),
        tb1=((3, 4, RT, 128), BF),
        tb3=((3, RT, 128), BF),
    )
    sems = dict(ss=430, rs=430, ls=36, bs=18, br=18, cs=64, cr_=64)
    names = list(ins) + list(outs) + list(scr) + list(sems)
    got = pl.pallas_call(
        functools.partial(layer_kernel, names),
        out_shape=[SD(a, t) for a, t, _ in outs.values()],
        in_specs=[HB if k in far else VM for k in ins],
        out_specs=[m for _, _, m in outs.values()],
        scratch_shapes=[pltpu.VMEM(a, t) for a, t in scr.values()]
        + [pltpu.SemaphoreType.DMA((n,)) for n in sems.values()],
        name="layer",
        compiler_params=pltpu.CompilerParams(
            collective_id=1, has_side_effects=True, vmem_limit_bytes=VMEM_LIMIT
        ),
    )(*ins.values())
    return SimpleNamespace(**dict(zip(outs, got)))


def on_device(
    hidden, cotangent, opening_flags, vectors, shift_first, shift_second, decay_first, decay_second,
    time_weights, time_output, channel_key, channel_value, channel_recept,
):
    sel, shmask, hm, levels, sums = constants()
    o = run_layer(
        dict(
            x=hidden,
            cot=cotangent,
            keep=(1.0 - opening_flags.astype(F32)).reshape(N, 1),
            sf=shift_first[0],
            s2nd=shift_second[0],
            d1st=decay_first[0],
            d2nd=decay_second[0],
            vectors=vectors[0],
            sel=sel,
            shmask=shmask,
            hm=hm,
            levels=levels,
            sums=sums,
            tw=time_weights[0],
            to=time_output[0],
            ck=channel_key[0],
            cv=channel_value[0],
            cr=channel_recept[0],
        )
    )
    return finish(o.result, o.hgrad, o.oca, o.ocb, o.oea, o.oeb, o.ota, o.otb, o.osm)


def finish_kernel(
    result, hg, ca, cb, ea, eb, ta, tb, sm,
    o_result, o_hidden, o_vec, o_first, o_second, o_decay1, o_decay2, o_time, o_out, o_key, o_value,
    o_recept,
):
    o_result[...] = result[...]
    o_hidden[...] = hg[...]
    o_first[0] = sm[0:10]
    o_second[0] = sm[10:20]
    o_decay1[0] = sm[20:24]
    o_decay2[0] = sm[24:28]
    o_vec[0] = sm[28:29]
    o_time[0, 0] = ta[0:W].T
    o_time[0, 1] = tb[0:W].T
    o_time[0, 2, :, 0:128] = ta[W:].T
    o_time[0, 2, :, 128:256] = tb[W:].T
    o_time[0, 3] = ea[...].T
    o_out[0] = eb[...]
    o_key[0] = ca[0:FFL].T
    o_value[0] = cb[...]
    o_recept[0] = ca[FFL:].T


def finish(*ins):
    shapes = [
        (2, TB, W), (2, TB, W), (1, 1, W), (1, 10, W), (1, 10, W), (1, 4, W), (1, 4, W),
        (1, 4, 128, W), (1, W, 128), (1, 128, FFL), (1, FFL, 128), (1, 128, W),
    ]
    return pl.pallas_call(
        finish_kernel,
        out_shape=[SD(q, F32) for q in shapes],
        in_specs=[VM] * len(ins),
        out_specs=[VM] * len(shapes),
        name="finish",
        compiler_params=pltpu.CompilerParams(vmem_limit_bytes=VMEM_LIMIT),
    )(*ins)


def solution(mesh):
    last = P(None, "seq", "head")
    turned = P(None, "head", "seq")
    four = P(None, None, "seq", "head")
    return jax.shard_map(
        on_device,
        mesh=mesh,
        in_specs=(last, last, P(None, "seq"), last, last, last, last, last, four, turned, last, turned, last),
        out_specs=(last, last, last, last, last, last, last, four, turned, last, turned, last),
        check_vma=False,
    )
```

```python
import functools
from types import SimpleNamespace

import jax
import jax.numpy as jnp
import numpy as np
from jax import lax
from jax.experimental import pallas as pl
from jax.experimental.pallas import tpu as pltpu
from jax.sharding import PartitionSpec as P

MESH = pl.DeviceIdType.MESH
BF = jnp.bfloat16
F32 = jnp.float32
EPS = 1e-5
GEPS = 64e-5
N = 512
TB = 256
TC = 32
W = 256
C = 64
LV = 6
D = 2048
FFL = 896
VMEM_LIMIT = 63 * 2**20
R_FIRST, R_SECOND, R_DECAY1, R_VEC, R_DECAY2 = 0, 160, 320, 384, 400


def nt(a, b):
    return lax.dot_general(a, b, (((1,), (1,)), ((), ())), preferred_element_type=F32)


def nn(a, b):
    return jnp.dot(a, b, preferred_element_type=F32)


def place():
    return lax.axis_index("seq"), lax.axis_index("head")


def sibling():
    s, h = place()
    return s, h // 2 * 2 + 1 - lax.rem(h, 2)


def chip(k, core=0):
    h = place()[1]
    c = lax.rem(h, 2)
    return lax.rem(h // 2 + k, 4) * 2 + (1 - c if core else c)


def zdev(k):
    return place()[0], chip(k)


def seq_index(first, ka, kb):
    s = place()[0]
    x, y = s // 4, lax.rem(s, 4)
    if first:
        return lax.rem(x + ka, 4) * 4 + lax.rem(y + kb, 4)
    return lax.rem(x + kb, 4) * 4 + lax.rem(y + ka, 4)


def seq_dev(first, ka, kb):
    return seq_index(first, ka, kb), place()[1]


class Copy:
    def __init__(self, net, i, make):
        self.net, self.i, self.make = net, i, make

    def desc(self):
        src, dst, dev = self.make()
        return pltpu.make_async_remote_copy(
            src_ref=src,
            dst_ref=dst,
            send_sem=self.net.ss.at[self.i],
            recv_sem=self.net.rs.at[self.i],
            device_id=dev,
            device_id_type=MESH,
        )

    def start(self):
        self.desc().start()
        self.net.out.append(self)

    def wait_recv(self):
        self.desc().wait_recv()

    def wait_send(self):
        self.desc().wait_send()


class Net:
    def __init__(self, ss, rs):
        self.ss, self.rs, self.n, self.out = ss, rs, 0, []

    def copy(self, make):
        self.n += 1
        return Copy(self, self.n - 1, make)

    def drain(self, copies=None):
        for c in list(self.out) if copies is None else copies:
            c.wait_send()
            self.out.remove(c)


def greet(peers):
    b = pltpu.get_barrier_semaphore()
    for p in peers:
        pl.semaphore_signal(b, inc=1, device_id=p, device_id_type=MESH)
    pl.semaphore_wait(b, len(peers))


def head_peers():
    s, h = place()
    return [(s, lax.rem(h + k, 8)) for k in range(1, 8)]


def seq_peers():
    s, h = place()
    return [(lax.rem(s + k, 16), h) for k in range(1, 16)]


def diagonal_peers(step):
    s, h = place()
    return [(lax.rem(s + step, 16), lax.rem(h + k, 8)) for k in range(1, 8)]


ORDER = (1, 3, 2)


def half(ref, i):
    n = ref.shape[0]
    m = n // 2 if len(ref.shape) == 3 else (n // 2 + 15) // 16 * 16
    return ref.at[m:n] if i else ref.at[0:m]


class HeadGather:
    def __init__(self, net, slot):
        self.net = net

        def own():
            return slot(place()[1])

        def at(k):
            return slot(chip(k))

        def copy(ref, dev):
            return net.copy(lambda: (ref(), ref(), dev()))

        up, down = lambda: zdev(1), lambda: zdev(3)
        self.ua = copy(lambda: half(own(), 0), up)
        self.db = copy(lambda: half(own(), 1), down)
        self.ub = copy(lambda: half(own(), 1), up)
        self.da = copy(lambda: half(own(), 0), down)
        self.mine = copy(own, sibling)
        self.fa = copy(lambda: half(at(3), 0), up)
        self.fb = copy(lambda: half(at(1), 1), down)
        self.s3 = copy(lambda: at(3), sibling)
        self.s1 = copy(lambda: at(1), sibling)
        self.sa = copy(lambda: half(at(2), 0), sibling)
        self.sb = copy(lambda: half(at(2), 1), sibling)

    def start(self):
        for c in (self.ua, self.db, self.ub, self.da, self.mine):
            c.start()

    def relay(self):
        self.ua.wait_recv()
        self.fa.start()
        self.db.wait_recv()
        self.fb.start()
        self.ub.wait_recv()
        self.s3.start()
        self.da.wait_recv()
        self.s1.start()

    def relay_far(self):
        self.fa.wait_recv()
        self.sa.start()
        self.fb.wait_recv()
        self.sb.start()

    def finish(self):
        for c in (self.mine, self.s3, self.s1, self.sa, self.sb):
            c.wait_recv()

    def drain(self):
        near = [self.ua, self.db, self.ub, self.da, self.mine]
        self.net.drain(near + [self.fa, self.fb, self.s3, self.s1, self.sa, self.sb])


class HeadScatter:
    def __init__(self, net, part, fromsib, tosend, fromz):
        self.net, self.part, self.fromsib, self.tosend, self.fromz = net, part, fromsib, tosend, fromz
        self.a = {
            k: net.copy(lambda k=k: (part.at[chip(k, 1)], fromsib.at[k], sibling()))
            for k in range(4)
        }

        def copy(i, j, k, dev):
            return net.copy(lambda: (half(tosend.at[i], k), half(fromz.at[j], k), zdev(dev)))

        self.fa, self.fb = copy(1, 2, 0, 1), copy(1, 2, 1, 3)
        self.ua, self.ub = copy(0, 0, 0, 1), copy(0, 0, 1, 1)
        self.da, self.db = copy(2, 1, 0, 3), copy(2, 1, 1, 3)
        self.all = [*self.a.values(), self.fa, self.fb, self.ua, self.ub, self.da, self.db]

    def theirs(self, k):
        return chip(k, 1)

    def ours(self, k):
        return chip(k)

    def give(self, k):
        self.a[k].start()

    def both(self, k, i):
        own = half(self.part.at[chip(k)], i)[...].astype(F32)
        return own + half(self.fromsib.at[k], i)[...].astype(F32)

    def put(self, i, k, x):
        half(self.tosend.at[i], k)[...] = x.astype(BF)

    def pass_far(self):
        self.a[2].wait_recv()
        self.put(1, 0, self.both(2, 0))
        self.fa.start()
        self.put(1, 1, self.both(2, 1))
        self.fb.start()
        self.a[1].wait_recv()
        self.put(0, 1, self.both(1, 1))
        self.ub.start()
        self.a[3].wait_recv()
        self.put(2, 0, self.both(3, 0))
        self.da.start()

    def pass_near(self):
        far = self.fromz.at[2]
        self.fa.wait_recv()
        self.put(0, 0, self.both(1, 0) + half(far, 0)[...].astype(F32))
        self.ua.start()
        self.fb.wait_recv()
        self.put(2, 1, self.both(3, 1) + half(far, 1)[...].astype(F32))
        self.db.start()

    def total(self):
        self.a[0].wait_recv()
        t = self.part[chip(0)].astype(F32) + self.fromsib[0].astype(F32)
        for c in (self.ub, self.da, self.ua, self.db):
            c.wait_recv()
        return t + self.fromz[0].astype(F32) + self.fromz[1].astype(F32)

    def drain(self):
        self.net.drain(self.all)


class SeqGather:
    def __init__(self, net, src, slot, xfirst, sem):
        self.net, self.src, self.slot, self.sem = net, src, slot, sem

        def at(k):
            return slot(seq_index(xfirst, k, 0))

        self.first = {
            k: net.copy(lambda k=k: (src, at(0), seq_dev(xfirst, k, 0))) for k in ORDER
        }
        self.own2 = [
            net.copy(lambda k=k: (src, at(0), seq_dev(xfirst, 0, k))) for k in (1, 3)
        ]
        self.second = {
            (k, j): net.copy(lambda k=k, j=j: (at(4 - k), at(4 - k), seq_dev(xfirst, 0, j)))
            for k in ORDER
            for j in (1, 3)
        }

        def came(k, j):
            return slot(seq_index(xfirst, (4 - k) % 4, j))

        self.far = {
            k: net.copy(
                lambda k=k, j=j: (came(k, 4 - j), came(k, 4 - j), seq_dev(xfirst, 0, j))
            )
            for k, j in ((0, 1), (1, 1), (3, 3), (2, 3))
        }

    def local(self):
        return pltpu.make_async_copy(self.src, self.slot(place()[0]), self.sem)

    def p0(self):
        self.local().start()
        for c in self.first.values():
            c.start()

    def p1(self):
        self.p0()
        for c in self.own2:
            c.start()

    def p2(self, own=False):
        if own:
            for c in self.own2:
                c.start()
        for k in ORDER:
            self.first[k].wait_recv()
            for j in (1, 3):
                self.second[k, j].start()

    def p3(self):
        self.own2[0].wait_recv()
        self.far[0].start()
        for k, j in ((1, 1), (3, 3), (2, 3)):
            self.second[k, j].wait_recv()
            self.far[k].start()

    def finish(self):
        self.local().wait()
        self.own2[1].wait_recv()
        for k, j in ((1, 3), (3, 1), (2, 1)):
            self.second[k, j].wait_recv()
        for c in self.far.values():
            c.wait_recv()

    def drain(self):
        self.net.drain(
            [*self.first.values(), *self.own2, *self.second.values(), *self.far.values()]
        )


class SeqScatter:
    def __init__(self, net, src, recv, acc, recv2, tmp, xfirst, own_sem=None, sems=None):
        self.net, self.src, self.recv, self.acc, self.recv2 = net, src, recv, acc, recv2
        self.tmp, self.xfirst, self.own_sem, self.sems = tmp, xfirst, own_sem, sems
        f = xfirst

        def copy(k, at, to, dst, step):
            return net.copy(
                lambda: (self.slots(k, at), recv.at[to, dst : dst + 2], seq_dev(f, step, 0))
            )

        self.fa, self.fb = copy(2, 0, 2, 0, 1), copy(2, 2, 2, 2, 3)
        self.ub, self.da = copy(1, 2, 0, 2, 1), copy(3, 0, 1, 0, 3)
        self.ua = net.copy(lambda: (self.tmp.at[0], recv.at[0, 0:2], seq_dev(f, 1, 0)))
        self.db = net.copy(lambda: (self.tmp.at[1], recv.at[1, 2:4], seq_dev(f, 3, 0)))
        self.c2 = {
            k: net.copy(lambda k=k: (acc.at[self.line(1, k)], recv2.at[k - 1], seq_dev(f, 0, k)))
            for k in ORDER
        }

    def slots(self, k, at):
        return self.src.at[pl.ds(self.line(0, k) * 4 + at, 2)]

    def line(self, axis, k):
        s = place()[0]
        x, y = s // 4, lax.rem(s, 4)
        return lax.rem((x if (axis == 0) == self.xfirst else y) + k, 4)

    def own(self):
        return pltpu.make_async_copy(
            self.src.at[pl.ds(self.line(0, 0) * 4, 4)], self.acc, self.own_sem
        )

    def near(self):
        for c in (self.fa, self.fb, self.ub, self.da):
            c.start()

    def far(self, stage=None):
        self.fa.wait_recv()
        self.fb.wait_recv()
        if stage is not None:
            loads = [
                pltpu.make_async_copy(a, b, self.sems.at[i])
                for i, (a, b) in enumerate(
                    (
                        (self.slots(1, 0), self.tmp.at[0]),
                        (self.slots(3, 2), self.tmp.at[1]),
                        (self.recv.at[2, 0:2], stage[0].at[0:2]),
                        (self.recv.at[2, 2:4], stage[1].at[0:2]),
                    )
                )
            ]
            for c in loads:
                c.start()
            for c in loads:
                c.wait()
        for e, c in ((0, self.ua), (1, self.db)):
            for i in range(2):
                if stage is None:
                    own = self.src[self.line(0, 3 if e else 1) * 4 + 2 * e + i]
                    way = self.recv[2, 2 * e + i]
                else:
                    own, way = self.tmp[e, i], stage[e][i]
                self.tmp[e, i] = (own.astype(F32) + way.astype(F32)).astype(BF)
            c.start()

    def p2(self, stage=None):
        for c in (self.ub, self.da, self.ua, self.db):
            c.wait_recv()
        if stage is None:
            a = self.line(0, 0) * 4

            def body(j):
                t = self.src[a + j].astype(F32) + self.recv[0, j].astype(F32)
                self.acc[j] = (t + self.recv[1, j].astype(F32)).astype(BF)

            fori(4, body)
        else:
            copies = [
                pltpu.make_async_copy(
                    self.recv.at[0:2, j], stage[j % 2].at[0:2], self.sems.at[j]
                )
                for j in range(4)
            ]
            copies[0].start()
            self.own().wait()
            for j in range(4):
                if j < 3:
                    copies[j + 1].start()
                copies[j].wait()
                st = stage[j % 2]
                t = self.acc[j].astype(F32) + st[0].astype(F32)
                self.acc[j] = (t + st[1].astype(F32)).astype(BF)
        for k in ORDER:
            self.c2[k].start()

    def finish(self, out):
        for k in ORDER:
            self.c2[k].wait_recv()
        t = self.acc[self.line(1, 0)].astype(F32) + self.recv2[0].astype(F32)
        out[...] = t + self.recv2[1].astype(F32) + self.recv2[2].astype(F32)


def fori(n, body):
    def step(i, carry):
        body(i)
        return carry

    lax.fori_loop(0, n, step, 0)


def row_stats(x3):
    m = jnp.sum(jnp.sum(x3, axis=0), axis=1, keepdims=True) / D
    d = x3 - m[None]
    v = jnp.sum(jnp.sum(d * d, axis=0), axis=1, keepdims=True) / D
    return m, lax.rsqrt(v + EPS)


def iota(shape, dim):
    return lax.broadcasted_iota(jnp.int32, shape, dim)


def shift_down(u, first, keep):
    r = pltpu.roll(u, 1, 0)
    return jnp.where(iota(u.shape, 0) == 0, first, r) * keep


def shift_up(u):
    return jnp.where(iota(u.shape, 0) == u.shape[0] - 1, 0.0, pltpu.roll(u, u.shape[0] - 1, 0))


def rows_of(b):
    return slice(b * TB, (b + 1) * TB)


def slab_of(ref, i):
    return ref[:, i].reshape(TB, W)


class Norm1:
    def __init__(self, R):
        self.R = R

    def stats(self, b):
        R = self.R

        def body(i):
            at = pl.multiple_of(i * 64, 64)
            m, r = row_stats(R.xF[b, :, pl.ds(at, 64), :].astype(F32))
            R.mean[pl.ds(b * TB + at, 64), :] = m
            R.rstd[pl.ds(b * TB + at, 64), :] = r

        fori(4, body)

    def edge_stats(self):
        m, r = row_stats(self.R.bord[...].astype(F32))
        self.R.bmean[...] = m
        self.R.brstd[...] = r

    def block(self, i, b):
        R = self.R
        v = R.smF[i, R_VEC : R_VEC + 16, :].astype(F32)
        rows = rows_of(b)
        n = (R.xF[b, i].astype(F32) - R.mean[rows, :]) * R.rstd[rows, :]
        normed = n * v[0:1] + v[1:2]
        at = slice(16 * b, 16 * b + 16)
        e = (R.bord[i, at, :].astype(F32) - R.bmean[at, :]) * R.brstd[at, :]
        first = (e * v[0:1] + v[1:2])[15:16]
        differ = shift_down(normed, first, R.keep[rows, :]) - normed
        return n, normed, differ, v


def tree(r, k, wk, keep):
    row = iota((C, W), 0)
    p = jnp.broadcast_to(keep, (C, W))
    q = jnp.ones((C, W), F32)
    t = wk
    out = []
    for level in range(LV):
        m = 1 << level
        second = (row // m) % 2 == 1
        e = jnp.where(second, p, q)
        out.append((jnp.where(second, r, k), e))
        other = jnp.where(second, pltpu.roll(t, m, 0), pltpu.roll(t, C - m, 0))
        p = jnp.where(second, p * other, p)
        q = jnp.where(second, q, q * other)
        t = t * other
    return out, p, q, t


def spread(x, hm):
    return jnp.concatenate([x] * 4, axis=0) * hm


def fold(st):
    f = st[:, 0:128] + st[:, 128:256]
    return jnp.concatenate([f[0:64] + f[64:128], f[128:192] + f[192:256]], axis=0)


def unfold(c, hmf):
    f = jnp.concatenate([c[0:64], c[0:64], c[64:128], c[64:128]], axis=0)
    return jnp.concatenate([f, f], axis=1) * hmf


def head_sum(x, hm):
    hi = x.astype(BF)
    lo = (x - hi.astype(F32)).astype(BF)
    return nn(hi, hm) + nn(lo, hm)


def constants():
    sel = np.zeros((464, 512), np.float32)
    for base, count, off in ((0, 10, 0), (160, 10, 10), (320, 4, 20), (384, 1, 28), (400, 4, 24)):
        for q in range(16):
            for i in range(count):
                sel[base + q * count + i, q * 32 + off + i] = 1
    shmask = np.zeros((8, 160), np.float32)
    for j in range(5):
        shmask[j, 32 * j : 32 * j + 32] = 1
    f = np.arange(256) // 64
    hm = (f[:, None] == f[None, :]).astype(np.float32)
    t = np.arange(64)[:, None]
    u = (np.arange(256) % 64)[None, :]
    lev, levt, sums = [], [], []
    a = np.arange(64)[:, None]
    e = np.arange(64)[None, :]
    for m in (1, 2, 4, 8, 16, 32):
        same = t // (2 * m) == u // (2 * m)
        lev.append(same & (t // m % 2 == 1) & (u // m % 2 == 0))
        levt.append(same & (t // m % 2 == 0) & (u // m % 2 == 1))
        half = a // m == e // m
        sums.append(half & np.where(a // m % 2 == 0, e < a, e > a))
    sums += [e < a, e > a]
    lev = np.stack(lev + levt).astype(np.float32)
    sums = np.concatenate(sums, axis=1).astype(np.float32)
    return (
        jnp.asarray(sel, BF),
        jnp.asarray(shmask, F32),
        jnp.asarray(hm, BF),
        jnp.asarray(lev, F32),
        jnp.asarray(sums, BF),
    )


def layer_kernel(names, *refs):
    R = SimpleNamespace(**dict(zip(names, refs)))
    s, h = place()
    prv, nxt = lax.rem(s + 15, 16), lax.rem(s + 1, 16)
    net = Net(R.ss, R.rs)
    both = (0, 1)
    z1 = jnp.zeros((1, W), F32)

    hid = [HeadGather(net, lambda i, b=b: R.xF.at[b, i]) for b in both]
    smg = HeadGather(net, lambda i: R.smF.at[i])
    midg = [HeadGather(net, lambda i, b=b: R.midF.at[b, i]) for b in both]
    gkvg = [HeadGather(net, lambda i, b=b: R.gF.at[b, i]) for b in both]
    gzg = [HeadGather(net, lambda i, b=b: R.midF.at[b, i]) for b in both]

    def scatter(b, e):
        return HeadScatter(
            net, R.part.at[b], R.fromsib.at[e, b], R.tosend.at[b], R.fromz.at[e, b]
        )

    rs1, rs2, rs3, rs4 = [[scatter(b, e) for b in both] for e in (0, 1, 0, 1)]

    def rows128(ref, q):
        return ref.at[pl.ds(pl.multiple_of(q * 128, 128), 128), :]

    def cols128(ref, q):
        return ref.at[:, pl.ds(pl.multiple_of(q * 128, 128), 128)]

    tws = [
        SeqGather(net, R.tw.at[i], lambda q, i=i: rows128(R.twV.at[i], q), i % 2 == 0, R.ls.at[i])
        for i in range(4)
    ]
    tos = SeqGather(net, R.to, lambda q: cols128(R.toV, q), True, R.ls.at[4])
    cks = [
        SeqGather(
            net,
            R.ck.at[:, a:e],
            lambda q, a=a, e=e: R.ckF.at[pl.ds(pl.multiple_of(q * 128, 128), 128), a:e],
            a == 0,
            R.ls.at[5 + (a > 0)],
        )
        for a, e in ((0, 512), (512, FFL))
    ]
    cks.append(SeqGather(net, R.cr, lambda q: rows128(R.crF, q), False, R.ls.at[7]))
    cvs = [
        SeqGather(
            net,
            R.cv.at[a : a + FFL // 2],
            lambda q, a=a: R.cvF.at[
                a : a + FFL // 2, pl.ds(pl.multiple_of(q * 128, 128), 128)
            ],
            a == 0,
            R.ls.at[36 + (a > 0)],
        )
        for a in (0, FFL // 2)
    ]
    sca = SeqScatter(net, R.gaH, R.ra1, R.ra2, R.ra3, None, True, R.ls.at[8], R.ls.at[20:24])
    scb = SeqScatter(net, R.gbH, R.rb1, R.rb2, R.rb3, None, False, R.ls.at[9], R.ls.at[24:28])

    def seq_step(k):
        sq, hq = place()
        return lax.rem(sq + k, 16), hq

    smalls = [
        net.copy(lambda k=k: (R.small, R.sm.at[place()[0]], seq_step(k))) for k in range(1, 16)
    ]

    def beside(k, step):
        sq, hq = place()
        return lax.rem(sq + step, 16), lax.rem(hq + k, 8)

    edges = [net.copy(lambda k=k: (R.bsrc, R.bord.at[place()[1]], beside(k, 1))) for k in range(8)]
    cots = {
        (b, k): net.copy(
            lambda b=b, k=k: (
                R.cot.at[b, pl.ds(pl.multiple_of(beside(k, 0)[1] * TC, TC), TC), :],
                R.gch.at[b, place()[1]],
                beside(k, 0),
            )
        )
        for b in both
        for k in range(1, 8)
    }
    last = [net.copy(lambda k=k: (R.bsend.at[beside(k, 0)[1]], R.brecv.at[place()[1]], beside(k, 15))) for k in range(8)]
    rex = [
        net.copy(lambda k=k: (R.rsend, R.rrecv.at[place()[1]], beside(k, 0))) for k in range(1, 8)
    ]
    smo = [
        net.copy(lambda k=k: (R.psend.at[seq_step(k)[0]], R.psrecv.at[place()[0]], seq_step(k)))
        for k in range(1, 16)
    ]

    def mid_border(b, k):
        return pltpu.make_async_remote_copy(
            src_ref=R.mb.at[b],
            dst_ref=R.bmid.at[b],
            send_sem=R.bs.at[b * 8 + k],
            recv_sem=R.br.at[b],
            device_id=(nxt, k),
            device_id_type=MESH,
        )

    def grad_border(b, frm):
        return pltpu.make_async_remote_copy(
            src_ref=R.gsend.at[b],
            dst_ref=R.grecv.at[b, frm],
            send_sem=R.bs.at[16 + b],
            recv_sem=R.br.at[2 + b * 8 + frm],
            device_id=(prv, 7),
            device_id_type=MESH,
        )

    def carry_copy(e, b, dst, frm):
        return pltpu.make_async_remote_copy(
            src_ref=R.csend.at[e, b],
            dst_ref=R.crecv.at[b, frm],
            send_sem=R.cs.at[(2 * e + b) * 16 + dst],
            recv_sem=R.cr_.at[(2 * e + b) * 16 + frm],
            device_id=(dst, h),
            device_id_type=MESH,
        )

    def carry_each(e, b, act):
        def body(i, _):
            act(carry_copy(e, b, i, s))
            return 0

        lo, hi = (s + 1, 16) if e == 0 else (0, s)
        lax.fori_loop(lo, hi, body, 0)

    def carry_send(e, b, state, total):
        R.csend[e, b, 0:128, :] = fold(state).astype(BF)
        R.csend[e, b, 128:144, :] = jnp.concatenate(
            [total[:, 0:128], total[:, 128:256], jnp.zeros((14, 128), F32)], axis=0
        ).astype(BF)
        carry_each(e, b, lambda c: c.start())

    def carry_wait(e, b, hmf):
        R.carry[b] = jnp.zeros((128, 128), F32)

        def body(i, _):
            j = i if e == 0 else 15 - i
            carry_copy(e, b, 0, j).wait_recv()
            tt = R.crecv[b, j, 128:144, :].astype(F32)
            for g in range(2):
                at = slice(g * 64, g * 64 + 64)
                R.carry[b, at, :] = R.carry[b, at, :] * tt[g : g + 1] + R.crecv[b, j, at, :].astype(F32)
            return 0

        lax.fori_loop(0, s if e == 0 else 15 - s, body, 0)
        return unfold(R.carry[b], hmf)

    R.small[...] = jnp.concatenate(
        [a[...].astype(F32) for a in (R.sf, R.s2nd, R.d1st, R.d2nd, R.vectors)]
        + [jnp.zeros((3, W), F32)],
        axis=0,
    ).astype(BF)
    for b in both:
        R.bsrc[16 * b : 16 * b + 16, :] = R.x[b, TB - 16 : TB, :]
        R.xF[b, h] = R.x[b]
    greet(head_peers() + seq_peers() + diagonal_peers(1) + diagonal_peers(15))
    hid[0].start()
    for c in smalls + edges:
        c.start()
    hid[1].start()
    R.sm[s] = R.small[...]
    for c in smalls:
        c.wait_recv()
    for t in tws:
        t.p1()
    comp = nn(R.sel[...], R.sm[...].reshape(512, W)).astype(BF)
    R.smF[h] = comp[0:400]
    R.ds2[...] = comp[400:464]
    smg.start()
    for b in both:
        hid[b].relay()
    for t in tws:
        t.p2()
    tos.p1()
    for b in both:
        hid[b].relay_far()
    smg.relay()
    hid[0].finish()
    n1 = Norm1(R)
    n1.stats(0)
    smg.relay_far()
    hid[1].finish()
    n1.stats(1)
    for c in edges:
        c.wait_recv()
    n1.edge_stats()
    smg.finish()
    vl = R.smF[h, R_VEC : R_VEC + 16, :].astype(F32)
    hmb = R.hm[...]
    hmf = hmb.astype(F32)

    def time_forward(**kw):
        L = SimpleNamespace(**kw)

        def shift(b):
            rows = rows_of(b)
            L.mixacc[...] = jnp.zeros_like(L.mixacc)

            def body(i):
                n, normed, differ, v = n1.block(i, b)
                mixed = (normed + differ * v[2:3]).astype(BF)
                L.mixacc[...] += nt(mixed, R.smF[i, R_FIRST : R_FIRST + 160, :])

            fori(8, body)
            hidden = jnp.tanh(L.mixacc[...])
            R.sh[rows, :] = hidden
            for j in range(5):
                L.shm[j, rows, :] = (hidden * R.shmask[j : j + 1, :]).astype(BF)

        def targets(b):
            rows = rows_of(b)
            L.proj[:, rows, :] = jnp.zeros((4, TB, W), F32)
            L.dacc[...] = jnp.zeros_like(L.dacc)

            def body(i):
                col = pl.ds(pl.multiple_of(i * W, W), W)
                n, normed, differ, v = n1.block(i, b)
                second = R.smF[i, R_SECOND : R_SECOND + 160, :]
                for j in range(5):
                    mix = nn(L.shm[j, rows, :], second)
                    target = (normed + differ * (v[3 + j : 4 + j] + mix)).astype(BF)
                    if j == 0:
                        L.dacc[...] += nt(target, R.smF[i, R_DECAY1 : R_DECAY1 + 64, :])
                    else:
                        L.proj[j - 1, rows, :] += nn(target, R.twV[j - 1, col, :])

            fori(8, body)
            hidden = jnp.tanh(L.dacc[...])
            R.dh[rows, :] = hidden
            ld = -jnp.exp(vl[8:9] + nn(hidden.astype(BF), R.ds2[...]))
            R.logd[rows, :] = ld
            L.wdec[rows, :] = jnp.exp(ld) * R.keep[rows, :]
            R.proj[:, rows, :] = L.proj[:, rows, :].astype(BF)

        def states(b):
            L.st[b] = jnp.zeros((W, W), F32)
            R.tpre[8 + b : 9 + b, :] = jnp.ones((1, W), F32)

            def body(c):
                rows = pl.ds(pl.multiple_of(b * TB + c * C, C), C)
                i = b * 4 + c
                r, k, v = L.proj[2, rows, :], L.proj[0, rows, :], L.proj[1, rows, :]
                lv, p, q, t = tree(r, k, L.wdec[rows, :], R.keep[rows, :])
                for l, (a, e) in enumerate(lv):
                    L.xs[l, rows, :] = (a * e).astype(BF)
                R.rp[rows, :] = (r * p).astype(BF)
                L.starts[i] = L.st[b].astype(BF)
                R.tch[pl.ds(i, 1), :] = t[0:1]
                before = R.tpre[8 + b : 9 + b, :]
                R.tpre[pl.ds(i, 1), :] = before
                R.tpre[8 + b : 9 + b, :] = before * t[0:1]
                L.st[b] = L.st[b] * t[0:1] + nn(v.T.astype(BF), (k * q).astype(BF)) * hmf

            fori(4, body)
            carry_send(0, b, L.st[b], R.tpre[8 + b : 9 + b, :])

        def inner(b):
            def body(c):
                rows = pl.ds(pl.multiple_of(b * TB + c * C, C), C)
                r, k, v = L.proj[2, rows, :], L.proj[0, rows, :], L.proj[1, rows, :]
                a = jnp.zeros((C, W), F32)
                at = jnp.zeros((C, W), F32)
                for l in range(LV):
                    xl = L.xs[l, rows, :]
                    y = nt(xl, spread(xl, hmb))
                    a = a + y * R.levels[l]
                    at = at + y * R.levels[LV + l]
                R.scores[rows, :] = at.astype(BF)
                bonus = head_sum(r * vl[9:10] * k, hmb)
                L.ov[rows, :] = nn(a.astype(BF), spread(v.astype(BF), hmb)) + bonus * v

            fori(4, body)

        def outer(b):
            st = carry_wait(0, b, hmf)
            L.st[b] = st
            if b == 1:
                for g in cks:
                    g.p2(True)

            def body(c):
                i = b * 4 + c
                rows = pl.ds(pl.multiple_of(b * TB + c * C, C), C)
                start = L.starts[i].astype(F32) + L.st[b] * R.tpre[pl.ds(i, 1), :]
                R.starts[i] = fold(start).astype(BF)
                o = L.ov[rows, :] + nt(R.rp[rows, :], start.astype(BF))
                d = o - head_sum(o, hmb) / 64.0
                sc = lax.rsqrt(head_sum(d * d, hmb) / 64.0 + GEPS)
                gn = d * sc
                R.gnorm[rows, :] = gn
                R.gscale[rows, :] = sc
                g = L.proj[3, rows, :]
                R.gate[rows, :] = (
                    (gn * vl[10:11] + vl[11:12]) * (g * jax.nn.sigmoid(g))
                ).astype(BF)

            fori(4, body)

        def out(b):
            def body(i):
                y = nn(R.gate[rows_of(b), :], R.toV[:, pl.ds(pl.multiple_of(i * W, W), W)])
                R.part[b, :, i] = y.astype(BF).reshape(8, TC, W)

            fori(8, body)
            for k in (2, 1, 3, 0):
                rs1[b].give(k)

        for t in tws:
            t.p3()
        tos.p2()
        shift(0)
        shift(1)
        for t in tws:
            t.finish()
        for g in cks + cvs:
            g.p0()
        targets(0)
        states(0)
        tos.p3()
        targets(1)
        states(1)
        saved = pltpu.make_async_copy(R.twV, R.twF, R.ls.at[10])
        saved.start()
        inner(0)
        for c in cots.values():
            c.start()
        inner(1)
        outer(0)
        tos.finish()
        out(0)
        outer(1)
        rs1[0].pass_far()
        out(1)
        rs1[0].pass_near()
        rs1[1].pass_far()
        saved.wait()

    f32n = pltpu.VMEM((N, W), F32)
    pl.run_scoped(
        time_forward,
        mixacc=pltpu.VMEM((TB, 160), F32),
        shm=pltpu.VMEM((5, N, 160), BF),
        dacc=pltpu.VMEM((TB, 64), F32),
        proj=pltpu.VMEM((4, N, W), F32),
        wdec=f32n,
        xs=pltpu.VMEM((LV, N, W), BF),
        starts=pltpu.VMEM((8, W, W), BF),
        st=pltpu.VMEM((2, W, W), F32),
        ov=f32n,
    )

    def middle(b):
        m = rs1[b].total() + R.xF[b, :, pl.ds(pl.multiple_of(h * TC, TC), TC), :].astype(F32)
        R.mid[b] = m
        R.midF[b, h] = m.astype(BF)
        for i in range(8):
            R.mb[b, i : i + 1, :] = R.mid[b, i, TC - 1 : TC, :]
        midg[b].start()

        @pl.when(h == 7)
        def _():
            for k in range(8):
                mid_border(b, k).start()

    def channel(**kw):
        L = SimpleNamespace(**kw)
        loads = [
            pltpu.make_async_copy(a, c, R.ls.at[11 + i])
            for i, (a, c) in enumerate(((R.ckF, L.ck), (R.crF, L.cr), (R.cvF, L.cv)))
        ]

        def pairs(i):
            at = pl.ds(pl.multiple_of(lax.rem(i, 4) * N, N), N)
            return R.twV.at[i // 4, at, :], R.twV.at[2 + i // 4, at, :]

        def block(i, b):
            rows = rows_of(b)
            v = R.smF[i, R_VEC : R_VEC + 16, :].astype(F32)
            u = slab_of(R.midF.at[b], i).astype(F32)
            n2 = (u - L.mean[rows, :]) * L.rstd[rows, :] * v[12:13] + v[13:14]
            first = L.bstat[b, pl.ds(i, 1), :] * v[12:13] + v[13:14]
            return n2, shift_down(n2, first, R.keep[rows, :]) - n2, v

        def mixing(b):
            rows = rows_of(b)

            def stat_body(i):
                m, r = row_stats(R.midF[b, i].astype(F32))
                at = pl.ds(pl.multiple_of(b * TB + i * TC, TC), TC)
                L.mean[at, :] = m
                L.rstd[at, :] = r

            fori(8, stat_body)
            mid_border(b, 0).wait_recv()
            e = R.bmid[b]
            m = jnp.sum(jnp.sum(e, axis=0, keepdims=True), axis=1, keepdims=True) / D
            d = e - m
            v = jnp.sum(jnp.sum(d * d, axis=0, keepdims=True), axis=1, keepdims=True) / D
            L.bstat[b] = d * lax.rsqrt(v + EPS)
            if b == 0:
                for c in loads[0:2]:
                    c.wait()
            L.kp[rows, :] = jnp.zeros((TB, FFL), F32)
            L.rec[rows, :] = jnp.zeros((TB, W), F32)

            def body(i):
                at = pl.ds(pl.multiple_of(i * W, W), W)
                n2, d2, v = block(i, b)
                a = (n2 + d2 * v[14:15]).astype(BF)
                c = (n2 + d2 * v[15:16]).astype(BF)
                pk, pr = pairs(i)
                pk[rows, :] = a
                pr[rows, :] = c
                L.kp[rows, :] += nn(a, L.ck[at, :])
                L.rec[rows, :] += nn(c, L.cr[at, :])

            fori(8, body)
            g = jax.nn.sigmoid(L.rec[rows, :])
            L.rec[rows, :] = g
            R.gF[b, h] = (R.cot[b] * g).astype(BF).reshape(8, TC, W)
            gkvg[b].start()

        def hidden_units(b):
            def square(i):
                at = pl.ds(pl.multiple_of(b * TB + i * 64, 64), 64)
                u = L.kp[at, :]
                e = jnp.exp(-jnp.abs(u))
                p = jnp.maximum(u, 0.0) + jnp.log(1.0 + e)
                L.sq[at, :] = (p * p).astype(BF)
                L.kp[at, :] = 2.0 * p * jnp.where(u >= 0, 1.0, e) / (1.0 + e)

            fori(4, square)
            if b == 0:
                for g in cvs:
                    g.finish()
                loads[2].start()
                loads[2].wait()
            rs1[b].drain()

            def out(i):
                y = nn(L.sq[rows_of(b), :], L.cv[:, pl.ds(pl.multiple_of(i * W, W), W)])
                R.part[b, i] = y.astype(BF).reshape(8, TC, W)

            for k in (2, 1, 3, 0):
                out(rs2[b].theirs(k))
                rs2[b].give(k)
                out(rs2[b].ours(k))

        def key_grad(b):
            rows = rows_of(b)
            gkvg[b].finish()
            L.gs[...] = jnp.zeros_like(L.gs)

            def body(i):
                a = R.gF[b, i].reshape(TB, W)
                L.gs[...] += nt(a, L.cv[:, pl.ds(pl.multiple_of(i * W, W), W)])

            fori(8, body)
            L.gk[rows, :] = (L.gs[...] * L.kp[rows, :]).astype(BF)

        def result(b):
            rows = rows_of(b)
            co = rs2[b].total().reshape(TB, W)
            g = L.rec[rows, :]
            R.result[b] = slab_of(R.midF.at[b], h).astype(F32) + g * co
            L.gr[rows, :] = (R.cot[b] * co * g * (1.0 - g)).astype(BF)

        def back(b):
            rows = rows_of(b)
            rs2[b].drain()
            midg[b].drain()

            def body(i):
                at = pl.ds(pl.multiple_of(i * W, W), W)
                n2, d2, v = block(i, b)
                gpk = nt(L.gk[rows, :], L.ck[at, :])
                gpr = nt(L.gr[rows, :], L.cr[at, :])
                R.vg[i, 2 + 2 * b : 3 + 2 * b, :] = jnp.sum(gpk * d2, axis=0, keepdims=True)
                R.vg[i, 3 + 2 * b : 4 + 2 * b, :] = jnp.sum(gpr * d2, axis=0, keepdims=True)
                gd = gpk * v[14:15] + gpr * v[15:16]
                kg = gd * R.keep[rows, :]
                R.gsend[b, pl.ds(i, 1), :] = kg[0:1]
                y = gpk + gpr - gd + shift_up(kg)
                R.part[b, :, i] = y.astype(BF).reshape(8, TC, W)

            fori(8, body)
            for k in (2, 1, 3, 0):
                rs3[b].give(k)
            grad_border(b, h).start()

        def norm_back(b):
            u = R.mid[b]
            m, r = row_stats(u)
            n2 = (u - m[None]) * r[None]
            L.gout[...] = rs3[b].total()

            @pl.when(h == 7)
            def _():
                for i in range(8):
                    grad_border(b, i).wait_recv()
                t = jnp.sum(R.grecv[b], axis=0)
                for i in range(8):
                    L.gout[i, TC - 1 : TC, :] += t[i : i + 1]

            go = L.gout[...]
            gain = R.smF[:, R_VEC + 12 : R_VEC + 13, :].astype(F32)
            v12 = jnp.sum(go * n2, axis=1, keepdims=True)
            v13 = jnp.sum(go, axis=1, keepdims=True)
            if b == 0:
                R.vg[:, 0:1, :] = v12
                R.vg[:, 1:2, :] = v13
            else:
                R.vg[:, 0:1, :] += v12
                R.vg[:, 1:2, :] += v13
            gn = go * gain
            ma = jnp.sum(jnp.sum(gn, axis=0), axis=1, keepdims=True) / D
            mb = jnp.sum(jnp.sum(gn * n2, axis=0), axis=1, keepdims=True) / D
            R.midF[b, h] = (R.gch[b] + (gn - ma[None] - n2 * mb[None]) * r[None]).astype(BF)
            gzg[b].start()

        def staged(home, rows, xfirst, sem, make):
            def copies(i):
                got = []
                for e in range(2):
                    q = 2 * i + e
                    if not xfirst:
                        q = lax.rem(q, 4) * 4 + q // 4
                    at = lax.rem(i, 2)
                    got.append(
                        pltpu.make_async_copy(
                            L.stage.at[at, e, 0:rows], home.at[q], R.ls.at[sem + 2 * at + e]
                        )
                    )
                return got

            def body(i):
                @pl.when(i >= 2)
                def _():
                    for c in copies(i - 2):
                        c.wait()

                y = make(i)
                for e in range(2):
                    at = 0
                    for t in y:
                        L.stage[lax.rem(i, 2), e, at : at + t.shape[0], :] = t[
                            :, 128 * e : 128 * e + 128
                        ].astype(BF)
                        at += t.shape[0]
                for c in copies(i):
                    c.start()

            fori(8, body)
            for i in (6, 7):
                for c in copies(i):
                    c.wait()

        def value_weight():
            L.tr[...] = L.sq[...].T
            staged(
                R.gbH, FFL, False, 28, lambda i: [nn(L.tr[...], R.gF[:, i].reshape(N, W))]
            )

        def key_weight():
            L.tr[...] = L.gk[...].T
            L.grT[...] = L.gr[...].T

            def make(i):
                pk, pr = pairs(i)
                return [nn(L.tr[...], pk[...]), nn(L.grT[...], pr[...])]

            staged(R.gaH, FFL + W, True, 32, make)

        middle(0)
        rs1[1].pass_near()
        for g in cks:
            g.p3()
        midg[0].relay()
        midg[0].relay_far()
        middle(1)
        for g in cvs:
            g.p2(True)
        for g in cks:
            g.finish()
        for c in loads[0:2]:
            c.start()
        for t in tws:
            t.drain()
        midg[0].finish()
        midg[1].relay()
        mixing(0)
        midg[1].relay_far()
        midg[1].finish()
        gkvg[0].relay()
        for g in cvs:
            g.p3()
        mixing(1)
        gkvg[0].relay_far()
        hidden_units(0)
        gkvg[1].relay()
        rs2[0].pass_far()
        gkvg[1].relay_far()
        key_grad(0)
        rs2[0].pass_near()
        hidden_units(1)
        rs2[1].pass_far()
        result(0)
        back(0)
        rs2[1].pass_near()
        key_grad(1)
        rs3[0].pass_far()
        value_weight()
        result(1)
        rs3[0].pass_near()
        back(1)
        for c in cots.values():
            c.wait_recv()
        scb.near()
        scb.own().start()
        norm_back(0)
        rs3[1].pass_far()
        key_weight()
        sca.near()
        sca.own().start()
        gzg[0].relay()
        rs3[1].pass_near()
        gzg[0].relay_far()
        norm_back(1)

    for b in both:
        R.gch[b, h] = R.cot[b, pl.ds(pl.multiple_of(h * TC, TC), TC), :]
    pl.run_scoped(
        channel,
        ck=pltpu.VMEM((D, FFL), BF),
        cv=pltpu.VMEM((FFL, D), BF),
        cr=pltpu.VMEM((D, W), BF),
        mean=pltpu.VMEM((N, 1), F32),
        rstd=pltpu.VMEM((N, 1), F32),
        bstat=pltpu.VMEM((2, 8, W), F32),
        kp=pltpu.VMEM((N, FFL), F32),
        rec=f32n,
        sq=pltpu.VMEM((N, FFL), BF),
        gk=pltpu.VMEM((N, FFL), BF),
        gr=pltpu.VMEM((N, W), BF),
        gs=pltpu.VMEM((TB, FFL), F32),
        tr=pltpu.VMEM((FFL, N), BF),
        grT=pltpu.VMEM((W, N), BF),
        gout=pltpu.VMEM((8, TC, W), F32),
        stage=pltpu.VMEM((2, 2, FFL + W, 128), BF),
    )

    def time_backward(**kw):
        O = SimpleNamespace(**kw)
        sea = SeqScatter(net, O.ea, R.ea1, O.ea2, R.ea3, O.eat, True)
        seb = SeqScatter(net, O.eb, R.eb1, O.eb2, R.eb3, O.ebt, False)
        O.shT[...] = R.sh[...].T.astype(BF)
        for b in both:
            gkvg[b].drain()

        def shm(j, rows):
            return (R.sh[rows, :] * R.shmask[j : j + 1, :]).astype(BF)

        def wkv_backward(**kw):
            L = SimpleNamespace(**kw)

            def gated(b):
                rows = rows_of(b)
                L.gated[rows, :] = jnp.zeros((TB, W), F32)

                def body(i):
                    a = slab_of(R.midF.at[b], i)
                    L.gated[rows, :] += nt(a, R.toV[:, pl.ds(pl.multiple_of(i * W, W), W)])

                fori(8, body)

                def gate_body(i, acc):
                    at = pl.ds(pl.multiple_of(b * TB + i * 64, 64), 64)
                    gd = L.gated[at, :]
                    gn = R.gnorm[at, :]
                    g = R.proj[3, at, :].astype(F32)
                    sg = jax.nn.sigmoid(g)
                    gno = gd * (g * sg)
                    dg = gd * (gn * vl[10:11] + vl[11:12]) * sg * (1.0 + g * (1.0 - sg))
                    O.gp[3, at, :] = dg.astype(BF)
                    gg = gno * vl[10:11]
                    ma = head_sum(gg, hmb) / 64.0
                    mb = head_sum(gg * gn, hmb) / 64.0
                    L.go[at, :] = R.gscale[at, :] * (gg - ma - gn * mb)
                    return (
                        acc[0] + jnp.sum(gno * gn, axis=0, keepdims=True),
                        acc[1] + jnp.sum(gno, axis=0, keepdims=True),
                    )

                return lax.fori_loop(0, 4, gate_body, (z1, z1))

            def adjoint(b):
                L.ds[b] = jnp.zeros((W, W), F32)
                L.tsuf[8 + b : 9 + b, :] = jnp.ones((1, W), F32)

                def body(e):
                    i = b * 4 + 3 - e
                    rows = pl.ds(pl.multiple_of(i * C, C), C)
                    L.dsl[i] = L.ds[b].astype(BF)
                    t = R.tch[pl.ds(i, 1), :]
                    after = L.tsuf[8 + b : 9 + b, :]
                    L.tsuf[pl.ds(i, 1), :] = after
                    L.tsuf[8 + b : 9 + b, :] = after * t
                    L.ds[b] = L.ds[b] * t + nn(L.go[rows, :].T.astype(BF), R.rp[rows, :]) * hmf

                fori(4, body)
                carry_send(1, b, L.ds[b], L.tsuf[8 + b : 9 + b, :])

            def output_weight():
                L.gatT[...] = R.gate[...].T

                def body(i):
                    a = R.midF[:, :, i].reshape(N, W)
                    put(O.eb, i, 0, nn(L.gatT[...], a).astype(BF), False)

                fori(8, body)

            def gate_weight():
                O.gpT[3] = O.gp[3].T

                def body(i):
                    y = jnp.zeros((W, W), F32)
                    for b in both:
                        rows = rows_of(b)
                        n, normed, differ, v = n1.block(i, b)
                        mix = nn(shm(4, rows), R.smF[i, R_SECOND : R_SECOND + 160, :])
                        target = (normed + differ * (v[7:8] + mix)).astype(BF)
                        y = y + nn(O.gpT[3, :, rows], target)
                    put(O.ea, i, 0, y.astype(BF), True)

                fori(8, body)

            def inner(b, gu):
                def body(c, gu):
                    rows = pl.ds(pl.multiple_of(b * TB + c * C, C), C)
                    r, k, v = [R.proj[j, rows, :].astype(F32) for j in (2, 0, 1)]
                    g, kp = L.go[rows, :], R.keep[rows, :]
                    lv, p, q, t = tree(r, k, jnp.exp(R.logd[rows, :]) * kp, kp)
                    L.pP[rows, :] = p
                    L.pQ[rows, :] = q
                    vb, gb = v.astype(BF), g.astype(BF)
                    gsp = spread(gb, hmb)
                    da = nt(gb, spread(vb, hmb))
                    dat = nt(vb, gsp)
                    row = iota((C, W), 0)
                    agr = jnp.zeros((C, W), F32)
                    agk = jnp.zeros((C, W), F32)
                    ys = []
                    for l, (a, e) in enumerate(lv):
                        x = (a * e).astype(BF)
                        d = (da * R.levels[l] + dat * R.levels[LV + l]).astype(BF)
                        gx = nn(d, spread(x, hmb))
                        second = (row // (1 << l)) % 2 == 1
                        ge = gx * e
                        agr = agr + jnp.where(second, ge, 0.0)
                        agk = agk + jnp.where(second, 0.0, ge)
                        ys.append((x.astype(F32) * gx).astype(BF))
                    L.gG[rows, :] = nn(R.sums[:, 0 : LV * C], jnp.concatenate(ys, axis=0))
                    u = vl[9:10]
                    dad = head_sum(g * v, hmb)
                    bonus = head_sum(r * u * k, hmb)
                    L.gr[rows, :] = agr + u * k * dad
                    L.gk[rows, :] = agk + u * r * dad
                    L.gv[rows, :] = nn(R.scores[rows, :], gsp) + bonus * g
                    return gu + jnp.sum(r * k * dad, axis=0, keepdims=True)

                return lax.fori_loop(0, 4, body, gu)

            def outer(b, g8):
                L.ds[b] = carry_wait(1, b, hmf)

                def body(c, g8):
                    i = b * 4 + c
                    rows = pl.ds(pl.multiple_of(i * C, C), C)
                    st = unfold(R.starts[i].astype(F32), hmf)
                    de = L.dsl[i].astype(F32) + L.ds[b] * L.tsuf[pl.ds(i, 1), :]
                    deb = de.astype(BF)
                    p, q = L.pP[rows, :], L.pQ[rows, :]
                    kq = (R.proj[0, rows, :].astype(F32) * q).astype(BF)
                    rpc = R.rp[rows, :]
                    gkq = nn(R.proj[1, rows, :], deb)
                    grp = nn(L.go[rows, :].astype(BF), st.astype(BF))
                    O.gp[1, rows, :] = (L.gv[rows, :] + nt(kq, deb)).astype(BF)
                    O.gp[0, rows, :] = (L.gk[rows, :] + gkq * q).astype(BF)
                    O.gp[2, rows, :] = (L.gr[rows, :] + grp * p).astype(BF)
                    ky = (kq.astype(F32) * gkq).astype(BF)
                    ry = (rpc.astype(F32) * grp).astype(BF)
                    cst = jnp.sum(st * de, axis=0, keepdims=True) * R.tch[pl.ds(i, 1), :]
                    gl = nn(R.sums[:, LV * C :], jnp.concatenate([ky, ry], axis=0))
                    gw = (L.gG[rows, :] + gl + cst) * R.logd[rows, :]
                    O.gw[rows, :] = gw.astype(BF)
                    return g8 + jnp.sum(gw, axis=0, keepdims=True)

                return lax.fori_loop(0, 4, body, g8)

            sca.tmp, scb.tmp = L.rat, L.rbt
            gzg[0].finish()
            gzg[1].relay()
            a10, a11 = gated(0)
            adjoint(0)
            gzg[1].relay_far()
            gzg[1].finish()
            b10, b11 = gated(1)
            adjoint(1)
            scb.far([L.stage.at[0, :, 0:FFL], L.stage.at[1, :, 0:FFL]])
            sca.far([L.stage.at[0], L.stage.at[1]])
            output_weight()
            seb.near()
            g9 = inner(0, z1)
            gate_weight()
            sea.near()
            seb.far()
            g9 = inner(1, g9)
            scb.p2([L.stage.at[0, :, 0:FFL], L.stage.at[1, :, 0:FFL]])
            sea.far()
            g8 = outer(0, z1)
            sca.p2([L.stage.at[0], L.stage.at[1]])
            g8 = outer(1, g8)
            net.drain([sca.ua, sca.db, scb.ua, scb.db])
            R.gvec[0:1, :] = g8
            R.gvec[1:2, :] = g9
            R.gvec[2:3, :] = a10 + b10
            R.gvec[3:4, :] = a11 + b11

        reload = pltpu.make_async_copy(R.twF, R.twV, R.ls.at[10])
        reload.start()
        pl.run_scoped(
            wkv_backward,
            gated=f32n,
            go=f32n,
            gr=f32n,
            gk=f32n,
            gv=f32n,
            gG=f32n,
            pP=f32n,
            pQ=f32n,
            dsl=pltpu.VMEM((8, W, W), BF),
            ds=pltpu.VMEM((2, W, W), F32),
            tsuf=pltpu.VMEM((16, W), F32),
            gatT=pltpu.VMEM((W, N), BF),
            rat=pltpu.VMEM((2, 2, FFL + W, 128), BF),
            rbt=pltpu.VMEM((2, 2, FFL, 128), BF),
            stage=pltpu.VMEM((2, 3, FFL + W, 128), BF),
        )

        for j in range(3):
            O.gpT[j] = O.gp[j].T
        dhv = R.dh[...]
        gdv = nt(O.gw[...], R.ds2[...]) * (1.0 - dhv * dhv)
        O.gdp[...] = gdv.astype(BF)
        O.gdpT[...] = gdv.T.astype(BF)
        O.lsm[400:464, :] = nn(dhv.T.astype(BF), O.gw[...])
        reload.wait()

        def normed_back(**kw):
            L = SimpleNamespace(**kw)
            sta = SeqScatter(net, L.ta, R.ta1, L.ta2, R.ta3, L.tat, True)
            stb = SeqScatter(net, L.tb, R.tb1, L.tb2, R.tb3, L.tbt, False)
            sms = HeadScatter(net, L.sg, R.sgsib, L.sgsend, R.sgz)
            L.gsh[...] = jnp.zeros_like(L.gsh)
            rank = iota((160, W), 0)

            def target_body(i):
                at = pl.ds(pl.multiple_of(i * W, W), W)
                second = R.smF[i, R_SECOND : R_SECOND + 160, :]
                dfirst = R.smF[i, R_DECAY1 : R_DECAY1 + 64, :]
                ws = [jnp.zeros((W, W), F32) for _ in range(3)]
                gsec = jnp.zeros((160, W), F32)
                gd1 = jnp.zeros((64, W), F32)
                rowsum = [z1] * 5
                for b in both:
                    rows = rows_of(b)
                    n, normed, differ, v = n1.block(i, b)
                    a1 = jnp.zeros((TB, W), F32)
                    a2 = jnp.zeros((TB, W), F32)
                    for j in range(5):
                        m = v[3 + j : 4 + j] + nn(shm(j, rows), second)
                        if j < 4:
                            target = (normed + differ * m).astype(BF)
                        if j == 0:
                            gt = nn(O.gdp[rows, :], dfirst)
                            gd1 = gd1 + nn(O.gdpT[:, rows], target)
                        else:
                            gt = nt(O.gp[j - 1, rows, :], R.twV[j - 1, at, :])
                            if j < 4:
                                ws[j - 1] = ws[j - 1] + nn(O.gpT[j - 1, :, rows], target)
                        a1 = a1 + gt
                        a2 = a2 + gt * m
                        qv = gt * differ
                        rowsum[j] = rowsum[j] + jnp.sum(qv, axis=0, keepdims=True)
                        qb = qv.astype(BF)
                        gsec = gsec + jnp.where(rank // 32 == j, nn(O.shT[:, rows], qb), 0.0)
                        L.gsh[rows, :] += nt(qb, second) * R.shmask[j : j + 1, :]
                    L.s1[i, rows, :] = a1.astype(BF)
                    R.gF[b, i] = a2.astype(BF).reshape(8, TC, W)
                put(L.ta, i, 0, ws[0].astype(BF), True)
                put(L.tb, i, 0, ws[1].astype(BF), False)
                put(L.ta, i, W, ws[2][0:128].astype(BF), True)
                put(L.tb, i, W, ws[2][128:256].astype(BF), False)
                L.sg[i, R_SECOND : R_SECOND + 160, :] = gsec.astype(BF)
                L.sg[i, R_DECAY1 : R_DECAY1 + 64, :] = gd1.astype(BF)
                for j in range(5):
                    L.psm[i, 3 + j : 4 + j, :] = rowsum[j]

            fori(8, target_body)
            sea.p2()
            seb.p2()
            sta.near()
            stb.near()
            hidden = R.sh[...]
            gs2 = L.gsh[...] * (1.0 - hidden * hidden)
            L.gshp[...] = gs2.astype(BF)
            L.gshpT[...] = gs2.T.astype(BF)
            L.rsum[...] = jnp.zeros_like(L.rsum)
            lane = iota((TB, 128), 1)

            def mixed_back(b):
                rows = rows_of(b)

                def body(i):
                    first = R.smF[i, R_FIRST : R_FIRST + 160, :]
                    n, normed, differ, v = n1.block(i, b)
                    mixed = (normed + differ * v[2:3]).astype(BF)
                    gm = nn(L.gshp[rows, :], first)
                    gf = nn(L.gshpT[:, rows], mixed)
                    g2 = jnp.sum(gm * differ, axis=0, keepdims=True)
                    gd = R.gF[b, i].reshape(TB, W).astype(F32) + gm * v[2:3]
                    kg = gd * R.keep[rows, :]
                    R.bsend[i, b : b + 1, :] = kg[0:1]
                    gn = L.s1[i, rows, :].astype(F32) + gm - gd + shift_up(kg)
                    R.part[b, i] = gn.astype(BF).reshape(8, TC, W)
                    gg = gn * v[0:1]
                    ra = jnp.sum(gg, axis=1, keepdims=True)
                    rb = jnp.sum(gg * n, axis=1, keepdims=True)
                    L.rsum[rows, :] += jnp.where(lane == 0, ra, jnp.where(lane == 1, rb, 0.0))
                    if b == 0:
                        L.sg[i, R_FIRST : R_FIRST + 160, :] = gf.astype(BF)
                        L.psm[i, 2:3, :] = g2
                    else:
                        had = L.sg[i, R_FIRST : R_FIRST + 160, :].astype(F32)
                        L.sg[i, R_FIRST : R_FIRST + 160, :] = (had + gf).astype(BF)
                        vg = R.vg[i]
                        L.sg[i, R_VEC : R_VEC + 16, :] = jnp.concatenate(
                            [
                                jnp.zeros((2, W), F32),
                                L.psm[i, 2:3, :] + g2,
                                L.psm[i, 3:8, :],
                                jnp.zeros((4, W), F32),
                                vg[0:2],
                                vg[2:4] + vg[4:6],
                            ],
                            axis=0,
                        ).astype(BF)

                if b == 0:
                    fori(8, body)
                else:
                    fori(4, body)
                    rs4[0].pass_far()
                    fori(4, lambda i: body(i + 4))
                for k in (2, 1, 3, 0):
                    rs4[b].give(k)

            for b in both:
                rs3[b].drain()
            R.bsend[...] = jnp.zeros_like(R.bsend)
            mixed_back(0)
            mixed_back(1)
            for c in last:
                c.start()
            for k in (2, 1, 3, 0):
                sms.give(k)
            sta.far()
            stb.far()
            rs4[0].pass_near()
            sms.pass_far()
            rs4[1].pass_far()
            sca.finish(R.oca)
            scb.finish(R.ocb)
            for c in last:
                c.wait_recv()
            edge = jnp.sum(R.brecv[...], axis=0)
            lane8 = iota((1, 128), 1)
            for b in both:
                at = slice(b * TB + TB - 16, b * TB + TB)
                n = (R.xF[b, h, TB - 16 : TB, :].astype(F32) - R.mean[at, :]) * R.rstd[at, :]
                e = edge[b : b + 1] * vl[0:1]
                ra = jnp.sum(e, axis=1, keepdims=True)
                rb = jnp.sum(e * n[15:16], axis=1, keepdims=True)
                end = slice(b * TB + TB - 1, b * TB + TB)
                L.rsum[end, :] += jnp.where(lane8 == 0, ra, jnp.where(lane8 == 1, rb, 0.0))
            R.rsend[...] = L.rsum[...].T[0:8]
            R.rrecv[h] = R.rsend[...]
            for c in rex:
                c.start()
            sms.pass_near()
            rs4[1].pass_near()
            g0, g1 = z1, z1
            for b in both:
                rows = rows_of(b)
                R.mid[b] = rs4[b].total()
                R.mid[b, 7, TC - 1 : TC, :] += edge[b : b + 1]
                gl = R.mid[b].reshape(TB, W)
                n = (R.xF[b, h].astype(F32) - R.mean[rows, :]) * R.rstd[rows, :]
                g0 = g0 + jnp.sum(gl * n, axis=0, keepdims=True)
                g1 = g1 + jnp.sum(gl, axis=0, keepdims=True)
            O.lsm[0:400, :] = sms.total()
            O.lsm[R_VEC : R_VEC + 2, :] += jnp.concatenate([g0, g1], axis=0)
            O.lsm[R_VEC + 8 : R_VEC + 12, :] += R.gvec[0:4, :]
            packed = lax.dot_general(
                R.sel[...],
                O.lsm[...].astype(BF),
                (((0,), (0,)), ((), ())),
                preferred_element_type=F32,
            )
            R.psend[...] = packed.astype(BF).reshape(16, 32, W)
            for c in smo:
                c.start()
            sta.p2()
            stb.p2()
            for c in rex:
                c.wait_recv()
            tot = jnp.sum(R.rrecv[...], axis=0)
            L.rsum[...] = jnp.concatenate([tot, jnp.zeros((120, N), F32)], axis=0).T / D
            for b in both:
                rows = rows_of(b)
                gl = R.mid[b].reshape(TB, W)
                n = (R.xF[b, h].astype(F32) - R.mean[rows, :]) * R.rstd[rows, :]
                R.hgrad[b] = slab_of(R.midF.at[b], h).astype(F32) + R.rstd[rows, :] * (
                    gl * vl[0:1] - L.rsum[rows, 0:1] - n * L.rsum[rows, 1:2]
                )
            sea.finish(R.oea)
            seb.finish(R.oeb)
            R.psrecv[s] = R.psend[s]
            for c in smo:
                c.wait_recv()
            R.osm[...] = jnp.sum(R.psrecv[...].astype(F32), axis=0)
            sta.finish(R.ota)
            stb.finish(R.otb)
            net.drain()

        RT = W + 128
        pl.run_scoped(
            normed_back,
            s1=pltpu.VMEM((8, N, W), BF),
            ta=pltpu.VMEM((16, RT, 128), BF),
            tb=pltpu.VMEM((16, RT, 128), BF),
            ta2=pltpu.VMEM((4, RT, 128), BF),
            tat=pltpu.VMEM((2, 2, RT, 128), BF),
            tbt=pltpu.VMEM((2, 2, RT, 128), BF),
            tb2=pltpu.VMEM((4, RT, 128), BF),
            sg=pltpu.VMEM((8, 400, W), BF),
            sgsend=pltpu.VMEM((3, 400, W), BF),
            gsh=pltpu.VMEM((N, 160), F32),
            gshp=pltpu.VMEM((N, 160), BF),
            gshpT=pltpu.VMEM((160, N), BF),
            rsum=pltpu.VMEM((N, 128), F32),
            psm=pltpu.VMEM((8, 8, W), F32),
        )

    pl.run_scoped(
        time_backward,
        ea=pltpu.VMEM((16, W, 128), BF),
        eb=pltpu.VMEM((16, W, 128), BF),
        ea2=pltpu.VMEM((4, W, 128), BF),
        eat=pltpu.VMEM((2, 2, W, 128), BF),
        ebt=pltpu.VMEM((2, 2, W, 128), BF),
        eb2=pltpu.VMEM((4, W, 128), BF),
        gp=pltpu.VMEM((4, N, W), BF),
        gpT=pltpu.VMEM((4, W, N), BF),
        shT=pltpu.VMEM((160, N), BF),
        gw=pltpu.VMEM((N, W), BF),
        gdp=pltpu.VMEM((N, 64), BF),
        gdpT=pltpu.VMEM((64, N), BF),
        lsm=pltpu.VMEM((464, W), F32),
    )
    for b in both:

        @pl.when(h == 7)
        def _():
            for k in range(8):
                mid_border(b, k).wait_send()

        grad_border(b, h).wait_send()
        for e in both:
            carry_each(e, b, lambda c: c.wait_send())


def put(ref, i, row, y, xfirst):
    for e in range(2):
        q = 2 * i + e
        if not xfirst:
            q = lax.rem(q, 4) * 4 + q // 4
        ref[q, row : row + y.shape[0], :] = y[:, 128 * e : 128 * e + 128]


VM = pl.BlockSpec(memory_space=pltpu.VMEM)
HB = pl.BlockSpec(memory_space=pl.ANY)
SD = jax.ShapeDtypeStruct


def run_layer(ins):
    far = ("tw", "to", "ck", "cv", "cr")
    RA, RB, RT = FFL + W, FFL, W + 128
    outs = dict(
        result=((2, TB, W), F32, VM),
        hgrad=((2, TB, W), F32, VM),
        oca=((RA, 128), F32, VM),
        ocb=((RB, 128), F32, VM),
        oea=((W, 128), F32, VM),
        oeb=((W, 128), F32, VM),
        ota=((RT, 128), F32, VM),
        otb=((RT, 128), F32, VM),
        osm=((32, W), F32, VM),
        twF=((4, D, W), BF, HB),
        ckF=((D, FFL), BF, HB),
        cvF=((FFL, D), BF, HB),
        crF=((D, W), BF, HB),
        gaH=((16, RA, 128), BF, HB),
        gbH=((16, RB, 128), BF, HB),
        ra1=((3, 4, RA, 128), BF, HB),
        rb1=((3, 4, RB, 128), BF, HB),
    )
    scr = dict(
        small=((32, W), BF),
        sm=((16, 32, W), BF),
        bsrc=((32, W), BF),
        xF=((2, 8, TB, W), BF),
        bord=((8, 32, W), BF),
        smF=((8, 400, W), BF),
        ds2=((64, W), BF),
        twV=((4, D, W), BF),
        toV=((W, D), BF),
        midF=((2, 8, 8, TC, W), BF),
        mid=((2, 8, TC, W), F32),
        mb=((2, 8, W), F32),
        bmid=((2, 8, W), F32),
        gch=((2, 8, TC, W), F32),
        gF=((2, 8, 8, TC, W), BF),
        mean=((N, 1), F32),
        rstd=((N, 1), F32),
        bmean=((32, 1), F32),
        brstd=((32, 1), F32),
        sh=((N, 160), F32),
        dh=((N, 64), F32),
        proj=((4, N, W), BF),
        logd=((N, W), F32),
        gnorm=((N, W), F32),
        gscale=((N, W), F32),
        scores=((N, W), BF),
        starts=((8, 128, 128), BF),
        rp=((N, W), BF),
        gate=((N, W), BF),
        tch=((8, W), F32),
        tpre=((16, W), F32),
        carry=((2, 128, 128), F32),
        csend=((2, 2, 144, 128), BF),
        crecv=((2, 16, 144, 128), BF),
        part=((2, 8, 8, TC, W), BF),
        tosend=((2, 3, 8, TC, W), BF),
        fromsib=((2, 2, 4, 8, TC, W), BF),
        fromz=((2, 2, 3, 8, TC, W), BF),
        gsend=((2, 8, W), F32),
        grecv=((2, 8, 8, W), F32),
        vg=((8, 8, W), F32),
        gvec=((8, W), F32),
        bsend=((8, 8, W), F32),
        brecv=((8, 8, W), F32),
        rsend=((8, N), F32),
        rrecv=((8, 8, N), F32),
        sgsib=((4, 400, W), BF),
        sgz=((3, 400, W), BF),
        psend=((16, 32, W), BF),
        psrecv=((16, 32, W), BF),
        ra2=((4, RA, 128), BF),
        ra3=((3, RA, 128), BF),
        rb2=((4, RB, 128), BF),
        rb3=((3, RB, 128), BF),
        ea1=((3, 4, W, 128), BF),
        ea3=((3, W, 128), BF),
        eb1=((3, 4, W, 128), BF),
        eb3=((3, W, 128), BF),
        ta1=((3, 4, RT, 128), BF),
        ta3=((3, RT, 128), BF),
        tb1=((3, 4, RT, 128), BF),
        tb3=((3, RT, 128), BF),
    )
    sems = dict(ss=480, rs=480, ls=38, bs=18, br=18, cs=64, cr_=64)
    names = list(ins) + list(outs) + list(scr) + list(sems)
    got = pl.pallas_call(
        functools.partial(layer_kernel, names),
        out_shape=[SD(a, t) for a, t, _ in outs.values()],
        in_specs=[HB if k in far else VM for k in ins],
        out_specs=[m for _, _, m in outs.values()],
        scratch_shapes=[pltpu.VMEM(a, t) for a, t in scr.values()]
        + [pltpu.SemaphoreType.DMA((n,)) for n in sems.values()],
        name="layer",
        compiler_params=pltpu.CompilerParams(
            collective_id=1, has_side_effects=True, vmem_limit_bytes=VMEM_LIMIT
        ),
    )(*ins.values())
    return SimpleNamespace(**dict(zip(outs, got)))


def on_device(
    hidden, cotangent, opening_flags, vectors, shift_first, shift_second, decay_first, decay_second,
    time_weights, time_output, channel_key, channel_value, channel_recept,
):
    sel, shmask, hm, levels, sums = constants()
    o = run_layer(
        dict(
            x=hidden,
            cot=cotangent,
            keep=(1.0 - opening_flags.astype(F32)).reshape(N, 1),
            sf=shift_first[0],
            s2nd=shift_second[0],
            d1st=decay_first[0],
            d2nd=decay_second[0],
            vectors=vectors[0],
            sel=sel,
            shmask=shmask,
            hm=hm,
            levels=levels,
            sums=sums,
            tw=time_weights[0],
            to=time_output[0],
            ck=channel_key[0],
            cv=channel_value[0],
            cr=channel_recept[0],
        )
    )
    return finish(o.result, o.hgrad, o.oca, o.ocb, o.oea, o.oeb, o.ota, o.otb, o.osm)


def finish_kernel(
    result, hg, ca, cb, ea, eb, ta, tb, sm,
    o_result, o_hidden, o_vec, o_first, o_second, o_decay1, o_decay2, o_time, o_out, o_key, o_value,
    o_recept,
):
    o_result[...] = result[...]
    o_hidden[...] = hg[...]
    o_first[0] = sm[0:10]
    o_second[0] = sm[10:20]
    o_decay1[0] = sm[20:24]
    o_decay2[0] = sm[24:28]
    o_vec[0] = sm[28:29]
    o_time[0, 0] = ta[0:W].T
    o_time[0, 1] = tb[0:W].T
    o_time[0, 2, :, 0:128] = ta[W:].T
    o_time[0, 2, :, 128:256] = tb[W:].T
    o_time[0, 3] = ea[...].T
    o_out[0] = eb[...]
    o_key[0] = ca[0:FFL].T
    o_value[0] = cb[...]
    o_recept[0] = ca[FFL:].T


def finish(*ins):
    shapes = [
        (2, TB, W), (2, TB, W), (1, 1, W), (1, 10, W), (1, 10, W), (1, 4, W), (1, 4, W),
        (1, 4, 128, W), (1, W, 128), (1, 128, FFL), (1, FFL, 128), (1, 128, W),
    ]
    return pl.pallas_call(
        finish_kernel,
        out_shape=[SD(q, F32) for q in shapes],
        in_specs=[VM] * len(ins),
        out_specs=[VM] * len(shapes),
        name="finish",
        compiler_params=pltpu.CompilerParams(vmem_limit_bytes=VMEM_LIMIT),
    )(*ins)


def solution(mesh):
    last = P(None, "seq", "head")
    turned = P(None, "head", "seq")
    four = P(None, None, "seq", "head")
    return jax.shard_map(
        on_device,
        mesh=mesh,
        in_specs=(last, last, P(None, "seq"), last, last, last, last, last, four, turned, last, turned, last),
        out_specs=(last, last, last, last, last, last, last, four, turned, last, turned, last),
        check_vma=False,
    )
```

```python
import functools
from types import SimpleNamespace

import jax
import jax.numpy as jnp
import numpy as np
from jax import lax
from jax.experimental import pallas as pl
from jax.experimental.pallas import tpu as pltpu
from jax.sharding import PartitionSpec as P

MESH = pl.DeviceIdType.MESH
BF = jnp.bfloat16
F32 = jnp.float32
EPS = 1e-5
GEPS = 64e-5
N = 512
TB = 256
TC = 32
W = 256
C = 64
LV = 6
D = 2048
FFL = 896
VMEM_LIMIT = 63 * 2**20
R_FIRST, R_SECOND, R_DECAY1, R_VEC, R_DECAY2 = 0, 160, 320, 384, 400


def nt(a, b):
    return lax.dot_general(a, b, (((1,), (1,)), ((), ())), preferred_element_type=F32)


def nn(a, b):
    return jnp.dot(a, b, preferred_element_type=F32)


def place():
    return lax.axis_index("seq"), lax.axis_index("head")


def sibling():
    s, h = place()
    return s, h // 2 * 2 + 1 - lax.rem(h, 2)


def chip(k, core=0):
    h = place()[1]
    c = lax.rem(h, 2)
    return lax.rem(h // 2 + k, 4) * 2 + (1 - c if core else c)


def zdev(k):
    return place()[0], chip(k)


def seq_index(first, ka, kb):
    s = place()[0]
    x, y = s // 4, lax.rem(s, 4)
    if first:
        return lax.rem(x + ka, 4) * 4 + lax.rem(y + kb, 4)
    return lax.rem(x + kb, 4) * 4 + lax.rem(y + ka, 4)


def seq_dev(first, ka, kb):
    return seq_index(first, ka, kb), place()[1]


class Copy:
    def __init__(self, net, i, make):
        self.net, self.i, self.make = net, i, make

    def desc(self):
        src, dst, dev = self.make()
        return pltpu.make_async_remote_copy(
            src_ref=src,
            dst_ref=dst,
            send_sem=self.net.ss.at[self.i],
            recv_sem=self.net.rs.at[self.i],
            device_id=dev,
            device_id_type=MESH,
        )

    def start(self):
        self.desc().start()
        self.net.out.append(self)

    def wait_recv(self):
        self.desc().wait_recv()

    def wait_send(self):
        self.desc().wait_send()


class Net:
    def __init__(self, ss, rs):
        self.ss, self.rs, self.n, self.out = ss, rs, 0, []

    def copy(self, make):
        self.n += 1
        return Copy(self, self.n - 1, make)

    def drain(self, copies=None):
        for c in list(self.out) if copies is None else copies:
            c.wait_send()
            self.out.remove(c)


def greet(peers):
    b = pltpu.get_barrier_semaphore()
    for p in peers:
        pl.semaphore_signal(b, inc=1, device_id=p, device_id_type=MESH)
    pl.semaphore_wait(b, len(peers))


def head_peers():
    s, h = place()
    return [(s, lax.rem(h + k, 8)) for k in range(1, 8)]


def seq_peers():
    s, h = place()
    return [(lax.rem(s + k, 16), h) for k in range(1, 16)]


def diagonal_peers(step):
    s, h = place()
    return [(lax.rem(s + step, 16), lax.rem(h + k, 8)) for k in range(1, 8)]


ORDER = (1, 3, 2)


def half(ref, i):
    n = ref.shape[0]
    m = n // 2 if len(ref.shape) == 3 else (n // 2 + 15) // 16 * 16
    return ref.at[m:n] if i else ref.at[0:m]


class HeadGather:
    def __init__(self, net, slot):
        self.net = net

        def own():
            return slot(place()[1])

        def at(k):
            return slot(chip(k))

        def copy(ref, dev):
            return net.copy(lambda: (ref(), ref(), dev()))

        up, down = lambda: zdev(1), lambda: zdev(3)
        self.ua = copy(lambda: half(own(), 0), up)
        self.db = copy(lambda: half(own(), 1), down)
        self.ub = copy(lambda: half(own(), 1), up)
        self.da = copy(lambda: half(own(), 0), down)
        self.mine = copy(own, sibling)
        self.fa = copy(lambda: half(at(3), 0), up)
        self.fb = copy(lambda: half(at(1), 1), down)
        self.s3 = copy(lambda: at(3), sibling)
        self.s1 = copy(lambda: at(1), sibling)
        self.sa = copy(lambda: half(at(2), 0), sibling)
        self.sb = copy(lambda: half(at(2), 1), sibling)

    def start(self):
        for c in (self.ua, self.db, self.ub, self.da, self.mine):
            c.start()

    def relay(self):
        self.ua.wait_recv()
        self.fa.start()
        self.db.wait_recv()
        self.fb.start()
        self.ub.wait_recv()
        self.s3.start()
        self.da.wait_recv()
        self.s1.start()

    def relay_far(self):
        self.fa.wait_recv()
        self.sa.start()
        self.fb.wait_recv()
        self.sb.start()

    def finish(self):
        for c in (self.mine, self.s3, self.s1, self.sa, self.sb):
            c.wait_recv()

    def drain(self):
        near = [self.ua, self.db, self.ub, self.da, self.mine]
        self.net.drain(near + [self.fa, self.fb, self.s3, self.s1, self.sa, self.sb])


class HeadScatter:
    def __init__(self, net, part, fromsib, tosend, fromz):
        self.net, self.part, self.fromsib, self.tosend, self.fromz = net, part, fromsib, tosend, fromz
        self.a = {
            k: net.copy(lambda k=k: (part.at[chip(k, 1)], fromsib.at[k], sibling()))
            for k in range(4)
        }

        def copy(i, j, k, dev):
            return net.copy(lambda: (half(tosend.at[i], k), half(fromz.at[j], k), zdev(dev)))

        self.fa, self.fb = copy(1, 2, 0, 1), copy(1, 2, 1, 3)
        self.ua, self.ub = copy(0, 0, 0, 1), copy(0, 0, 1, 1)
        self.da, self.db = copy(2, 1, 0, 3), copy(2, 1, 1, 3)
        self.all = [*self.a.values(), self.fa, self.fb, self.ua, self.ub, self.da, self.db]

    def theirs(self, k):
        return chip(k, 1)

    def ours(self, k):
        return chip(k)

    def give(self, k):
        self.a[k].start()

    def both(self, k, i):
        own = half(self.part.at[chip(k)], i)[...].astype(F32)
        return own + half(self.fromsib.at[k], i)[...].astype(F32)

    def put(self, i, k, x):
        half(self.tosend.at[i], k)[...] = x.astype(BF)

    def pass_far(self):
        self.a[2].wait_recv()
        self.put(1, 0, self.both(2, 0))
        self.fa.start()
        self.put(1, 1, self.both(2, 1))
        self.fb.start()
        self.a[1].wait_recv()
        self.put(0, 1, self.both(1, 1))
        self.ub.start()
        self.a[3].wait_recv()
        self.put(2, 0, self.both(3, 0))
        self.da.start()

    def pass_near(self):
        far = self.fromz.at[2]
        self.fa.wait_recv()
        self.put(0, 0, self.both(1, 0) + half(far, 0)[...].astype(F32))
        self.ua.start()
        self.fb.wait_recv()
        self.put(2, 1, self.both(3, 1) + half(far, 1)[...].astype(F32))
        self.db.start()

    def total(self):
        self.a[0].wait_recv()
        t = self.part[chip(0)].astype(F32) + self.fromsib[0].astype(F32)
        for c in (self.ub, self.da, self.ua, self.db):
            c.wait_recv()
        return t + self.fromz[0].astype(F32) + self.fromz[1].astype(F32)

    def drain(self):
        self.net.drain(self.all)


class SeqGather:
    def __init__(self, net, src, slot, xfirst, sem):
        self.net, self.src, self.slot, self.sem = net, src, slot, sem

        def at(k):
            return slot(seq_index(xfirst, k, 0))

        self.first = {
            k: net.copy(lambda k=k: (src, at(0), seq_dev(xfirst, k, 0))) for k in ORDER
        }
        self.own2 = [
            net.copy(lambda k=k: (src, at(0), seq_dev(xfirst, 0, k))) for k in (1, 3)
        ]
        self.second = {
            (k, j): net.copy(lambda k=k, j=j: (at(4 - k), at(4 - k), seq_dev(xfirst, 0, j)))
            for k in ORDER
            for j in (1, 3)
        }

        def came(k, j):
            return slot(seq_index(xfirst, (4 - k) % 4, j))

        self.far = {
            k: net.copy(
                lambda k=k, j=j: (came(k, 4 - j), came(k, 4 - j), seq_dev(xfirst, 0, j))
            )
            for k, j in ((0, 1), (1, 1), (3, 3), (2, 3))
        }

    def local(self):
        return pltpu.make_async_copy(self.src, self.slot(place()[0]), self.sem)

    def p0(self):
        self.local().start()
        for c in self.first.values():
            c.start()

    def p1(self):
        self.p0()
        for c in self.own2:
            c.start()

    def p2(self, own=False):
        if own:
            for c in self.own2:
                c.start()
        for k in ORDER:
            self.first[k].wait_recv()
            for j in (1, 3):
                self.second[k, j].start()

    def p3(self):
        self.own2[0].wait_recv()
        self.far[0].start()
        for k, j in ((1, 1), (3, 3), (2, 3)):
            self.second[k, j].wait_recv()
            self.far[k].start()

    def finish(self):
        self.local().wait()
        self.own2[1].wait_recv()
        for k, j in ((1, 3), (3, 1), (2, 1)):
            self.second[k, j].wait_recv()
        for c in self.far.values():
            c.wait_recv()

    def drain(self):
        self.net.drain(
            [*self.first.values(), *self.own2, *self.second.values(), *self.far.values()]
        )


class SeqScatter:
    def __init__(self, net, src, recv, acc, recv2, tmp, xfirst, own_sem=None, sems=None):
        self.net, self.src, self.recv, self.acc, self.recv2 = net, src, recv, acc, recv2
        self.tmp, self.xfirst, self.own_sem, self.sems = tmp, xfirst, own_sem, sems
        f = xfirst

        def copy(k, at, to, dst, step):
            return net.copy(
                lambda: (self.slots(k, at), recv.at[to, dst : dst + 2], seq_dev(f, step, 0))
            )

        self.fa, self.fb = copy(2, 0, 2, 0, 1), copy(2, 2, 2, 2, 3)
        self.ub, self.da = copy(1, 2, 0, 2, 1), copy(3, 0, 1, 0, 3)
        self.ua = net.copy(lambda: (self.tmp.at[0], recv.at[0, 0:2], seq_dev(f, 1, 0)))
        self.db = net.copy(lambda: (self.tmp.at[1], recv.at[1, 2:4], seq_dev(f, 3, 0)))
        self.c2 = {
            k: net.copy(lambda k=k: (acc.at[self.line(1, k)], recv2.at[k - 1], seq_dev(f, 0, k)))
            for k in ORDER
        }

    def slots(self, k, at):
        return self.src.at[pl.ds(self.line(0, k) * 4 + at, 2)]

    def line(self, axis, k):
        s = place()[0]
        x, y = s // 4, lax.rem(s, 4)
        return lax.rem((x if (axis == 0) == self.xfirst else y) + k, 4)

    def own(self):
        return pltpu.make_async_copy(
            self.src.at[pl.ds(self.line(0, 0) * 4, 4)], self.acc, self.own_sem
        )

    def near(self):
        for c in (self.fa, self.fb, self.ub, self.da):
            c.start()

    def far(self, stage=None):
        self.fa.wait_recv()
        self.fb.wait_recv()
        if stage is not None:
            loads = [
                pltpu.make_async_copy(a, b, self.sems.at[i])
                for i, (a, b) in enumerate(
                    (
                        (self.slots(1, 0), self.tmp.at[0]),
                        (self.slots(3, 2), self.tmp.at[1]),
                        (self.recv.at[2, 0:2], stage[0].at[0:2]),
                        (self.recv.at[2, 2:4], stage[1].at[0:2]),
                    )
                )
            ]
            for c in loads:
                c.start()
            for c in loads:
                c.wait()
        for e, c in ((0, self.ua), (1, self.db)):
            for i in range(2):
                if stage is None:
                    own = self.src[self.line(0, 3 if e else 1) * 4 + 2 * e + i]
                    way = self.recv[2, 2 * e + i]
                else:
                    own, way = self.tmp[e, i], stage[e][i]
                self.tmp[e, i] = (own.astype(F32) + way.astype(F32)).astype(BF)
            c.start()

    def p2(self, stage=None):
        for c in (self.ub, self.da, self.ua, self.db):
            c.wait_recv()
        if stage is None:
            a = self.line(0, 0) * 4

            def body(j):
                t = self.src[a + j].astype(F32) + self.recv[0, j].astype(F32)
                self.acc[j] = (t + self.recv[1, j].astype(F32)).astype(BF)

            fori(4, body)
        else:
            copies = [
                pltpu.make_async_copy(
                    self.recv.at[0:2, j], stage[j % 2].at[0:2], self.sems.at[j]
                )
                for j in range(4)
            ]
            copies[0].start()
            self.own().wait()
            for j in range(4):
                if j < 3:
                    copies[j + 1].start()
                copies[j].wait()
                st = stage[j % 2]
                t = self.acc[j].astype(F32) + st[0].astype(F32)
                self.acc[j] = (t + st[1].astype(F32)).astype(BF)
        for k in ORDER:
            self.c2[k].start()

    def finish(self, out):
        for k in ORDER:
            self.c2[k].wait_recv()
        t = self.acc[self.line(1, 0)].astype(F32) + self.recv2[0].astype(F32)
        out[...] = t + self.recv2[1].astype(F32) + self.recv2[2].astype(F32)


def fori(n, body):
    def step(i, carry):
        body(i)
        return carry

    lax.fori_loop(0, n, step, 0)


def row_stats(x3):
    m = jnp.sum(jnp.sum(x3, axis=0), axis=1, keepdims=True) / D
    d = x3 - m[None]
    v = jnp.sum(jnp.sum(d * d, axis=0), axis=1, keepdims=True) / D
    return m, lax.rsqrt(v + EPS)


def iota(shape, dim):
    return lax.broadcasted_iota(jnp.int32, shape, dim)


def shift_down(u, first, keep):
    r = pltpu.roll(u, 1, 0)
    return jnp.where(iota(u.shape, 0) == 0, first, r) * keep


def shift_up(u):
    return jnp.where(iota(u.shape, 0) == u.shape[0] - 1, 0.0, pltpu.roll(u, u.shape[0] - 1, 0))


def rows_of(b):
    return slice(b * TB, (b + 1) * TB)


def slab_of(ref, i):
    return ref[:, i].reshape(TB, W)


class Norm1:
    def __init__(self, R):
        self.R = R

    def stats(self, b):
        R = self.R

        def body(i):
            at = pl.multiple_of(i * 64, 64)
            m, r = row_stats(R.xF[b, :, pl.ds(at, 64), :].astype(F32))
            R.mean[pl.ds(b * TB + at, 64), :] = m
            R.rstd[pl.ds(b * TB + at, 64), :] = r

        fori(4, body)

    def edge_stats(self):
        m, r = row_stats(self.R.bord[...].astype(F32))
        self.R.bmean[...] = m
        self.R.brstd[...] = r

    def block(self, i, b):
        R = self.R
        v = R.smF[i, R_VEC : R_VEC + 16, :].astype(F32)
        rows = rows_of(b)
        n = (R.xF[b, i].astype(F32) - R.mean[rows, :]) * R.rstd[rows, :]
        normed = n * v[0:1] + v[1:2]
        at = slice(16 * b, 16 * b + 16)
        e = (R.bord[i, at, :].astype(F32) - R.bmean[at, :]) * R.brstd[at, :]
        first = (e * v[0:1] + v[1:2])[15:16]
        differ = shift_down(normed, first, R.keep[rows, :]) - normed
        return n, normed, differ, v


def tree(r, k, wk, keep):
    row = iota((C, W), 0)
    p = jnp.broadcast_to(keep, (C, W))
    q = jnp.ones((C, W), F32)
    t = wk
    out = []
    for level in range(LV):
        m = 1 << level
        second = (row // m) % 2 == 1
        e = jnp.where(second, p, q)
        out.append((jnp.where(second, r, k), e))
        other = jnp.where(second, pltpu.roll(t, m, 0), pltpu.roll(t, C - m, 0))
        p = jnp.where(second, p * other, p)
        q = jnp.where(second, q, q * other)
        t = t * other
    return out, p, q, t


def spread(x, hm):
    return jnp.concatenate([x] * 4, axis=0) * hm


def fold(st):
    f = st[:, 0:128] + st[:, 128:256]
    return jnp.concatenate([f[0:64] + f[64:128], f[128:192] + f[192:256]], axis=0)


def unfold(c, hmf):
    f = jnp.concatenate([c[0:64], c[0:64], c[64:128], c[64:128]], axis=0)
    return jnp.concatenate([f, f], axis=1) * hmf


def head_sum(x, hm):
    hi = x.astype(BF)
    lo = (x - hi.astype(F32)).astype(BF)
    return nn(hi, hm) + nn(lo, hm)


def constants():
    sel = np.zeros((464, 512), np.float32)
    for base, count, off in ((0, 10, 0), (160, 10, 10), (320, 4, 20), (384, 1, 28), (400, 4, 24)):
        for q in range(16):
            for i in range(count):
                sel[base + q * count + i, q * 32 + off + i] = 1
    shmask = np.zeros((8, 160), np.float32)
    for j in range(5):
        shmask[j, 32 * j : 32 * j + 32] = 1
    f = np.arange(256) // 64
    hm = (f[:, None] == f[None, :]).astype(np.float32)
    t = np.arange(64)[:, None]
    u = (np.arange(256) % 64)[None, :]
    lev, levt, sums = [], [], []
    a = np.arange(64)[:, None]
    e = np.arange(64)[None, :]
    for m in (1, 2, 4, 8, 16, 32):
        same = t // (2 * m) == u // (2 * m)
        lev.append(same & (t // m % 2 == 1) & (u // m % 2 == 0))
        levt.append(same & (t // m % 2 == 0) & (u // m % 2 == 1))
        half = a // m == e // m
        sums.append(half & np.where(a // m % 2 == 0, e < a, e > a))
    sums += [e < a, e > a]
    lev = np.stack(lev + levt).astype(np.float32)
    sums = np.concatenate(sums, axis=1).astype(np.float32)
    return (
        jnp.asarray(sel, BF),
        jnp.asarray(shmask, F32),
        jnp.asarray(hm, BF),
        jnp.asarray(lev, F32),
        jnp.asarray(sums, BF),
    )


def layer_kernel(names, *refs):
    R = SimpleNamespace(**dict(zip(names, refs)))
    s, h = place()
    prv, nxt = lax.rem(s + 15, 16), lax.rem(s + 1, 16)
    net = Net(R.ss, R.rs)
    both = (0, 1)
    z1 = jnp.zeros((1, W), F32)

    hid = [HeadGather(net, lambda i, b=b: R.xF.at[b, i]) for b in both]
    smg = HeadGather(net, lambda i: R.smF.at[i])
    midg = [HeadGather(net, lambda i, b=b: R.midF.at[b, i]) for b in both]
    gkvg = [HeadGather(net, lambda i, b=b: R.gF.at[b, i]) for b in both]
    gzg = [HeadGather(net, lambda i, b=b: R.midF.at[b, i]) for b in both]

    def scatter(b, e):
        return HeadScatter(
            net, R.part.at[b], R.fromsib.at[e, b], R.tosend.at[b], R.fromz.at[e, b]
        )

    rs1, rs2, rs3, rs4 = [[scatter(b, e) for b in both] for e in (0, 1, 0, 1)]

    def rows128(ref, q):
        return ref.at[pl.ds(pl.multiple_of(q * 128, 128), 128), :]

    def cols128(ref, q):
        return ref.at[:, pl.ds(pl.multiple_of(q * 128, 128), 128)]

    tws = [
        SeqGather(net, R.tw.at[i], lambda q, i=i: rows128(R.twV.at[i], q), i % 2 == 0, R.ls.at[i])
        for i in range(4)
    ]
    tos = SeqGather(net, R.to, lambda q: cols128(R.toV, q), True, R.ls.at[4])
    cks = [
        SeqGather(
            net,
            R.ck.at[:, a:e],
            lambda q, a=a, e=e: R.ckF.at[pl.ds(pl.multiple_of(q * 128, 128), 128), a:e],
            a == 0,
            R.ls.at[5 + (a > 0)],
        )
        for a, e in ((0, 512), (512, FFL))
    ]
    cks.append(SeqGather(net, R.cr, lambda q: rows128(R.crF, q), False, R.ls.at[7]))
    cvs = [
        SeqGather(
            net,
            R.cv.at[a : a + FFL // 2],
            lambda q, a=a: R.cvF.at[
                a : a + FFL // 2, pl.ds(pl.multiple_of(q * 128, 128), 128)
            ],
            a == 0,
            R.ls.at[36 + (a > 0)],
        )
        for a in (0, FFL // 2)
    ]
    sca = SeqScatter(net, R.gaH, R.ra1, R.ra2, R.ra3, None, True, R.ls.at[8], R.ls.at[20:24])
    scb = SeqScatter(net, R.gbH, R.rb1, R.rb2, R.rb3, None, False, R.ls.at[9], R.ls.at[24:28])

    def seq_step(k):
        sq, hq = place()
        return lax.rem(sq + k, 16), hq

    smalls = [
        net.copy(lambda k=k: (R.small, R.sm.at[place()[0]], seq_step(k))) for k in range(1, 16)
    ]

    def beside(k, step):
        sq, hq = place()
        return lax.rem(sq + step, 16), lax.rem(hq + k, 8)

    edges = [net.copy(lambda k=k: (R.bsrc, R.bord.at[place()[1]], beside(k, 1))) for k in range(8)]
    cots = {
        (b, k): net.copy(
            lambda b=b, k=k: (
                R.cot.at[b, pl.ds(pl.multiple_of(beside(k, 0)[1] * TC, TC), TC), :],
                R.gch.at[b, place()[1]],
                beside(k, 0),
            )
        )
        for b in both
        for k in range(1, 8)
    }
    last = [net.copy(lambda k=k: (R.bsend.at[beside(k, 0)[1]], R.brecv.at[place()[1]], beside(k, 15))) for k in range(8)]
    rex = [
        net.copy(lambda k=k: (R.rsend, R.rrecv.at[place()[1]], beside(k, 0))) for k in range(1, 8)
    ]
    smo = [
        net.copy(lambda k=k: (R.psend.at[seq_step(k)[0]], R.psrecv.at[place()[0]], seq_step(k)))
        for k in range(1, 16)
    ]

    def mid_border(b, k):
        return pltpu.make_async_remote_copy(
            src_ref=R.mb.at[b],
            dst_ref=R.bmid.at[b],
            send_sem=R.bs.at[b * 8 + k],
            recv_sem=R.br.at[b],
            device_id=(nxt, k),
            device_id_type=MESH,
        )

    def grad_border(b, frm):
        return pltpu.make_async_remote_copy(
            src_ref=R.gsend.at[b],
            dst_ref=R.grecv.at[b, frm],
            send_sem=R.bs.at[16 + b],
            recv_sem=R.br.at[2 + b * 8 + frm],
            device_id=(prv, 7),
            device_id_type=MESH,
        )

    def carry_copy(e, b, dst, frm):
        return pltpu.make_async_remote_copy(
            src_ref=R.csend.at[e, b],
            dst_ref=R.crecv.at[b, frm],
            send_sem=R.cs.at[(2 * e + b) * 16 + dst],
            recv_sem=R.cr_.at[(2 * e + b) * 16 + frm],
            device_id=(dst, h),
            device_id_type=MESH,
        )

    def carry_each(e, b, act):
        def body(i, _):
            act(carry_copy(e, b, i, s))
            return 0

        lo, hi = (s + 1, 16) if e == 0 else (0, s)
        lax.fori_loop(lo, hi, body, 0)

    def carry_send(e, b, state, total):
        R.csend[e, b, 0:128, :] = fold(state).astype(BF)
        R.csend[e, b, 128:144, :] = jnp.concatenate(
            [total[:, 0:128], total[:, 128:256], jnp.zeros((14, 128), F32)], axis=0
        ).astype(BF)
        carry_each(e, b, lambda c: c.start())

    def carry_wait(e, b, hmf):
        R.carry[b] = jnp.zeros((128, 128), F32)

        def body(i, _):
            j = i if e == 0 else 15 - i
            carry_copy(e, b, 0, j).wait_recv()
            tt = R.crecv[b, j, 128:144, :].astype(F32)
            for g in range(2):
                at = slice(g * 64, g * 64 + 64)
                R.carry[b, at, :] = R.carry[b, at, :] * tt[g : g + 1] + R.crecv[b, j, at, :].astype(F32)
            return 0

        lax.fori_loop(0, s if e == 0 else 15 - s, body, 0)
        return unfold(R.carry[b], hmf)

    R.small[...] = jnp.concatenate(
        [a[...].astype(F32) for a in (R.sf, R.s2nd, R.d1st, R.d2nd, R.vectors)]
        + [jnp.zeros((3, W), F32)],
        axis=0,
    ).astype(BF)
    for b in both:
        R.bsrc[16 * b : 16 * b + 16, :] = R.x[b, TB - 16 : TB, :]
        R.xF[b, h] = R.x[b]
    greet(head_peers() + seq_peers() + diagonal_peers(1) + diagonal_peers(15))
    hid[0].start()
    for c in smalls + edges:
        c.start()
    hid[1].start()
    R.sm[s] = R.small[...]
    for c in smalls:
        c.wait_recv()
    for t in tws:
        t.p1()
    comp = nn(R.sel[...], R.sm[...].reshape(512, W)).astype(BF)
    R.smF[h] = comp[0:400]
    R.ds2[...] = comp[400:464]
    smg.start()
    for b in both:
        hid[b].relay()
    for t in tws:
        t.p2()
    tos.p1()
    for b in both:
        hid[b].relay_far()
    smg.relay()
    hid[0].finish()
    n1 = Norm1(R)
    n1.stats(0)
    smg.relay_far()
    hid[1].finish()
    n1.stats(1)
    for c in edges:
        c.wait_recv()
    n1.edge_stats()
    smg.finish()
    vl = R.smF[h, R_VEC : R_VEC + 16, :].astype(F32)
    hmb = R.hm[...]
    hmf = hmb.astype(F32)

    def time_forward(**kw):
        L = SimpleNamespace(**kw)

        def shift(b):
            rows = rows_of(b)
            L.mixacc[...] = jnp.zeros_like(L.mixacc)

            def body(i):
                n, normed, differ, v = n1.block(i, b)
                mixed = (normed + differ * v[2:3]).astype(BF)
                L.mixacc[...] += nt(mixed, R.smF[i, R_FIRST : R_FIRST + 160, :])

            fori(8, body)
            hidden = jnp.tanh(L.mixacc[...])
            R.sh[rows, :] = hidden
            for j in range(5):
                L.shm[j, rows, :] = (hidden * R.shmask[j : j + 1, :]).astype(BF)

        def targets(b):
            rows = rows_of(b)
            L.proj[:, rows, :] = jnp.zeros((4, TB, W), F32)
            L.dacc[...] = jnp.zeros_like(L.dacc)

            def body(i):
                col = pl.ds(pl.multiple_of(i * W, W), W)
                n, normed, differ, v = n1.block(i, b)
                second = R.smF[i, R_SECOND : R_SECOND + 160, :]
                for j in range(5):
                    mix = nn(L.shm[j, rows, :], second)
                    target = (normed + differ * (v[3 + j : 4 + j] + mix)).astype(BF)
                    if j == 0:
                        L.dacc[...] += nt(target, R.smF[i, R_DECAY1 : R_DECAY1 + 64, :])
                    else:
                        L.proj[j - 1, rows, :] += nn(target, R.twV[j - 1, col, :])

            fori(8, body)
            hidden = jnp.tanh(L.dacc[...])
            R.dh[rows, :] = hidden
            ld = -jnp.exp(vl[8:9] + nn(hidden.astype(BF), R.ds2[...]))
            R.logd[rows, :] = ld
            L.wdec[rows, :] = jnp.exp(ld) * R.keep[rows, :]
            R.proj[:, rows, :] = L.proj[:, rows, :].astype(BF)

        def states(b):
            L.st[b] = jnp.zeros((W, W), F32)
            R.tpre[8 + b : 9 + b, :] = jnp.ones((1, W), F32)

            def body(c):
                rows = pl.ds(pl.multiple_of(b * TB + c * C, C), C)
                i = b * 4 + c
                r, k, v = L.proj[2, rows, :], L.proj[0, rows, :], L.proj[1, rows, :]
                lv, p, q, t = tree(r, k, L.wdec[rows, :], R.keep[rows, :])
                for l, (a, e) in enumerate(lv):
                    L.xs[l, rows, :] = (a * e).astype(BF)
                R.rp[rows, :] = (r * p).astype(BF)
                L.starts[i] = L.st[b].astype(BF)
                R.tch[pl.ds(i, 1), :] = t[0:1]
                before = R.tpre[8 + b : 9 + b, :]
                R.tpre[pl.ds(i, 1), :] = before
                R.tpre[8 + b : 9 + b, :] = before * t[0:1]
                L.st[b] = L.st[b] * t[0:1] + nn(v.T.astype(BF), (k * q).astype(BF)) * hmf

            fori(4, body)
            carry_send(0, b, L.st[b], R.tpre[8 + b : 9 + b, :])

        def inner(b):
            def body(c):
                rows = pl.ds(pl.multiple_of(b * TB + c * C, C), C)
                r, k, v = L.proj[2, rows, :], L.proj[0, rows, :], L.proj[1, rows, :]
                a = jnp.zeros((C, W), F32)
                at = jnp.zeros((C, W), F32)
                for l in range(LV):
                    xl = L.xs[l, rows, :]
                    y = nt(xl, spread(xl, hmb))
                    a = a + y * R.levels[l]
                    at = at + y * R.levels[LV + l]
                R.scores[rows, :] = at.astype(BF)
                bonus = head_sum(r * vl[9:10] * k, hmb)
                L.ov[rows, :] = nn(a.astype(BF), spread(v.astype(BF), hmb)) + bonus * v

            fori(4, body)

        def outer(b):
            st = carry_wait(0, b, hmf)
            L.st[b] = st
            if b == 1:
                for g in cks:
                    g.p2(True)

            def body(c):
                i = b * 4 + c
                rows = pl.ds(pl.multiple_of(b * TB + c * C, C), C)
                start = L.starts[i].astype(F32) + L.st[b] * R.tpre[pl.ds(i, 1), :]
                R.starts[i] = fold(start).astype(BF)
                o = L.ov[rows, :] + nt(R.rp[rows, :], start.astype(BF))
                d = o - head_sum(o, hmb) / 64.0
                sc = lax.rsqrt(head_sum(d * d, hmb) / 64.0 + GEPS)
                gn = d * sc
                R.gnorm[rows, :] = gn
                R.gscale[rows, :] = sc
                g = L.proj[3, rows, :]
                R.gate[rows, :] = (
                    (gn * vl[10:11] + vl[11:12]) * (g * jax.nn.sigmoid(g))
                ).astype(BF)

            fori(4, body)

        def out(b):
            def body(i):
                y = nn(R.gate[rows_of(b), :], R.toV[:, pl.ds(pl.multiple_of(i * W, W), W)])
                R.part[b, :, i] = y.astype(BF).reshape(8, TC, W)

            fori(8, body)
            for k in (2, 1, 3, 0):
                rs1[b].give(k)

        for t in tws:
            t.p3()
        tos.p2()
        shift(0)
        shift(1)
        for t in tws:
            t.finish()
        for g in cks + cvs:
            g.p0()
        targets(0)
        states(0)
        tos.p3()
        targets(1)
        states(1)
        saved = pltpu.make_async_copy(R.twV, R.twF, R.ls.at[10])
        saved.start()
        inner(0)
        for c in cots.values():
            c.start()
        inner(1)
        outer(0)
        tos.finish()
        out(0)
        outer(1)
        rs1[0].pass_far()
        out(1)
        rs1[0].pass_near()
        rs1[1].pass_far()
        saved.wait()

    f32n = pltpu.VMEM((N, W), F32)
    pl.run_scoped(
        time_forward,
        mixacc=pltpu.VMEM((TB, 160), F32),
        shm=pltpu.VMEM((5, N, 160), BF),
        dacc=pltpu.VMEM((TB, 64), F32),
        proj=pltpu.VMEM((4, N, W), F32),
        wdec=f32n,
        xs=pltpu.VMEM((LV, N, W), BF),
        starts=pltpu.VMEM((8, W, W), BF),
        st=pltpu.VMEM((2, W, W), F32),
        ov=f32n,
    )

    def middle(b):
        m = rs1[b].total() + R.xF[b, :, pl.ds(pl.multiple_of(h * TC, TC), TC), :].astype(F32)
        R.mid[b] = m
        R.midF[b, h] = m.astype(BF)
        for i in range(8):
            R.mb[b, i : i + 1, :] = R.mid[b, i, TC - 1 : TC, :]
        midg[b].start()

        @pl.when(h == 7)
        def _():
            for k in range(8):
                mid_border(b, k).start()

    def channel(**kw):
        L = SimpleNamespace(**kw)
        loads = [
            pltpu.make_async_copy(a, c, R.ls.at[11 + i])
            for i, (a, c) in enumerate(((R.ckF, L.ck), (R.crF, L.cr), (R.cvF, L.cv)))
        ]

        def pairs(i):
            at = pl.ds(pl.multiple_of(lax.rem(i, 4) * N, N), N)
            return R.twV.at[i // 4, at, :], R.twV.at[2 + i // 4, at, :]

        def block(i, b):
            rows = rows_of(b)
            v = R.smF[i, R_VEC : R_VEC + 16, :].astype(F32)
            u = slab_of(R.midF.at[b], i).astype(F32)
            n2 = (u - L.mean[rows, :]) * L.rstd[rows, :] * v[12:13] + v[13:14]
            first = L.bstat[b, pl.ds(i, 1), :] * v[12:13] + v[13:14]
            return n2, shift_down(n2, first, R.keep[rows, :]) - n2, v

        def mixing(b):
            rows = rows_of(b)

            def stat_body(i):
                m, r = row_stats(R.midF[b, i].astype(F32))
                at = pl.ds(pl.multiple_of(b * TB + i * TC, TC), TC)
                L.mean[at, :] = m
                L.rstd[at, :] = r

            fori(8, stat_body)
            mid_border(b, 0).wait_recv()
            e = R.bmid[b]
            m = jnp.sum(jnp.sum(e, axis=0, keepdims=True), axis=1, keepdims=True) / D
            d = e - m
            v = jnp.sum(jnp.sum(d * d, axis=0, keepdims=True), axis=1, keepdims=True) / D
            L.bstat[b] = d * lax.rsqrt(v + EPS)
            if b == 0:
                for c in loads[0:2]:
                    c.wait()
            L.kp[rows, :] = jnp.zeros((TB, FFL), F32)
            L.rec[rows, :] = jnp.zeros((TB, W), F32)

            def body(i):
                at = pl.ds(pl.multiple_of(i * W, W), W)
                n2, d2, v = block(i, b)
                a = (n2 + d2 * v[14:15]).astype(BF)
                c = (n2 + d2 * v[15:16]).astype(BF)
                pk, pr = pairs(i)
                pk[rows, :] = a
                pr[rows, :] = c
                L.kp[rows, :] += nn(a, L.ck[at, :])
                L.rec[rows, :] += nn(c, L.cr[at, :])

            fori(8, body)
            g = jax.nn.sigmoid(L.rec[rows, :])
            L.rec[rows, :] = g
            R.gF[b, h] = (R.cot[b] * g).astype(BF).reshape(8, TC, W)
            gkvg[b].start()

        def hidden_units(b):
            def square(i):
                at = pl.ds(pl.multiple_of(b * TB + i * 64, 64), 64)
                u = L.kp[at, :]
                e = jnp.exp(-jnp.abs(u))
                p = jnp.maximum(u, 0.0) + jnp.log(1.0 + e)
                L.sq[at, :] = (p * p).astype(BF)
                L.kp[at, :] = 2.0 * p * jnp.where(u >= 0, 1.0, e) / (1.0 + e)

            fori(4, square)
            if b == 0:
                for g in cvs:
                    g.finish()
                loads[2].start()
                loads[2].wait()
            rs1[b].drain()

            def out(i):
                y = nn(L.sq[rows_of(b), :], L.cv[:, pl.ds(pl.multiple_of(i * W, W), W)])
                R.part[b, i] = y.astype(BF).reshape(8, TC, W)

            for k in (2, 1, 3, 0):
                out(rs2[b].theirs(k))
                rs2[b].give(k)
                out(rs2[b].ours(k))

        def key_grad(b):
            rows = rows_of(b)
            gkvg[b].finish()
            L.gs[...] = jnp.zeros_like(L.gs)

            def body(i):
                a = R.gF[b, i].reshape(TB, W)
                L.gs[...] += nt(a, L.cv[:, pl.ds(pl.multiple_of(i * W, W), W)])

            fori(8, body)
            L.gk[rows, :] = (L.gs[...] * L.kp[rows, :]).astype(BF)

        def result(b):
            rows = rows_of(b)
            co = rs2[b].total().reshape(TB, W)
            g = L.rec[rows, :]
            R.result[b] = slab_of(R.midF.at[b], h).astype(F32) + g * co
            L.gr[rows, :] = (R.cot[b] * co * g * (1.0 - g)).astype(BF)

        def back(b):
            rows = rows_of(b)
            rs2[b].drain()
            midg[b].drain()

            def body(i):
                at = pl.ds(pl.multiple_of(i * W, W), W)
                n2, d2, v = block(i, b)
                gpk = nt(L.gk[rows, :], L.ck[at, :])
                gpr = nt(L.gr[rows, :], L.cr[at, :])
                R.vg[i, 2 + 2 * b : 3 + 2 * b, :] = jnp.sum(gpk * d2, axis=0, keepdims=True)
                R.vg[i, 3 + 2 * b : 4 + 2 * b, :] = jnp.sum(gpr * d2, axis=0, keepdims=True)
                gd = gpk * v[14:15] + gpr * v[15:16]
                kg = gd * R.keep[rows, :]
                R.gsend[b, pl.ds(i, 1), :] = kg[0:1]
                y = gpk + gpr - gd + shift_up(kg)
                R.part[b, :, i] = y.astype(BF).reshape(8, TC, W)

            fori(8, body)
            for k in (2, 1, 3, 0):
                rs3[b].give(k)
            grad_border(b, h).start()

        def norm_back(b):
            u = R.mid[b]
            m, r = row_stats(u)
            n2 = (u - m[None]) * r[None]
            L.gout[...] = rs3[b].total()

            @pl.when(h == 7)
            def _():
                for i in range(8):
                    grad_border(b, i).wait_recv()
                t = jnp.sum(R.grecv[b], axis=0)
                for i in range(8):
                    L.gout[i, TC - 1 : TC, :] += t[i : i + 1]

            go = L.gout[...]
            gain = R.smF[:, R_VEC + 12 : R_VEC + 13, :].astype(F32)
            v12 = jnp.sum(go * n2, axis=1, keepdims=True)
            v13 = jnp.sum(go, axis=1, keepdims=True)
            if b == 0:
                R.vg[:, 0:1, :] = v12
                R.vg[:, 1:2, :] = v13
            else:
                R.vg[:, 0:1, :] += v12
                R.vg[:, 1:2, :] += v13
            gn = go * gain
            ma = jnp.sum(jnp.sum(gn, axis=0), axis=1, keepdims=True) / D
            mb = jnp.sum(jnp.sum(gn * n2, axis=0), axis=1, keepdims=True) / D
            R.midF[b, h] = (R.gch[b] + (gn - ma[None] - n2 * mb[None]) * r[None]).astype(BF)
            gzg[b].start()

        def staged(home, rows, xfirst, sem, make):
            def copies(i):
                got = []
                for e in range(2):
                    q = 2 * i + e
                    if not xfirst:
                        q = lax.rem(q, 4) * 4 + q // 4
                    at = lax.rem(i, 2)
                    got.append(
                        pltpu.make_async_copy(
                            L.stage.at[at, e, 0:rows], home.at[q], R.ls.at[sem + 2 * at + e]
                        )
                    )
                return got

            def body(i):
                @pl.when(i >= 2)
                def _():
                    for c in copies(i - 2):
                        c.wait()

                y = make(i)
                for e in range(2):
                    at = 0
                    for t in y:
                        L.stage[lax.rem(i, 2), e, at : at + t.shape[0], :] = t[
                            :, 128 * e : 128 * e + 128
                        ].astype(BF)
                        at += t.shape[0]
                for c in copies(i):
                    c.start()

            fori(8, body)
            for i in (6, 7):
                for c in copies(i):
                    c.wait()

        def value_weight():
            L.tr[...] = L.sq[...].T
            staged(
                R.gbH, FFL, False, 28, lambda i: [nn(L.tr[...], R.gF[:, i].reshape(N, W))]
            )

        def key_weight():
            L.tr[...] = L.gk[...].T
            L.grT[...] = L.gr[...].T

            def make(i):
                pk, pr = pairs(i)
                return [nn(L.tr[...], pk[...]), nn(L.grT[...], pr[...])]

            staged(R.gaH, FFL + W, True, 32, make)

        middle(0)
        rs1[1].pass_near()
        for g in cks:
            g.p3()
        midg[0].relay()
        midg[0].relay_far()
        middle(1)
        for g in cvs:
            g.p2(True)
        for g in cks:
            g.finish()
        for c in loads[0:2]:
            c.start()
        for t in tws:
            t.drain()
        midg[0].finish()
        midg[1].relay()
        mixing(0)
        midg[1].relay_far()
        midg[1].finish()
        gkvg[0].relay()
        for g in cvs:
            g.p3()
        mixing(1)
        gkvg[0].relay_far()
        hidden_units(0)
        gkvg[1].relay()
        rs2[0].pass_far()
        gkvg[1].relay_far()
        key_grad(0)
        rs2[0].pass_near()
        hidden_units(1)
        rs2[1].pass_far()
        result(0)
        back(0)
        rs2[1].pass_near()
        key_grad(1)
        rs3[0].pass_far()
        value_weight()
        result(1)
        rs3[0].pass_near()
        back(1)
        for c in cots.values():
            c.wait_recv()
        scb.near()
        scb.own().start()
        norm_back(0)
        rs3[1].pass_far()
        key_weight()
        sca.near()
        sca.own().start()
        gzg[0].relay()
        rs3[1].pass_near()
        gzg[0].relay_far()
        norm_back(1)

    for b in both:
        R.gch[b, h] = R.cot[b, pl.ds(pl.multiple_of(h * TC, TC), TC), :]
    pl.run_scoped(
        channel,
        ck=pltpu.VMEM((D, FFL), BF),
        cv=pltpu.VMEM((FFL, D), BF),
        cr=pltpu.VMEM((D, W), BF),
        mean=pltpu.VMEM((N, 1), F32),
        rstd=pltpu.VMEM((N, 1), F32),
        bstat=pltpu.VMEM((2, 8, W), F32),
        kp=pltpu.VMEM((N, FFL), F32),
        rec=f32n,
        sq=pltpu.VMEM((N, FFL), BF),
        gk=pltpu.VMEM((N, FFL), BF),
        gr=pltpu.VMEM((N, W), BF),
        gs=pltpu.VMEM((TB, FFL), F32),
        tr=pltpu.VMEM((FFL, N), BF),
        grT=pltpu.VMEM((W, N), BF),
        gout=pltpu.VMEM((8, TC, W), F32),
        stage=pltpu.VMEM((2, 2, FFL + W, 128), BF),
    )

    def time_backward(**kw):
        O = SimpleNamespace(**kw)
        sea = SeqScatter(net, O.ea, R.ea1, O.ea2, R.ea3, O.eat, True)
        seb = SeqScatter(net, O.eb, R.eb1, O.eb2, R.eb3, O.ebt, False)
        O.shT[...] = R.sh[...].T.astype(BF)
        for b in both:
            gkvg[b].drain()

        def shm(j, rows):
            return (R.sh[rows, :] * R.shmask[j : j + 1, :]).astype(BF)

        def wkv_backward(**kw):
            L = SimpleNamespace(**kw)

            def gated(b):
                rows = rows_of(b)
                L.gated[rows, :] = jnp.zeros((TB, W), F32)

                def body(i):
                    a = slab_of(R.midF.at[b], i)
                    L.gated[rows, :] += nt(a, R.toV[:, pl.ds(pl.multiple_of(i * W, W), W)])

                fori(8, body)

                def gate_body(i, acc):
                    at = pl.ds(pl.multiple_of(b * TB + i * 64, 64), 64)
                    gd = L.gated[at, :]
                    gn = R.gnorm[at, :]
                    g = R.proj[3, at, :].astype(F32)
                    sg = jax.nn.sigmoid(g)
                    gno = gd * (g * sg)
                    dg = gd * (gn * vl[10:11] + vl[11:12]) * sg * (1.0 + g * (1.0 - sg))
                    O.gp[3, at, :] = dg.astype(BF)
                    gg = gno * vl[10:11]
                    ma = head_sum(gg, hmb) / 64.0
                    mb = head_sum(gg * gn, hmb) / 64.0
                    L.go[at, :] = R.gscale[at, :] * (gg - ma - gn * mb)
                    return (
                        acc[0] + jnp.sum(gno * gn, axis=0, keepdims=True),
                        acc[1] + jnp.sum(gno, axis=0, keepdims=True),
                    )

                return lax.fori_loop(0, 4, gate_body, (z1, z1))

            def adjoint(b):
                L.ds[b] = jnp.zeros((W, W), F32)
                L.tsuf[8 + b : 9 + b, :] = jnp.ones((1, W), F32)

                def body(e):
                    i = b * 4 + 3 - e
                    rows = pl.ds(pl.multiple_of(i * C, C), C)
                    L.dsl[i] = L.ds[b].astype(BF)
                    t = R.tch[pl.ds(i, 1), :]
                    after = L.tsuf[8 + b : 9 + b, :]
                    L.tsuf[pl.ds(i, 1), :] = after
                    L.tsuf[8 + b : 9 + b, :] = after * t
                    L.ds[b] = L.ds[b] * t + nn(L.go[rows, :].T.astype(BF), R.rp[rows, :]) * hmf

                fori(4, body)
                carry_send(1, b, L.ds[b], L.tsuf[8 + b : 9 + b, :])

            def output_weight():
                L.gatT[...] = R.gate[...].T

                def body(i):
                    a = R.midF[:, :, i].reshape(N, W)
                    put(O.eb, i, 0, nn(L.gatT[...], a).astype(BF), False)

                fori(8, body)

            def gate_weight():
                O.gpT[3] = O.gp[3].T

                def body(i):
                    y = jnp.zeros((W, W), F32)
                    for b in both:
                        rows = rows_of(b)
                        n, normed, differ, v = n1.block(i, b)
                        mix = nn(shm(4, rows), R.smF[i, R_SECOND : R_SECOND + 160, :])
                        target = (normed + differ * (v[7:8] + mix)).astype(BF)
                        y = y + nn(O.gpT[3, :, rows], target)
                    put(O.ea, i, 0, y.astype(BF), True)

                fori(8, body)

            def inner(b, gu):
                def body(c, gu):
                    rows = pl.ds(pl.multiple_of(b * TB + c * C, C), C)
                    r, k, v = [R.proj[j, rows, :].astype(F32) for j in (2, 0, 1)]
                    g, kp = L.go[rows, :], R.keep[rows, :]
                    lv, p, q, t = tree(r, k, jnp.exp(R.logd[rows, :]) * kp, kp)
                    L.pP[rows, :] = p
                    L.pQ[rows, :] = q
                    vb, gb = v.astype(BF), g.astype(BF)
                    gsp = spread(gb, hmb)
                    da = nt(gb, spread(vb, hmb))
                    dat = nt(vb, gsp)
                    row = iota((C, W), 0)
                    agr = jnp.zeros((C, W), F32)
                    agk = jnp.zeros((C, W), F32)
                    ys = []
                    for l, (a, e) in enumerate(lv):
                        x = (a * e).astype(BF)
                        d = (da * R.levels[l] + dat * R.levels[LV + l]).astype(BF)
                        gx = nn(d, spread(x, hmb))
                        second = (row // (1 << l)) % 2 == 1
                        ge = gx * e
                        agr = agr + jnp.where(second, ge, 0.0)
                        agk = agk + jnp.where(second, 0.0, ge)
                        ys.append((x.astype(F32) * gx).astype(BF))
                    L.gG[rows, :] = nn(R.sums[:, 0 : LV * C], jnp.concatenate(ys, axis=0))
                    u = vl[9:10]
                    dad = head_sum(g * v, hmb)
                    bonus = head_sum(r * u * k, hmb)
                    L.gr[rows, :] = agr + u * k * dad
                    L.gk[rows, :] = agk + u * r * dad
                    L.gv[rows, :] = nn(R.scores[rows, :], gsp) + bonus * g
                    return gu + jnp.sum(r * k * dad, axis=0, keepdims=True)

                return lax.fori_loop(0, 4, body, gu)

            def outer(b, g8):
                L.ds[b] = carry_wait(1, b, hmf)

                def body(c, g8):
                    i = b * 4 + c
                    rows = pl.ds(pl.multiple_of(i * C, C), C)
                    st = unfold(R.starts[i].astype(F32), hmf)
                    de = L.dsl[i].astype(F32) + L.ds[b] * L.tsuf[pl.ds(i, 1), :]
                    deb = de.astype(BF)
                    p, q = L.pP[rows, :], L.pQ[rows, :]
                    kq = (R.proj[0, rows, :].astype(F32) * q).astype(BF)
                    rpc = R.rp[rows, :]
                    gkq = nn(R.proj[1, rows, :], deb)
                    grp = nn(L.go[rows, :].astype(BF), st.astype(BF))
                    O.gp[1, rows, :] = (L.gv[rows, :] + nt(kq, deb)).astype(BF)
                    O.gp[0, rows, :] = (L.gk[rows, :] + gkq * q).astype(BF)
                    O.gp[2, rows, :] = (L.gr[rows, :] + grp * p).astype(BF)
                    ky = (kq.astype(F32) * gkq).astype(BF)
                    ry = (rpc.astype(F32) * grp).astype(BF)
                    cst = jnp.sum(st * de, axis=0, keepdims=True) * R.tch[pl.ds(i, 1), :]
                    gl = nn(R.sums[:, LV * C :], jnp.concatenate([ky, ry], axis=0))
                    gw = (L.gG[rows, :] + gl + cst) * R.logd[rows, :]
                    O.gw[rows, :] = gw.astype(BF)
                    return g8 + jnp.sum(gw, axis=0, keepdims=True)

                return lax.fori_loop(0, 4, body, g8)

            sca.tmp, scb.tmp = L.rat, L.rbt
            gzg[0].finish()
            gzg[1].relay()
            a10, a11 = gated(0)
            adjoint(0)
            gzg[1].relay_far()
            gzg[1].finish()
            b10, b11 = gated(1)
            adjoint(1)
            scb.far([L.stage.at[0, :, 0:FFL], L.stage.at[1, :, 0:FFL]])
            sca.far([L.stage.at[0], L.stage.at[1]])
            output_weight()
            seb.near()
            g9 = inner(0, z1)
            gate_weight()
            sea.near()
            seb.far()
            g9 = inner(1, g9)
            scb.p2([L.stage.at[0, :, 0:FFL], L.stage.at[1, :, 0:FFL]])
            sea.far()
            g8 = outer(0, z1)
            sca.p2([L.stage.at[0], L.stage.at[1]])
            g8 = outer(1, g8)
            net.drain([sca.ua, sca.db, scb.ua, scb.db])
            R.gvec[0:1, :] = g8
            R.gvec[1:2, :] = g9
            R.gvec[2:3, :] = a10 + b10
            R.gvec[3:4, :] = a11 + b11

        reload = pltpu.make_async_copy(R.twF, R.twV, R.ls.at[10])
        reload.start()
        pl.run_scoped(
            wkv_backward,
            gated=f32n,
            go=f32n,
            gr=f32n,
            gk=f32n,
            gv=f32n,
            gG=f32n,
            pP=f32n,
            pQ=f32n,
            dsl=pltpu.VMEM((8, W, W), BF),
            ds=pltpu.VMEM((2, W, W), F32),
            tsuf=pltpu.VMEM((16, W), F32),
            gatT=pltpu.VMEM((W, N), BF),
            rat=pltpu.VMEM((2, 2, FFL + W, 128), BF),
            rbt=pltpu.VMEM((2, 2, FFL, 128), BF),
            stage=pltpu.VMEM((2, 3, FFL + W, 128), BF),
        )

        for j in range(3):
            O.gpT[j] = O.gp[j].T
        dhv = R.dh[...]
        gdv = nt(O.gw[...], R.ds2[...]) * (1.0 - dhv * dhv)
        O.gdp[...] = gdv.astype(BF)
        O.gdpT[...] = gdv.T.astype(BF)
        O.lsm[400:464, :] = nn(dhv.T.astype(BF), O.gw[...])
        reload.wait()

        def normed_back(**kw):
            L = SimpleNamespace(**kw)
            sta = SeqScatter(net, L.ta, R.ta1, L.ta2, R.ta3, L.tat, True)
            stb = SeqScatter(net, L.tb, R.tb1, L.tb2, R.tb3, L.tbt, False)
            sms = HeadScatter(net, L.sg, R.sgsib, L.sgsend, R.sgz)
            L.gsh[...] = jnp.zeros_like(L.gsh)
            rank = iota((160, W), 0)

            def target_body(i):
                at = pl.ds(pl.multiple_of(i * W, W), W)
                second = R.smF[i, R_SECOND : R_SECOND + 160, :]
                dfirst = R.smF[i, R_DECAY1 : R_DECAY1 + 64, :]
                ws = [jnp.zeros((W, W), F32) for _ in range(3)]
                gsec = jnp.zeros((160, W), F32)
                gd1 = jnp.zeros((64, W), F32)
                rowsum = [z1] * 5
                for b in both:
                    rows = rows_of(b)
                    n, normed, differ, v = n1.block(i, b)
                    a1 = jnp.zeros((TB, W), F32)
                    a2 = jnp.zeros((TB, W), F32)
                    for j in range(5):
                        m = v[3 + j : 4 + j] + nn(shm(j, rows), second)
                        if j < 4:
                            target = (normed + differ * m).astype(BF)
                        if j == 0:
                            gt = nn(O.gdp[rows, :], dfirst)
                            gd1 = gd1 + nn(O.gdpT[:, rows], target)
                        else:
                            gt = nt(O.gp[j - 1, rows, :], R.twV[j - 1, at, :])
                            if j < 4:
                                ws[j - 1] = ws[j - 1] + nn(O.gpT[j - 1, :, rows], target)
                        a1 = a1 + gt
                        a2 = a2 + gt * m
                        qv = gt * differ
                        rowsum[j] = rowsum[j] + jnp.sum(qv, axis=0, keepdims=True)
                        qb = qv.astype(BF)
                        gsec = gsec + jnp.where(rank // 32 == j, nn(O.shT[:, rows], qb), 0.0)
                        L.gsh[rows, :] += nt(qb, second) * R.shmask[j : j + 1, :]
                    L.s1[i, rows, :] = a1.astype(BF)
                    R.gF[b, i] = a2.astype(BF).reshape(8, TC, W)
                put(L.ta, i, 0, ws[0].astype(BF), True)
                put(L.tb, i, 0, ws[1].astype(BF), False)
                put(L.ta, i, W, ws[2][0:128].astype(BF), True)
                put(L.tb, i, W, ws[2][128:256].astype(BF), False)
                L.sg[i, R_SECOND : R_SECOND + 160, :] = gsec.astype(BF)
                L.sg[i, R_DECAY1 : R_DECAY1 + 64, :] = gd1.astype(BF)
                for j in range(5):
                    L.psm[i, 3 + j : 4 + j, :] = rowsum[j]

            fori(8, target_body)
            sea.p2()
            seb.p2()
            sta.near()
            stb.near()
            hidden = R.sh[...]
            gs2 = L.gsh[...] * (1.0 - hidden * hidden)
            L.gshp[...] = gs2.astype(BF)
            L.gshpT[...] = gs2.T.astype(BF)
            L.rsum[...] = jnp.zeros_like(L.rsum)
            lane = iota((TB, 128), 1)

            def mixed_back(b):
                rows = rows_of(b)

                def body(i):
                    first = R.smF[i, R_FIRST : R_FIRST + 160, :]
                    n, normed, differ, v = n1.block(i, b)
                    mixed = (normed + differ * v[2:3]).astype(BF)
                    gm = nn(L.gshp[rows, :], first)
                    gf = nn(L.gshpT[:, rows], mixed)
                    g2 = jnp.sum(gm * differ, axis=0, keepdims=True)
                    gd = R.gF[b, i].reshape(TB, W).astype(F32) + gm * v[2:3]
                    kg = gd * R.keep[rows, :]
                    R.bsend[i, b : b + 1, :] = kg[0:1]
                    gn = L.s1[i, rows, :].astype(F32) + gm - gd + shift_up(kg)
                    R.part[b, i] = gn.astype(BF).reshape(8, TC, W)
                    gg = gn * v[0:1]
                    ra = jnp.sum(gg, axis=1, keepdims=True)
                    rb = jnp.sum(gg * n, axis=1, keepdims=True)
                    L.rsum[rows, :] += jnp.where(lane == 0, ra, jnp.where(lane == 1, rb, 0.0))
                    if b == 0:
                        L.sg[i, R_FIRST : R_FIRST + 160, :] = gf.astype(BF)
                        L.psm[i, 2:3, :] = g2
                    else:
                        had = L.sg[i, R_FIRST : R_FIRST + 160, :].astype(F32)
                        L.sg[i, R_FIRST : R_FIRST + 160, :] = (had + gf).astype(BF)
                        vg = R.vg[i]
                        L.sg[i, R_VEC : R_VEC + 16, :] = jnp.concatenate(
                            [
                                jnp.zeros((2, W), F32),
                                L.psm[i, 2:3, :] + g2,
                                L.psm[i, 3:8, :],
                                jnp.zeros((4, W), F32),
                                vg[0:2],
                                vg[2:4] + vg[4:6],
                            ],
                            axis=0,
                        ).astype(BF)

                if b == 0:
                    fori(8, body)
                else:
                    fori(4, body)
                    rs4[0].pass_far()
                    fori(4, lambda i: body(i + 4))
                for k in (2, 1, 3, 0):
                    rs4[b].give(k)

            for b in both:
                rs3[b].drain()
            R.bsend[...] = jnp.zeros_like(R.bsend)
            mixed_back(0)
            mixed_back(1)
            for c in last:
                c.start()
            for k in (2, 1, 3, 0):
                sms.give(k)
            sta.far()
            stb.far()
            rs4[0].pass_near()
            sms.pass_far()
            rs4[1].pass_far()
            sca.finish(R.oca)
            scb.finish(R.ocb)
            for c in last:
                c.wait_recv()
            edge = jnp.sum(R.brecv[...], axis=0)
            lane8 = iota((1, 128), 1)
            for b in both:
                at = slice(b * TB + TB - 16, b * TB + TB)
                n = (R.xF[b, h, TB - 16 : TB, :].astype(F32) - R.mean[at, :]) * R.rstd[at, :]
                e = edge[b : b + 1] * vl[0:1]
                ra = jnp.sum(e, axis=1, keepdims=True)
                rb = jnp.sum(e * n[15:16], axis=1, keepdims=True)
                end = slice(b * TB + TB - 1, b * TB + TB)
                L.rsum[end, :] += jnp.where(lane8 == 0, ra, jnp.where(lane8 == 1, rb, 0.0))
            R.rsend[...] = L.rsum[...].T[0:8]
            R.rrecv[h] = R.rsend[...]
            for c in rex:
                c.start()
            sms.pass_near()
            rs4[1].pass_near()
            g0, g1 = z1, z1
            for b in both:
                rows = rows_of(b)
                R.mid[b] = rs4[b].total()
                R.mid[b, 7, TC - 1 : TC, :] += edge[b : b + 1]
                gl = R.mid[b].reshape(TB, W)
                n = (R.xF[b, h].astype(F32) - R.mean[rows, :]) * R.rstd[rows, :]
                g0 = g0 + jnp.sum(gl * n, axis=0, keepdims=True)
                g1 = g1 + jnp.sum(gl, axis=0, keepdims=True)
            O.lsm[0:400, :] = sms.total()
            O.lsm[R_VEC : R_VEC + 2, :] += jnp.concatenate([g0, g1], axis=0)
            O.lsm[R_VEC + 8 : R_VEC + 12, :] += R.gvec[0:4, :]
            packed = lax.dot_general(
                R.sel[...],
                O.lsm[...].astype(BF),
                (((0,), (0,)), ((), ())),
                preferred_element_type=F32,
            )
            R.psend[...] = packed.astype(BF).reshape(16, 32, W)
            for c in smo:
                c.start()
            sta.p2()
            stb.p2()
            for c in rex:
                c.wait_recv()
            tot = jnp.sum(R.rrecv[...], axis=0)
            L.rsum[...] = jnp.concatenate([tot, jnp.zeros((120, N), F32)], axis=0).T / D
            for b in both:
                rows = rows_of(b)
                gl = R.mid[b].reshape(TB, W)
                n = (R.xF[b, h].astype(F32) - R.mean[rows, :]) * R.rstd[rows, :]
                R.hgrad[b] = slab_of(R.midF.at[b], h).astype(F32) + R.rstd[rows, :] * (
                    gl * vl[0:1] - L.rsum[rows, 0:1] - n * L.rsum[rows, 1:2]
                )
            sea.finish(R.oea)
            seb.finish(R.oeb)
            R.psrecv[s] = R.psend[s]
            for c in smo:
                c.wait_recv()
            R.osm[...] = jnp.sum(R.psrecv[...].astype(F32), axis=0)
            sta.finish(R.ota)
            stb.finish(R.otb)
            net.drain()

        RT = W + 128
        pl.run_scoped(
            normed_back,
            s1=pltpu.VMEM((8, N, W), BF),
            ta=pltpu.VMEM((16, RT, 128), BF),
            tb=pltpu.VMEM((16, RT, 128), BF),
            ta2=pltpu.VMEM((4, RT, 128), BF),
            tat=pltpu.VMEM((2, 2, RT, 128), BF),
            tbt=pltpu.VMEM((2, 2, RT, 128), BF),
            tb2=pltpu.VMEM((4, RT, 128), BF),
            sg=pltpu.VMEM((8, 400, W), BF),
            sgsend=pltpu.VMEM((3, 400, W), BF),
            gsh=pltpu.VMEM((N, 160), F32),
            gshp=pltpu.VMEM((N, 160), BF),
            gshpT=pltpu.VMEM((160, N), BF),
            rsum=pltpu.VMEM((N, 128), F32),
            psm=pltpu.VMEM((8, 8, W), F32),
        )

    pl.run_scoped(
        time_backward,
        ea=pltpu.VMEM((16, W, 128), BF),
        eb=pltpu.VMEM((16, W, 128), BF),
        ea2=pltpu.VMEM((4, W, 128), BF),
        eat=pltpu.VMEM((2, 2, W, 128), BF),
        ebt=pltpu.VMEM((2, 2, W, 128), BF),
        eb2=pltpu.VMEM((4, W, 128), BF),
        gp=pltpu.VMEM((4, N, W), BF),
        gpT=pltpu.VMEM((4, W, N), BF),
        shT=pltpu.VMEM((160, N), BF),
        gw=pltpu.VMEM((N, W), BF),
        gdp=pltpu.VMEM((N, 64), BF),
        gdpT=pltpu.VMEM((64, N), BF),
        lsm=pltpu.VMEM((464, W), F32),
    )
    for b in both:

        @pl.when(h == 7)
        def _():
            for k in range(8):
                mid_border(b, k).wait_send()

        grad_border(b, h).wait_send()
        for e in both:
            carry_each(e, b, lambda c: c.wait_send())


def put(ref, i, row, y, xfirst):
    for e in range(2):
        q = 2 * i + e
        if not xfirst:
            q = lax.rem(q, 4) * 4 + q // 4
        ref[q, row : row + y.shape[0], :] = y[:, 128 * e : 128 * e + 128]


VM = pl.BlockSpec(memory_space=pltpu.VMEM)
HB = pl.BlockSpec(memory_space=pl.ANY)
SD = jax.ShapeDtypeStruct


def run_layer(ins):
    far = ("tw", "to", "ck", "cv", "cr")
    RA, RB, RT = FFL + W, FFL, W + 128
    outs = dict(
        result=((2, TB, W), F32, VM),
        hgrad=((2, TB, W), F32, VM),
        oca=((RA, 128), F32, VM),
        ocb=((RB, 128), F32, VM),
        oea=((W, 128), F32, VM),
        oeb=((W, 128), F32, VM),
        ota=((RT, 128), F32, VM),
        otb=((RT, 128), F32, VM),
        osm=((32, W), F32, VM),
        twF=((4, D, W), BF, HB),
        ckF=((D, FFL), BF, HB),
        cvF=((FFL, D), BF, HB),
        crF=((D, W), BF, HB),
        gaH=((16, RA, 128), BF, HB),
        gbH=((16, RB, 128), BF, HB),
        ra1=((3, 4, RA, 128), BF, HB),
        rb1=((3, 4, RB, 128), BF, HB),
    )
    scr = dict(
        small=((32, W), BF),
        sm=((16, 32, W), BF),
        bsrc=((32, W), BF),
        xF=((2, 8, TB, W), BF),
        bord=((8, 32, W), BF),
        smF=((8, 400, W), BF),
        ds2=((64, W), BF),
        twV=((4, D, W), BF),
        toV=((W, D), BF),
        midF=((2, 8, 8, TC, W), BF),
        mid=((2, 8, TC, W), F32),
        mb=((2, 8, W), F32),
        bmid=((2, 8, W), F32),
        gch=((2, 8, TC, W), F32),
        gF=((2, 8, 8, TC, W), BF),
        mean=((N, 1), F32),
        rstd=((N, 1), F32),
        bmean=((32, 1), F32),
        brstd=((32, 1), F32),
        sh=((N, 160), F32),
        dh=((N, 64), F32),
        proj=((4, N, W), BF),
        logd=((N, W), F32),
        gnorm=((N, W), F32),
        gscale=((N, W), F32),
        scores=((N, W), BF),
        starts=((8, 128, 128), BF),
        rp=((N, W), BF),
        gate=((N, W), BF),
        tch=((8, W), F32),
        tpre=((16, W), F32),
        carry=((2, 128, 128), F32),
        csend=((2, 2, 144, 128), BF),
        crecv=((2, 16, 144, 128), BF),
        part=((2, 8, 8, TC, W), BF),
        tosend=((2, 3, 8, TC, W), BF),
        fromsib=((2, 2, 4, 8, TC, W), BF),
        fromz=((2, 2, 3, 8, TC, W), BF),
        gsend=((2, 8, W), F32),
        grecv=((2, 8, 8, W), F32),
        vg=((8, 8, W), F32),
        gvec=((8, W), F32),
        bsend=((8, 8, W), F32),
        brecv=((8, 8, W), F32),
        rsend=((8, N), F32),
        rrecv=((8, 8, N), F32),
        sgsib=((4, 400, W), BF),
        sgz=((3, 400, W), BF),
        psend=((16, 32, W), BF),
        psrecv=((16, 32, W), BF),
        ra2=((4, RA, 128), BF),
        ra3=((3, RA, 128), BF),
        rb2=((4, RB, 128), BF),
        rb3=((3, RB, 128), BF),
        ea1=((3, 4, W, 128), BF),
        ea3=((3, W, 128), BF),
        eb1=((3, 4, W, 128), BF),
        eb3=((3, W, 128), BF),
        ta1=((3, 4, RT, 128), BF),
        ta3=((3, RT, 128), BF),
        tb1=((3, 4, RT, 128), BF),
        tb3=((3, RT, 128), BF),
    )
    sems = dict(ss=480, rs=480, ls=38, bs=18, br=18, cs=64, cr_=64)
    names = list(ins) + list(outs) + list(scr) + list(sems)
    got = pl.pallas_call(
        functools.partial(layer_kernel, names),
        out_shape=[SD(a, t) for a, t, _ in outs.values()],
        in_specs=[HB if k in far else VM for k in ins],
        out_specs=[m for _, _, m in outs.values()],
        scratch_shapes=[pltpu.VMEM(a, t) for a, t in scr.values()]
        + [pltpu.SemaphoreType.DMA((n,)) for n in sems.values()],
        name="layer",
        compiler_params=pltpu.CompilerParams(
            collective_id=1, has_side_effects=True, vmem_limit_bytes=VMEM_LIMIT
        ),
    )(*ins.values())
    return SimpleNamespace(**dict(zip(outs, got)))


def on_device(
    hidden, cotangent, opening_flags, vectors, shift_first, shift_second, decay_first, decay_second,
    time_weights, time_output, channel_key, channel_value, channel_recept,
):
    sel, shmask, hm, levels, sums = constants()
    o = run_layer(
        dict(
            x=hidden,
            cot=cotangent,
            keep=(1.0 - opening_flags.astype(F32)).reshape(N, 1),
            sf=shift_first[0],
            s2nd=shift_second[0],
            d1st=decay_first[0],
            d2nd=decay_second[0],
            vectors=vectors[0],
            sel=sel,
            shmask=shmask,
            hm=hm,
            levels=levels,
            sums=sums,
            tw=time_weights[0],
            to=time_output[0],
            ck=channel_key[0],
            cv=channel_value[0],
            cr=channel_recept[0],
        )
    )
    return finish(o.result, o.hgrad, o.oca, o.ocb, o.oea, o.oeb, o.ota, o.otb, o.osm)


def finish_kernel(
    result, hg, ca, cb, ea, eb, ta, tb, sm,
    o_result, o_hidden, o_vec, o_first, o_second, o_decay1, o_decay2, o_time, o_out, o_key, o_value,
    o_recept,
):
    o_result[...] = result[...]
    o_hidden[...] = hg[...]
    o_first[...] = sm[0:10].reshape(10, 1, W)
    o_second[...] = sm[10:20].reshape(10, 1, W)
    o_decay1[0] = sm[20:24]
    o_decay2[0] = sm[24:28]
    o_vec[0] = sm[28:29]
    o_time[0, 0] = ta[0:W].T
    o_time[0, 1] = tb[0:W].T
    o_time[0, 2, :, 0:128] = ta[W:].T
    o_time[0, 2, :, 128:256] = tb[W:].T
    o_time[0, 3] = ea[...].T
    o_out[0] = eb[...]
    o_key[0] = ca[0:FFL].T
    o_value[0] = cb[...]
    o_recept[0] = ca[FFL:].T


def finish(*ins):
    shapes = [
        (2, TB, W), (2, TB, W), (1, 1, W), (10, 1, W), (10, 1, W), (1, 4, W), (1, 4, W),
        (1, 4, 128, W), (1, W, 128), (1, 128, FFL), (1, FFL, 128), (1, 128, W),
    ]
    got = pl.pallas_call(
        finish_kernel,
        out_shape=[SD(q, F32) for q in shapes],
        in_specs=[VM] * len(ins),
        out_specs=[VM] * len(shapes),
        name="finish",
        compiler_params=pltpu.CompilerParams(vmem_limit_bytes=VMEM_LIMIT),
    )(*ins)
    return tuple(a.transpose(1, 0, 2) if a.shape[:2] == (10, 1) else a for a in got)


def solution(mesh):
    last = P(None, "seq", "head")
    turned = P(None, "head", "seq")
    four = P(None, None, "seq", "head")
    return jax.shard_map(
        on_device,
        mesh=mesh,
        in_specs=(last, last, P(None, "seq"), last, last, last, last, last, four, turned, last, turned, last),
        out_specs=(last, last, last, last, last, last, last, four, turned, last, turned, last),
        check_vma=False,
    )
```
